32 devices in a mesh: seq: 16 (over z, x, core), tok: 2 (over y).
Axes of the slice: x: 2, y: 2, z: 4, core: 2. Of those that a mesh axis runs over, the one named last changes fastest.
Arguments:
- tokens: bfloat16 [128, 128, 1024], P('seq', 'tok'), may hold values from -6 to 6
- noise_times: int32 [128], P('seq'), may hold values from 0 to 999
- time_proj: bfloat16 [256, 1024], replicated, may hold values from -0.375 to 0.375
- time_bias: bfloat16 [1024], replicated, may hold values from -1.5 to 1.5
- gain_one: bfloat16 [1024], replicated, may hold values from 0.5 to 1.5
- shift_one: bfloat16 [1024], replicated, may hold values from -1.5 to 1.5
- w_qkv: bfloat16 [1024, 3072], replicated, may hold values from -0.1875 to 0.1875
- w_out: bfloat16 [1024, 1024], replicated, may hold values from -1.25 to 1.25
- gain_two: bfloat16 [1024], replicated, may hold values from 0.5 to 1.5
- shift_two: bfloat16 [1024], replicated, may hold values from -1.5 to 1.5
- w_up: bfloat16 [1024, 4096], replicated, may hold values from -0.1875 to 0.1875
- b_up: bfloat16 [4096], replicated, may hold values from -2.5 to 2.5
- w_down: bfloat16 [4096, 1024], replicated, may hold values from -0.09375 to 0.09375
- b_down: bfloat16 [1024], replicated, may hold values from -1.5 to 1.5
- cotangent: bfloat16 [128, 128, 1024], P('seq', 'tok'), may hold values from -6 to 6
Outputs:
- mixed_out: bfloat16 [128, 128, 1024], P('seq', 'tok')
- grad_tokens: bfloat16 [128, 128, 1024], P('seq', 'tok')
- grad_time_proj: float32 [256, 1024], P(None, 'seq')
- grad_time_bias: float32 [1024], P('seq')
- grad_gain_one: float32 [1024], P('seq')
- grad_shift_one: float32 [1024], P('seq')
- grad_w_qkv: float32 [1024, 3072], P(None, 'seq')
- grad_w_out: float32 [1024, 1024], P(None, 'seq')
- grad_gain_two: float32 [1024], P('seq')
- grad_shift_two: float32 [1024], P('seq')
- grad_w_up: float32 [1024, 4096], P(None, 'seq')
- grad_b_up: float32 [4096], P('seq')
- grad_w_down: float32 [4096, 1024], P(None, 'seq')
- grad_b_down: float32 [1024], P('seq')
The draws below stay inside these ranges and needn't reach their ends.
All inputs are finite; a program needn't handle non-finite values.
Results may differ from the reference program's by a relative error of at most 0.017.
Values may be sent and summed in bfloat16 or wider, within the bound.
A program may use at most 256 MiB of HBM per device.

```python
import math
import jax
import jax.numpy as jnp
from jax import lax

D = 1024
HEADS = 16
HD = 64
FF = 4096
TEMB = 256
NOISE_STEPS = 1000
LEN = 128
SEQUENCES = 128


def plant(array, stream_key, smallest, largest):
    spot = [jax.random.randint(jax.random.fold_in(stream_key, axis), (), 0, length) for axis, length in enumerate(array.shape)]
    longest = array.shape.index(max(array.shape))
    neighbour = spot[:longest] + [(spot[longest] + 1) % array.shape[longest]] + spot[longest + 1:]
    return array.at[tuple(spot)].set(smallest).at[tuple(neighbour)].set(largest)


def with_spikes(entries, rng, source, target, blocks, factor):
    def block_of(axis_at):
        return (jnp.arange(entries.shape[axis_at]) // (entries.shape[axis_at] // blocks)).reshape((-1,) + (1,) * (entries.ndim - 1 - axis_at))

    near = jax.random.permutation(rng, blocks)[block_of(target)]
    second = (block_of(target) + blocks // 2) % blocks
    return jnp.where((block_of(source) == near) | (block_of(source) == second), factor * entries, entries)


def steps_of(rng, dims, split, least, top_value):
    gain, own = 1.0, jax.random.fold_in(rng, 6)
    for position, blocks in split:
        heights = jnp.exp(jax.random.uniform(jax.random.fold_in(own, position), (blocks,), jnp.float32, least / len(split), top_value / len(split)))
        gain = gain * jnp.repeat(heights, dims[position] // blocks).reshape([-1 if axis == position else 1 for axis in range(len(dims))])
    return gain


def noise(stream_key, shape, deviation, reach, split=(), held_as=jnp.bfloat16):
    array = deviation * jax.random.normal(stream_key, shape, jnp.float32)
    if split:
        array = array * steps_of(stream_key, shape, split, -0.22, 0.18)
    return jnp.clip(array, -reach, reach).astype(held_as)


def bell_draw_with(key, extent, deviation, bound, shards, heavy, kind=jnp.bfloat16):
    values = deviation * jax.random.normal(key, extent, jnp.float32)
    if shards:
        values = values * steps_of(key, extent, shards, -0.22, 0.18)
    return jnp.clip(with_spikes(values, jax.random.fold_in(key, 3), *heavy), -bound, bound).astype(kind)


def setup_inputs(seed: int = 0) -> dict:
    key_of = jax.random.split(jax.random.key(seed), 16)
    tokens = noise(key_of[0], (SEQUENCES, LEN, D), 1.0, 6.0, ((0, 16), (1, 2)))
    noise_times = plant(jax.random.randint(key_of[1], (SEQUENCES,), 0, NOISE_STEPS), jax.random.fold_in(key_of[1], 1), 0, NOISE_STEPS - 1).astype(jnp.int32)
    time_proj = noise(key_of[2], (TEMB, D), TEMB ** -0.5, 0.375)
    time_bias = noise(key_of[3], (D,), 0.3, 1.5)
    gain_one = jnp.clip(1.0 + 0.1 * jax.random.normal(key_of[4], (D,), jnp.float32), 0.5, 1.5).astype(jnp.bfloat16)
    shift_one = noise(key_of[5], (D,), 0.3, 1.5)
    w_qkv = noise(key_of[6], (D, 3 * D), D ** -0.5, 0.1875)
    w_out = noise(key_of[7], (D, D), (max(1, 3 * D // LEN)) ** -0.5, 1.25)
    gain_two = jnp.clip(1.0 + 0.1 * jax.random.normal(key_of[8], (D,), jnp.float32), 0.5, 1.5).astype(jnp.bfloat16)
    shift_two = noise(key_of[9], (D,), 0.3, 1.5)
    w_up = noise(key_of[10], (D, FF), D ** -0.5, 0.1875)
    b_up = noise(key_of[11], (FF,), 0.5, 2.5)
    w_down = noise(key_of[12], (FF, D), FF ** -0.5, 0.09375)
    b_down = noise(key_of[13], (D,), 0.3, 1.5)
    cotangent = bell_draw_with(key_of[14], (SEQUENCES, LEN, D), 1.0, 6.0, ((0, 16), (1, 2)), (0, 2, 16, 2.0))
    return {"tokens": tokens, "noise_times": noise_times, "time_proj": time_proj, "time_bias": time_bias, "gain_one": gain_one, "shift_one": shift_one, "w_qkv": w_qkv, "w_out": w_out, "gain_two": gain_two, "shift_two": shift_two, "w_up": w_up, "b_up": b_up, "w_down": w_down, "b_down": b_down, "cotangent": cotangent}


@jax.custom_vjp
def low(v):
    return lax.optimization_barrier(v.astype(jnp.bfloat16)).astype(jnp.float32)

@jax.custom_vjp
def low_back(v):
    return v

def low_keep(v):
    return (low(v), None)

def low_pass(kept, grad):
    return (grad,)

def back_keep(v):
    return (v, None)

def back_low(kept, grad):
    return (low(grad),)
low.defvjp(low_keep, low_pass)
low_back.defvjp(back_keep, back_low)

def matmul(left_side, right_side):
    return jnp.dot(left_side, right_side, precision=lax.Precision.HIGHEST)

def layer_norm(hidden, gain_vec, shift_vec):
    center = hidden - lax.optimization_barrier(jnp.mean(hidden, axis=-1, keepdims=True))
    spread = lax.optimization_barrier(jnp.mean(center * center, axis=-1, keepdims=True))
    return center * lax.rsqrt(spread + 1e-05) * gain_vec + shift_vec

def noise_table(noise_steps):
    halves = TEMB // 2
    frequency = jnp.exp(-math.log(10000.0) * jnp.arange(halves, dtype=jnp.float32) / halves)
    angles = noise_steps.astype(jnp.float32)[:, None] * frequency[None, :]
    return jnp.concatenate([jnp.sin(angles), jnp.cos(angles)], axis=-1)

def rotary_tables():
    halves = HD // 2
    frequency = jnp.exp(-math.log(10000.0) * jnp.arange(halves, dtype=jnp.float32) / halves)
    angles = jnp.arange(LEN, dtype=jnp.float32)[:, None] * frequency[None, :]
    angles = jnp.concatenate([angles, angles], axis=-1)[:, None, :]
    return (jnp.cos(angles), jnp.sin(angles))

def rotate(values, cosine, sine_tab):
    halves = values.shape[-1] // 2
    turned = jnp.concatenate([-values[..., halves:], values[..., :halves]], axis=-1)
    return values * cosine + turned * sine_tab

def attention(head_parts):
    cosine, sine_tab = rotary_tables()
    scaling = 1.0 / math.sqrt(HD)
    queries = low(rotate(head_parts[:, :, 0], cosine, sine_tab))
    keys_rot = low(rotate(head_parts[:, :, 1], cosine, sine_tab))
    values = head_parts[:, :, 2]
    scores = low_back(jnp.einsum('gqhd,gkhd->ghqk', queries, keys_rot, precision=lax.Precision.HIGHEST) * scaling)
    weights = low(jax.nn.softmax(scores, axis=-1))
    return jnp.einsum('ghqk,gkhd->gqhd', weights, values, precision=lax.Precision.HIGHEST)

def forward(hidden_in, embed_table, time_proj, time_bias, gain_one, shift_one, w_qkv, w_out, gain_two, shift_two, w_up, b_up, w_down, b_down):
    batch_size = hidden_in.shape[0]
    time_embed = matmul(embed_table, time_proj) + time_bias
    hidden_zero = hidden_in + time_embed[:, None, :]
    normed_one = low(layer_norm(hidden_zero, gain_one, shift_one))
    projected = low(low_back(matmul(normed_one, w_qkv)))
    head_parts = projected.reshape(batch_size, LEN, 3, HEADS, HD)
    attended = jax.checkpoint(attention)(head_parts).reshape(batch_size, LEN, D)
    attended = low(low_back(attended))
    hidden_one = hidden_zero + low_back(matmul(attended, w_out))
    normed_two = low(layer_norm(hidden_one, gain_two, shift_two))
    upward = low_back(matmul(normed_two, w_up) + b_up)
    active = low(jax.nn.gelu(upward))
    return hidden_one + low_back(matmul(active, w_down) + b_down)

def reference(tokens, noise_times, time_proj, time_bias, gain_one, shift_one, w_qkv, w_out, gain_two, shift_two, w_up, b_up, w_down, b_down, cotangent):
    params = tuple((member.astype(jnp.float32) for member in (time_proj, time_bias, gain_one, shift_one, w_qkv, w_out, gain_two, shift_two, w_up, b_up, w_down, b_down)))
    per_group = math.gcd(SEQUENCES, max(1, 4096 // LEN))
    groups = SEQUENCES // per_group
    inputs = tokens.astype(jnp.float32).reshape(groups, per_group, LEN, D)
    steps_in = noise_times.reshape(groups, per_group)
    seeds = cotangent.astype(jnp.float32).reshape(groups, per_group, LEN, D)

    def group_step(totals, sliced):
        hidden_in, noise_steps, incoming = sliced
        embed_table = low(noise_table(noise_steps))

        def run_layer(hidden, *weights):
            return forward(hidden, embed_table, *weights)
        result, pullback = jax.vjp(run_layer, hidden_in, *params)
        gradients = pullback(incoming)
        totals = tuple((total + gradient for total, gradient in zip(totals, gradients[1:])))
        return (totals, (result, gradients[0]))
    starts = tuple((jnp.zeros_like(param) for param in params))
    totals, (results, grad_in) = lax.scan(group_step, starts, (inputs, steps_in, seeds))
    mixed_out = results.reshape(SEQUENCES, LEN, D).astype(jnp.bfloat16)
    grad_tokens = grad_in.reshape(SEQUENCES, LEN, D).astype(jnp.bfloat16)
    return (mixed_out, grad_tokens, totals[0], totals[1], totals[2], totals[3], totals[4], totals[5], totals[6], totals[7], totals[8], totals[9], totals[10], totals[11])
```

```python
import math

import jax
import jax.numpy as jnp
from jax import lax
from jax.sharding import PartitionSpec as P

HD = 64
TEMB = 256


def layer_norm(hidden, gain_vec, shift_vec):
    center = hidden - jnp.mean(hidden, axis=-1, keepdims=True)
    spread = jnp.mean(center * center, axis=-1, keepdims=True)
    return center * lax.rsqrt(spread + 1e-05) * gain_vec + shift_vec


def noise_table(noise_steps):
    halves = TEMB // 2
    frequency = jnp.exp(-math.log(10000.0) * jnp.arange(halves, dtype=jnp.float32) / halves)
    angles = noise_steps.astype(jnp.float32)[:, None] * frequency[None, :]
    return jnp.concatenate([jnp.sin(angles), jnp.cos(angles)], axis=-1)


def rotary_tables(length):
    halves = HD // 2
    frequency = jnp.exp(-math.log(10000.0) * jnp.arange(halves, dtype=jnp.float32) / halves)
    angles = jnp.arange(length, dtype=jnp.float32)[:, None] * frequency[None, :]
    angles = jnp.concatenate([angles, angles], axis=-1)[:, None, :]
    return (jnp.cos(angles), jnp.sin(angles))


def rotate(values, cosine, sine_tab):
    halves = values.shape[-1] // 2
    turned = jnp.concatenate([-values[..., halves:], values[..., :halves]], axis=-1)
    return values * cosine + turned * sine_tab


def unrotate(gradient, cosine, sine_tab):
    halves = gradient.shape[-1] // 2
    scaled = gradient * sine_tab
    turned = jnp.concatenate([scaled[..., halves:], -scaled[..., :halves]], axis=-1)
    return gradient * cosine + turned


def product(left_side, right_side):
    return jnp.dot(left_side, right_side, preferred_element_type=jnp.float32)


def contract_rows(left_side, right_side):
    return jnp.einsum("ra,rb->ab", left_side, right_side, preferred_element_type=jnp.float32)


def times_transpose(left_side, right_side):
    return jnp.einsum("rb,ab->ra", left_side, right_side, preferred_element_type=jnp.float32)


def split_heads(received):
    batch_size, length = (received.shape[0], received.shape[1])
    local_heads = received.shape[-1] // HD
    split_view = received.reshape(batch_size, length, 3, local_heads, HD)
    cosine, sine_tab = rotary_tables(length)
    queries = rotate(split_view[:, :, 0].astype(jnp.float32), cosine, sine_tab).astype(jnp.bfloat16)
    keys_rot = rotate(split_view[:, :, 1].astype(jnp.float32), cosine, sine_tab).astype(
        jnp.bfloat16
    )
    return (queries, keys_rot, split_view[:, :, 2], cosine, sine_tab)


def attend_items(received):
    batch_size, length = (received.shape[0], received.shape[1])
    scaling = 1.0 / math.sqrt(HD)
    queries, keys_rot, values, cosine, sine_tab = split_heads(received)
    scores = (
        jnp.einsum("gqhd,gkhd->ghqk", queries, keys_rot, preferred_element_type=jnp.float32)
        * scaling
    )
    highest = jnp.max(scores, axis=-1, keepdims=True)
    exponent = jnp.exp(scores - highest)
    totals = jnp.sum(exponent, axis=-1, keepdims=True)
    prob_rows = (exponent / totals).astype(jnp.bfloat16)
    log_total = (highest + jnp.log(totals))[..., 0]
    attended = jnp.einsum("ghqk,gkhd->gqhd", prob_rows, values, preferred_element_type=jnp.float32)
    attended = attended.astype(jnp.bfloat16).reshape(batch_size, length, 1, -1)
    return (received, attended, log_total)


def attention_grad(received, log_total, grad_heads):
    batch_size, length = (received.shape[0], received.shape[1])
    scaling = 1.0 / math.sqrt(HD)
    queries, keys_rot, values, cosine, sine_tab = split_heads(received)
    scores = (
        jnp.einsum("gqhd,gkhd->ghqk", queries, keys_rot, preferred_element_type=jnp.float32)
        * scaling
    )
    prob_rows = jnp.exp(scores - log_total[..., None])
    grad_out = grad_heads.reshape(batch_size, length, values.shape[2], HD)
    grad_probs = jnp.einsum("gqhd,gkhd->ghqk", grad_out, values, preferred_element_type=jnp.float32)
    grad_values = jnp.einsum(
        "ghqk,gqhd->gkhd",
        prob_rows.astype(jnp.bfloat16),
        grad_out,
        preferred_element_type=jnp.float32,
    )
    inner_sum = jnp.sum(prob_rows * grad_probs, axis=-1, keepdims=True)
    grad_scores = (prob_rows * (grad_probs - inner_sum)).astype(jnp.bfloat16)
    grad_queries = (
        jnp.einsum("ghqk,gkhd->gqhd", grad_scores, keys_rot, preferred_element_type=jnp.float32)
        * scaling
    )
    grad_keys = (
        jnp.einsum("ghqk,gqhd->gkhd", grad_scores, queries, preferred_element_type=jnp.float32)
        * scaling
    )
    stacked = jnp.stack(
        [
            unrotate(grad_queries, cosine, sine_tab),
            unrotate(grad_keys, cosine, sine_tab),
            grad_values,
        ],
        axis=2,
    )
    return stacked.astype(jnp.bfloat16).reshape(batch_size, length, 3, 1, -1)


def gather_sequences(values):
    return lax.all_to_all(values, "tok", split_axis=0, concat_axis=1, tiled=True)


def return_positions(values):
    return lax.all_to_all(values, "tok", split_axis=1, concat_axis=0, tiled=True)


def group_scatter(parts, own, size, axis, perm_of):
    total = lax.dynamic_index_in_dim(parts, own, 0, keepdims=False).astype(jnp.float32)
    for shift in range(1, size):
        piece = lax.dynamic_index_in_dim(parts, (own + shift) % size, 0, keepdims=False)
        total = total + lax.ppermute(piece, axis, perm_of(shift)).astype(jnp.float32)
    return total.astype(jnp.bfloat16)


def group_gather(piece, own, size, axis, perm_of):
    held = jnp.zeros((size,) + piece.shape, piece.dtype)
    held = lax.dynamic_update_index_in_dim(held, piece, own, 0)
    for shift in range(1, size):
        other = lax.ppermute(piece, axis, perm_of(shift))
        held = lax.dynamic_update_index_in_dim(held, other, (own - shift) % size, 0)
    return held


def scatter_sum(gradient):
    seq_ways, tok_ways = lax.axis_size("seq"), lax.axis_size("tok")
    outer, middle = 4, seq_ways // 8
    place, turn = lax.axis_index("seq"), lax.axis_index("tok")
    core, mid, out = place % 2, (place // 2) % middle, place // (2 * middle)

    def core_perm(shift):
        return [(i, i ^ 1) for i in range(seq_ways)]

    def mid_perm(shift):
        return [
            (i, (i // (2 * middle)) * 2 * middle + ((i // 2 + shift) % middle) * 2 + i % 2)
            for i in range(seq_ways)
        ]

    def out_perm(shift):
        return [(i, (i + shift * 2 * middle) % seq_ways) for i in range(seq_ways)]

    def tok_perm(shift):
        return [(i, (i + shift) % tok_ways) for i in range(tok_ways)]

    rows, width = gradient.shape[0] // seq_ways, gradient.shape[1]
    parts = gradient.astype(jnp.bfloat16).reshape(outer * middle, 2, rows, width)
    parts = group_scatter(jnp.swapaxes(parts, 0, 1), core, 2, "seq", core_perm)
    parts = parts.reshape(outer, middle, rows, 2, tok_ways, width // (2 * tok_ways))
    first = jnp.transpose(parts[:, :, :, 0], (1, 3, 0, 2, 4))
    second = jnp.transpose(parts[:, :, :, 1], (3, 1, 0, 2, 4))
    first = group_scatter(first, mid, middle, "seq", mid_perm)
    second = group_scatter(second, turn, tok_ways, "tok", tok_perm)
    first = group_scatter(first, turn, tok_ways, "tok", tok_perm)
    second = group_scatter(second, mid, middle, "seq", mid_perm)
    both = jnp.stack([first, second], axis=1)
    both = group_scatter(both, out, outer, "seq", out_perm)
    both = group_gather(both, turn, tok_ways, "tok", tok_perm)
    return jnp.transpose(both, (2, 1, 0, 3)).reshape(rows, width).T.astype(jnp.float32)


def body(
    tokens,
    noise_times,
    time_proj,
    time_bias,
    gain_one,
    shift_one,
    w_qkv,
    w_out,
    gain_two,
    shift_two,
    w_up,
    b_up,
    w_down,
    b_down,
    cotangent,
):
    seq_ways, tok_ways = lax.axis_size("seq"), lax.axis_size("tok")
    model_width = tokens.shape[-1]
    seq_count, length = tokens.shape[0] // tok_ways, tokens.shape[1] * tok_ways
    row_count = seq_count * length
    all_times = lax.all_gather(noise_times, "seq", tiled=True)
    own_times = lax.dynamic_slice_in_dim(
        noise_times, lax.axis_index("tok") * seq_count, seq_count
    )
    embed_table = noise_table(own_times).astype(jnp.bfloat16)
    time_embed = product(embed_table, time_proj) + time_bias.astype(jnp.float32)
    tokens = gather_sequences(tokens)
    incoming = gather_sequences(cotangent).reshape(row_count, model_width)
    hidden_zero = (tokens.astype(jnp.float32) + time_embed[:, None, :]).reshape(
        row_count, model_width
    )
    normed_one, pull_one = jax.vjp(
        layer_norm, hidden_zero, gain_one.astype(jnp.float32), shift_one.astype(jnp.float32)
    )
    normed_one = normed_one.astype(jnp.bfloat16)
    projected = product(normed_one, w_qkv).astype(jnp.bfloat16)
    received, attended, log_total = attend_items(
        projected.reshape(seq_count, length, 3, 1, model_width)
    )
    attended = attended.reshape(row_count, model_width)
    hidden_one = hidden_zero + product(attended, w_out)
    normed_two, pull_two = jax.vjp(
        layer_norm, hidden_one, gain_two.astype(jnp.float32), shift_two.astype(jnp.float32)
    )
    normed_two = normed_two.astype(jnp.bfloat16)
    upward = product(normed_two, w_up) + b_up.astype(jnp.float32)
    active, pull_gelu = jax.vjp(jax.nn.gelu, upward)
    active = active.astype(jnp.bfloat16)
    out_wdown = scatter_sum(contract_rows(incoming, active))
    result = hidden_one + (product(active, w_down) + b_down.astype(jnp.float32))
    mixed_out = return_positions(
        result.astype(jnp.bfloat16).reshape(seq_count, length, model_width)
    )
    sum_down = jnp.sum(incoming, axis=0, dtype=jnp.float32)
    grad_active = times_transpose(incoming, w_down)
    (grad_upward,) = pull_gelu(grad_active)
    grad_upward = grad_upward.astype(jnp.bfloat16)
    sum_up = jnp.sum(grad_upward, axis=0, dtype=jnp.float32)
    out_wup = scatter_sum(contract_rows(grad_upward, normed_two))
    grad_norm_two = times_transpose(grad_upward, w_up)
    grad_hidden_two, grad_gain_two, grad_shift_two = pull_two(grad_norm_two)
    grad_hidden_one = incoming.astype(jnp.float32) + grad_hidden_two
    grad_attn = grad_hidden_one.astype(jnp.bfloat16)
    out_wout = scatter_sum(contract_rows(grad_attn, attended))
    grad_mixed = times_transpose(grad_attn, w_out).astype(jnp.bfloat16)
    grad_parts = attention_grad(
        received, log_total, grad_mixed.reshape(seq_count, length, 1, model_width)
    ).reshape(row_count, 3 * model_width)
    out_wqkv = scatter_sum(contract_rows(grad_parts, normed_one))
    grad_norm_one = times_transpose(grad_parts, w_qkv)
    grad_hidden_zero, grad_gain_one, grad_shift_one = pull_one(grad_norm_one)
    grad_total = grad_hidden_one + grad_hidden_zero
    grad_tokens = return_positions(
        grad_total.astype(jnp.bfloat16).reshape(seq_count, length, model_width)
    )
    grad_embed = jnp.sum(grad_total.reshape(seq_count, length, model_width), axis=1)
    wide = sum_up.shape[0] // model_width
    small = jnp.concatenate(
        [
            grad_embed.reshape(seq_count, seq_ways, -1).swapaxes(0, 1),
            grad_gain_one.reshape(seq_ways, 1, -1),
            grad_shift_one.reshape(seq_ways, 1, -1),
            grad_gain_two.reshape(seq_ways, 1, -1),
            grad_shift_two.reshape(seq_ways, 1, -1),
            sum_down.reshape(seq_ways, 1, -1),
            sum_up.reshape(seq_ways, wide, -1),
        ],
        axis=1,
    )
    small = lax.all_to_all(small, "seq", split_axis=0, concat_axis=0, tiled=True)
    small = lax.all_gather(small, "tok", axis=1)
    embeds = small[:, :, :seq_count].reshape(-1, small.shape[-1])
    out_proj = jnp.dot(
        noise_table(all_times).astype(jnp.bfloat16).astype(jnp.float32).T,
        embeds,
        precision=lax.Precision.HIGHEST,
    )
    out_bias = jnp.sum(embeds, axis=0)
    sums = jnp.sum(small[:, :, seq_count:], axis=(0, 1))
    return (
        mixed_out,
        grad_tokens,
        out_proj,
        out_bias,
        sums[0],
        sums[1],
        out_wqkv,
        out_wout,
        sums[2],
        sums[3],
        out_wup,
        sums[5:].reshape(-1),
        out_wdown,
        sums[4],
    )


def solution(mesh):
    in_specs = (
        P("seq", "tok", None),
        P("seq"),
        P(),
        P(),
        P(),
        P(),
        P(),
        P(),
        P(),
        P(),
        P(),
        P(),
        P(),
        P(),
        P("seq", "tok", None),
    )
    out_specs = (
        P("seq", "tok", None),
        P("seq", "tok", None),
        P(None, "seq"),
        P("seq"),
        P("seq"),
        P("seq"),
        P(None, "seq"),
        P(None, "seq"),
        P("seq"),
        P("seq"),
        P(None, "seq"),
        P("seq"),
        P(None, "seq"),
        P("seq"),
    )
    return jax.shard_map(body, mesh=mesh, in_specs=in_specs, out_specs=out_specs, check_vma=False)
```

```python
import math

import jax
import jax.numpy as jnp
from jax import lax
from jax.experimental import pallas as pl
from jax.experimental.pallas import tpu as pltpu
from jax.sharding import PartitionSpec as P

HD = 64
TEMB = 256
VMEM_LIMIT = 64 * 1024 * 1024 - 65536


def layer_norm(hidden, gain_vec, shift_vec):
    center = hidden - jnp.mean(hidden, axis=-1, keepdims=True)
    spread = jnp.mean(center * center, axis=-1, keepdims=True)
    return center * lax.rsqrt(spread + 1e-05) * gain_vec + shift_vec


def noise_table(noise_steps):
    halves = TEMB // 2
    frequency = jnp.exp(-math.log(10000.0) * jnp.arange(halves, dtype=jnp.float32) / halves)
    angles = noise_steps.astype(jnp.float32)[:, None] * frequency[None, :]
    return jnp.concatenate([jnp.sin(angles), jnp.cos(angles)], axis=-1)


def rotary_tables(length):
    halves = HD // 2
    frequency = jnp.exp(-math.log(10000.0) * jnp.arange(halves, dtype=jnp.float32) / halves)
    angles = jnp.arange(length, dtype=jnp.float32)[:, None] * frequency[None, :]
    angles = jnp.concatenate([angles, angles], axis=-1)[:, None, :]
    return (jnp.cos(angles), jnp.sin(angles))


def rotate(values, cosine, sine_tab):
    halves = values.shape[-1] // 2
    turned = jnp.concatenate([-values[..., halves:], values[..., :halves]], axis=-1)
    return values * cosine + turned * sine_tab


def unrotate(gradient, cosine, sine_tab):
    halves = gradient.shape[-1] // 2
    scaled = gradient * sine_tab
    turned = jnp.concatenate([scaled[..., halves:], -scaled[..., :halves]], axis=-1)
    return gradient * cosine + turned


def product(left_side, right_side):
    return jnp.dot(left_side, right_side, preferred_element_type=jnp.float32)


def contract_rows(left_side, right_side):
    return jnp.einsum("ra,rb->ab", left_side, right_side, preferred_element_type=jnp.float32)


def times_transpose(left_side, right_side):
    return jnp.einsum("rb,ab->ra", left_side, right_side, preferred_element_type=jnp.float32)


def split_heads(received):
    batch_size, length = (received.shape[0], received.shape[1])
    local_heads = received.shape[-1] // HD
    split_view = received.reshape(batch_size, length, 3, local_heads, HD)
    cosine, sine_tab = rotary_tables(length)
    queries = rotate(split_view[:, :, 0].astype(jnp.float32), cosine, sine_tab).astype(jnp.bfloat16)
    keys_rot = rotate(split_view[:, :, 1].astype(jnp.float32), cosine, sine_tab).astype(
        jnp.bfloat16
    )
    return (queries, keys_rot, split_view[:, :, 2], cosine, sine_tab)


def attend_items(received):
    batch_size, length = (received.shape[0], received.shape[1])
    scaling = 1.0 / math.sqrt(HD)
    queries, keys_rot, values, cosine, sine_tab = split_heads(received)
    scores = (
        jnp.einsum("gqhd,gkhd->ghqk", queries, keys_rot, preferred_element_type=jnp.float32)
        * scaling
    )
    highest = jnp.max(scores, axis=-1, keepdims=True)
    exponent = jnp.exp(scores - highest)
    totals = jnp.sum(exponent, axis=-1, keepdims=True)
    prob_rows = (exponent / totals).astype(jnp.bfloat16)
    log_total = (highest + jnp.log(totals))[..., 0]
    attended = jnp.einsum("ghqk,gkhd->gqhd", prob_rows, values, preferred_element_type=jnp.float32)
    attended = attended.astype(jnp.bfloat16).reshape(batch_size, length, 1, -1)
    return (received, attended, log_total)


def attention_grad(received, log_total, grad_heads):
    batch_size, length = (received.shape[0], received.shape[1])
    scaling = 1.0 / math.sqrt(HD)
    queries, keys_rot, values, cosine, sine_tab = split_heads(received)
    scores = (
        jnp.einsum("gqhd,gkhd->ghqk", queries, keys_rot, preferred_element_type=jnp.float32)
        * scaling
    )
    prob_rows = jnp.exp(scores - log_total[..., None])
    grad_out = grad_heads.reshape(batch_size, length, values.shape[2], HD)
    grad_probs = jnp.einsum("gqhd,gkhd->ghqk", grad_out, values, preferred_element_type=jnp.float32)
    grad_values = jnp.einsum(
        "ghqk,gqhd->gkhd",
        prob_rows.astype(jnp.bfloat16),
        grad_out,
        preferred_element_type=jnp.float32,
    )
    inner_sum = jnp.sum(prob_rows * grad_probs, axis=-1, keepdims=True)
    grad_scores = (prob_rows * (grad_probs - inner_sum)).astype(jnp.bfloat16)
    grad_queries = (
        jnp.einsum("ghqk,gkhd->gqhd", grad_scores, keys_rot, preferred_element_type=jnp.float32)
        * scaling
    )
    grad_keys = (
        jnp.einsum("ghqk,gqhd->gkhd", grad_scores, queries, preferred_element_type=jnp.float32)
        * scaling
    )
    stacked = jnp.stack(
        [
            unrotate(grad_queries, cosine, sine_tab),
            unrotate(grad_keys, cosine, sine_tab),
            grad_values,
        ],
        axis=2,
    )
    return stacked.astype(jnp.bfloat16).reshape(batch_size, length, 3, 1, -1)


def gather_sequences(values):
    return lax.all_to_all(values, "tok", split_axis=0, concat_axis=1, tiled=True)


def return_positions(values):
    return lax.all_to_all(values, "tok", split_axis=1, concat_axis=0, tiled=True)


def group_scatter(parts, own, size, axis, perm_of):
    total = lax.dynamic_index_in_dim(parts, own, 0, keepdims=False).astype(jnp.float32)
    for shift in range(1, size):
        piece = lax.dynamic_index_in_dim(parts, (own + shift) % size, 0, keepdims=False)
        total = total + lax.ppermute(piece, axis, perm_of(shift)).astype(jnp.float32)
    return total.astype(jnp.bfloat16)


def group_gather(piece, own, size, axis, perm_of):
    held = jnp.zeros((size,) + piece.shape, piece.dtype)
    held = lax.dynamic_update_index_in_dim(held, piece, own, 0)
    for shift in range(1, size):
        other = lax.ppermute(piece, axis, perm_of(shift))
        held = lax.dynamic_update_index_in_dim(held, other, (own - shift) % size, 0)
    return held


def scatter_sum(gradient):
    seq_ways, tok_ways = lax.axis_size("seq"), lax.axis_size("tok")
    outer, middle = 4, seq_ways // 8
    place, turn = lax.axis_index("seq"), lax.axis_index("tok")
    core, mid, out = place % 2, (place // 2) % middle, place // (2 * middle)

    def core_perm(shift):
        return [(i, i ^ 1) for i in range(seq_ways)]

    def mid_perm(shift):
        return [
            (i, (i // (2 * middle)) * 2 * middle + ((i // 2 + shift) % middle) * 2 + i % 2)
            for i in range(seq_ways)
        ]

    def out_perm(shift):
        return [(i, (i + shift * 2 * middle) % seq_ways) for i in range(seq_ways)]

    def tok_perm(shift):
        return [(i, (i + shift) % tok_ways) for i in range(tok_ways)]

    rows, width = gradient.shape[0] // seq_ways, gradient.shape[1]
    parts = gradient.astype(jnp.bfloat16).reshape(outer * middle, 2, rows, width)
    parts = group_scatter(jnp.swapaxes(parts, 0, 1), core, 2, "seq", core_perm)
    parts = parts.reshape(outer, middle, rows, 2, tok_ways, width // (2 * tok_ways))
    first = jnp.transpose(parts[:, :, :, 0], (1, 3, 0, 2, 4))
    second = jnp.transpose(parts[:, :, :, 1], (3, 1, 0, 2, 4))
    first = group_scatter(first, mid, middle, "seq", mid_perm)
    second = group_scatter(second, turn, tok_ways, "tok", tok_perm)
    first = group_scatter(first, turn, tok_ways, "tok", tok_perm)
    second = group_scatter(second, mid, middle, "seq", mid_perm)
    both = jnp.stack([first, second], axis=1)
    both = group_scatter(both, out, outer, "seq", out_perm)
    both = group_gather(both, turn, tok_ways, "tok", tok_perm)
    return jnp.transpose(both, (2, 1, 0, 3)).reshape(rows, width).T.astype(jnp.float32)


MESH_ID = pl.DeviceIdType.MESH
BF = jnp.bfloat16
F32 = jnp.float32
UNITS = 12
UNIT_DOWN, UNIT_UP, UNIT_OUT, UNIT_QKV = 0, 4, 8, 9
ORDERS = "xyxyxyxyxyxy"
MIB = 1 << 20


def mm(left, right, left_dim, right_dim):
    return lax.dot_general(
        left, right, (((left_dim,), (right_dim,)), ((), ())), preferred_element_type=F32
    )


def rotated_partner(values):
    lane = lax.broadcasted_iota(jnp.int32, values.shape, 1)
    return jnp.where(lane % 64 < 32, pltpu.roll(values, 96, 1), pltpu.roll(values, 32, 1))


def backward_kernel(
    incoming_in,
    active_in,
    slope_in,
    normed_two_in,
    hidden_one_in,
    attended_in,
    qkv_in,
    normed_one_in,
    hidden_zero_in,
    w_down,
    w_up,
    w_out,
    w_qkv,
    vectors,
    cosine,
    sine,
    mixed_out,
    tokens_out,
    shares_out,
    small_out,
    partial,
    core_send,
    core_recv,
    recv_one,
    recv_two,
    recv_three,
    weight,
    wide_a,
    wide_g,
    inc,
    normed,
    hidden,
    hidden_z,
    total,
    grad_attn,
    attended,
    grad_mixed,
    mixed,
    message,
    small_recv,
    vec_rows,
    load_sem,
    weight_sem,
    core_ssem,
    core_rsem,
    credit,
    one_ssem,
    one_rsem,
    two_ssem,
    two_rsem,
    three_ssem,
    three_rsem,
    gather_ssem,
    gather_rsem,
    small_ssem,
    small_rsem,
    back_ssem,
    back_rsem,
):
    place, turn = lax.axis_index("seq"), lax.axis_index("tok")
    core, xx, zz = place % 2, (place // 2) % 2, place // 4
    yy = turn
    me = place * 2 + turn
    devices = 32

    def at_seq(z, x, c):
        return ((z * 2 + x) * 2 + c, turn)

    core_peer = at_seq(zz, xx, 1 - core)
    x_peer = at_seq(zz, 1 - xx, core)
    y_peer = (place, 1 - turn)

    def load(index, source, target):
        return pltpu.make_async_copy(source, target, load_sem.at[index])

    def load_weight(tile):
        if tile < 4:
            source = w_down.at[pl.ds(tile * 1024, 1024), :]
        elif tile < 8:
            source = w_up.at[:, pl.ds((tile - 4) * 1024, 1024)]
        elif tile == 8:
            source = w_out
        else:
            source = w_qkv.at[:, pl.ds((tile - 9) * 1024, 1024)]
        return pltpu.make_async_copy(source, weight.at[tile % 2], weight_sem.at[tile % 2])

    load(0, incoming_in, inc).start()
    for part in range(4):
        columns = pl.ds(part * 1024, 1024)
        load(1 + part, active_in.at[:, columns], wide_a.at[:, columns]).start()
    load_weight(0).start()
    load_weight(1).start()
    load(5, slope_in, wide_g).start()
    load(6, hidden_one_in, hidden).start()
    load(7, normed_two_in, normed).start()
    load(8, attended_in, attended).start()
    load(9, hidden_zero_in, hidden_z).start()

    barrier = pltpu.get_barrier_semaphore()

    def greet(step, carry):
        other = lax.rem(me + step, devices)
        pl.semaphore_signal(
            barrier, inc=1, device_id=(other // 2, other % 2), device_id_type=MESH_ID
        )
        return carry

    lax.fori_loop(1, devices, greet, 0)
    pl.semaphore_wait(barrier, devices - 1)

    def remote(source, target, send, recv, device):
        return pltpu.make_async_remote_copy(
            src_ref=source,
            dst_ref=target,
            send_sem=send,
            recv_sem=recv,
            device_id=device,
            device_id_type=MESH_ID,
        )

    def core_copy(unit):
        slot = unit % 4
        return remote(
            core_send.at[slot],
            core_recv.at[slot],
            core_ssem.at[slot],
            core_rsem.at[slot],
            core_peer,
        )

    def one_copy(unit):
        if ORDERS[unit] == "x":
            source, device = partial.at[2 * unit + 1 - xx], x_peer
        else:
            source, device = partial.at[pl.ds(2 * unit, 2), 1 - yy], y_peer
        return remote(
            source, recv_one.at[unit], one_ssem.at[unit], one_rsem.at[unit], device
        )

    def two_copy(unit):
        if ORDERS[unit] == "x":
            source, device = partial.at[2 * unit + xx, 1 - yy], y_peer
        else:
            source, device = partial.at[2 * unit + 1 - xx, yy], x_peer
        return remote(
            source, recv_two.at[unit], two_ssem.at[unit], two_rsem.at[unit], device
        )

    def three_copy(unit, step):
        other = (zz + step) % 4
        index = 3 * unit + step - 1
        return remote(
            partial.at[2 * unit + xx, yy, other],
            recv_three.at[unit, step - 1],
            three_ssem.at[index],
            three_rsem.at[index],
            at_seq(other, xx, core),
        )

    def gather_copy(unit):
        return remote(
            shares_out.at[unit, yy],
            shares_out.at[unit, yy],
            gather_ssem.at[unit],
            gather_rsem.at[unit],
            y_peer,
        )

    def start_core(unit):
        if unit >= 4:
            pl.semaphore_wait(credit.at[unit % 4], 1)
        core_copy(unit).start()

    def stage_core(unit):
        core_copy(unit).wait_recv()

        def add(index, carry):
            x, h, z = index // 8, (index // 4) % 2, index % 4
            partial[2 * unit + x, h, z] = (
                partial[2 * unit + x, h, z] + core_recv[unit % 4, x, h, z]
            )
            return carry

        lax.fori_loop(0, 16, add, 0)
        if unit < UNITS - 4:
            pl.semaphore_signal(
                credit.at[unit % 4], inc=1, device_id=core_peer, device_id_type=MESH_ID
            )
        one_copy(unit).start()

    def stage_one(unit):
        one_copy(unit).wait_recv()

        def add(index, carry):
            a, z = index // 4, index % 4
            if ORDERS[unit] == "x":
                partial[2 * unit + xx, a, z] = partial[2 * unit + xx, a, z] + recv_one[unit, a, z]
            else:
                partial[2 * unit + a, yy, z] = partial[2 * unit + a, yy, z] + recv_one[unit, a, z]
            return carry

        lax.fori_loop(0, 8, add, 0)
        two_copy(unit).start()

    def stage_two(unit):
        two_copy(unit).wait_recv()

        def add(z, carry):
            partial[2 * unit + xx, yy, z] = partial[2 * unit + xx, yy, z] + recv_two[unit, z]
            return carry

        lax.fori_loop(0, 4, add, 0)
        for step in (2, 1, 3):
            three_copy(unit, step).start()

    def stage_three(unit):
        value = partial[2 * unit + xx, yy, zz].astype(F32)
        for step in (1, 2, 3):
            three_copy(unit, step).wait_recv()
        for step in (1, 2, 3):
            value = value + recv_three[unit, step - 1].astype(F32)
        shares_out[unit, yy] = value.astype(BF)
        gather_copy(unit).start()

    def stage_gather(unit):
        gather_copy(unit).wait_recv()

    stages = (stage_core, stage_one, stage_two, stage_three, stage_gather)
    plan = schedule()
    cursor = [0]

    def pump(label):
        while cursor[0] < len(plan):
            kind, stage, unit = plan[cursor[0]]
            cursor[0] += 1
            if kind == "mark":
                assert stage == label
                return
            if stage == -1:
                start_core(unit)
            else:
                stages[stage](unit)

    def wait_sent(units):
        for unit in units:
            core_copy(unit).wait_send()

    def place_block(value, unit, x, z):
        low, high = value[:64], value[64:]
        own = jnp.where(core == 0, low, high).astype(BF)
        other = jnp.where(core == 0, high, low).astype(BF)
        for h in range(2):
            partial[2 * unit + x, h, z] = own[:, h * 512 : (h + 1) * 512]
            core_send[unit % 4, x, h, z] = other[:, h * 512 : (h + 1) * 512]

    load(0, incoming_in, inc).wait()

    def down_unit(unit):
        def step(m, carry):
            rows = pl.ds(pl.multiple_of(m * 512, 512), 512)
            value = mm(inc[:, rows], wide_a[:, unit * 1024 : (unit + 1) * 1024], 0, 0)
            for q in range(4):
                place_block(value[q * 128 : (q + 1) * 128], unit, q % 2, 2 * m + q // 2)
            return carry

        lax.fori_loop(0, 2, step, 0)

    for part in range(4):
        columns = pl.ds(part * 1024, 1024)
        load(1 + part, active_in.at[:, columns], wide_a.at[:, columns]).wait()
        down_unit(UNIT_DOWN + part)
        pump("down%d" % part)

    message[...] = jnp.zeros_like(message)
    vec_rows[...] = jnp.zeros_like(vec_rows)
    load(5, slope_in, wide_g).wait()
    load(6, hidden_one_in, hidden).wait()
    for tile in range(4):
        load_weight(tile).wait()
        columns = slice(tile * 1024, (tile + 1) * 1024)

        def rows_step(m, carry, tile=tile, columns=columns):
            rows = pl.ds(pl.multiple_of(m * 256, 256), 256)
            grad = mm(inc[rows, :], weight[tile % 2], 1, 1) * wide_g[rows, columns].astype(F32)
            grad = grad.astype(BF)
            wide_g[rows, columns] = grad
            return carry + jnp.sum(grad.astype(F32), axis=0, keepdims=True)

        sums = lax.fori_loop(0, 2, rows_step, jnp.zeros((1, 1024), F32))
        for pair in range(2):
            for row in range(4):
                at = pair * 512 + row * 128
                message[2 * tile + pair, 16 + row : 17 + row, :] = sums[:, at : at + 128]

        def mixed_step(m, carry, tile=tile, columns=columns):
            rows = pl.ds(pl.multiple_of(m * 256, 256), 256)
            add = mm(wide_a[rows, columns], weight[tile % 2], 1, 0)
            if tile == 0:
                total[rows, :] = hidden[rows, :] + vectors[2:3, :] + add
            elif tile < 3:
                total[rows, :] = total[rows, :] + add
            else:
                mixed[pl.ds(2 * m, 2)] = (total[rows, :] + add).astype(BF).reshape(2, 128, 1024)
            return carry

        lax.fori_loop(0, 2, mixed_step, 0)
        load_weight(tile + 2).start()
        pump("mix%d" % tile)
    load(10, qkv_in, wide_a.at[:, pl.ds(0, 3072)]).start()

    load(7, normed_two_in, normed).wait()
    wait_sent(range(0, 4))

    def up_step(p, carry):
        columns = pl.ds(pl.multiple_of(p * 512, 512), 512)
        value = mm(wide_g[:, columns], normed[...], 0, 0)
        for j in range(4):
            low = value[j * 64 : (j + 1) * 64]
            high = value[256 + j * 64 : 256 + (j + 1) * 64]
            place_block(jnp.concatenate([low, high], axis=0), UNIT_UP + j, p % 2, p // 2)
        return carry

    lax.fori_loop(0, 4, up_step, 0)
    pump("up0")
    lax.fori_loop(4, 8, up_step, 0)
    load(11, normed_one_in, normed).start()
    pump("up1")

    for tile in range(4, 8):
        load_weight(tile).wait()
        columns = slice((tile - 4) * 1024, (tile - 3) * 1024)

        def norm_step(m, carry, tile=tile, columns=columns):
            rows = pl.ds(pl.multiple_of(m * 256, 256), 256)
            add = mm(wide_g[rows, columns], weight[tile % 2], 1, 1)
            total[rows, :] = add if tile == 4 else total[rows, :] + add
            return carry

        lax.fori_loop(0, 2, norm_step, 0)
        if tile + 2 < UNITS:
            load_weight(tile + 2).start()
        pump("gn%d" % (tile - 4))

    def norm_back(source_ref, gain, rows):
        h = source_ref[rows, :]
        center = h - jnp.mean(h, axis=1, keepdims=True)
        scale = lax.rsqrt(jnp.mean(center * center, axis=1, keepdims=True) + 1e-05)
        xh = center * scale
        q = total[rows, :]
        e = q * gain
        grad = (
            e - jnp.mean(e, axis=1, keepdims=True) - xh * jnp.mean(e * xh, axis=1, keepdims=True)
        ) * scale
        return (
            grad,
            jnp.sum(q * xh, axis=0, keepdims=True),
            jnp.sum(q, axis=0, keepdims=True),
        )

    def norm_two_step(m, carry):
        rows = pl.ds(pl.multiple_of(m * 32, 32), 32)
        grad, gain_sum, shift_sum = norm_back(hidden, vectors[1:2, :], rows)
        cot = inc[rows, :].astype(F32)
        grad = cot + grad
        hidden[rows, :] = grad
        grad_attn[rows, :] = grad.astype(BF)
        return (
            carry[0] + gain_sum,
            carry[1] + shift_sum,
            carry[2] + jnp.sum(cot, axis=0, keepdims=True),
        )

    none = jnp.zeros((1, 1024), F32)
    gain_sum, shift_sum, down_sum = lax.fori_loop(0, 16, norm_two_step, (none, none, none))
    vec_rows[6:7, :] = gain_sum
    vec_rows[7:8, :] = shift_sum
    vec_rows[8:9, :] = down_sum
    pump("ln2")

    load(8, attended_in, attended).wait()
    wait_sent(range(4, 5))

    def out_step(m, carry):
        rows = pl.ds(pl.multiple_of(m * 512, 512), 512)
        value = mm(grad_attn[:, rows], attended[...], 0, 0)
        for q in range(4):
            place_block(value[q * 128 : (q + 1) * 128], UNIT_OUT, q % 2, 2 * m + q // 2)
        return carry

    lax.fori_loop(0, 2, out_step, 0)
    pump("out")
    load_weight(8).wait()

    def mixed_back(m, carry):
        rows = pl.ds(pl.multiple_of(m * 256, 256), 256)
        grad_mixed[rows, :] = mm(grad_attn[rows, :], weight[0], 1, 1).astype(BF)
        return carry

    lax.fori_loop(0, 2, mixed_back, 0)
    load_weight(10).start()

    load(10, qkv_in, wide_a.at[:, pl.ds(0, 3072)]).wait()

    def heads(seq, pair):
        rows = pl.ds(pl.multiple_of(seq * 128, 128), 128)

        def lanes(base):
            return pl.ds(pl.multiple_of(base + pair * 128, 128), 128)

        first = lax.broadcasted_iota(jnp.int32, (128, 128), 1) < 64
        zero = jnp.zeros((128, 128), BF)

        def split(value):
            return jnp.concatenate(
                [jnp.where(first, value, zero), jnp.where(first, zero, value)], axis=0
            )

        q = wide_a[rows, lanes(0)]
        k_two = split(wide_a[rows, lanes(1024)])
        v_two = split(wide_a[rows, lanes(2048)])
        grad_out = grad_mixed[rows, lanes(0)]
        scores = mm(q, k_two, 1, 1) * 0.125
        grad_probs = mm(grad_out, v_two, 1, 1)
        probs, grad_scores = [], []
        for half in range(2):
            s = scores[:, half * 128 : (half + 1) * 128]
            dp = grad_probs[:, half * 128 : (half + 1) * 128]
            e = jnp.exp(s - jnp.max(s, axis=1, keepdims=True))
            soft = e / jnp.sum(e, axis=1, keepdims=True)
            inner = jnp.sum(soft * dp, axis=1, keepdims=True)
            probs.append(soft.astype(BF))
            grad_scores.append((soft * (dp - inner)).astype(BF))
        probs = jnp.concatenate(probs, axis=1)
        grad_scores = jnp.concatenate(grad_scores, axis=1)
        grad_q = mm(grad_scores, k_two, 1, 0) * 0.125
        grad_k = mm(grad_scores, q, 0, 0) * 0.125
        grad_v = mm(probs, grad_out, 0, 0)
        grad_k = jnp.where(first, grad_k[:128], grad_k[128:])
        grad_v = jnp.where(first, grad_v[:128], grad_v[128:])

        def unturn(value):
            return value * cosine[...] - rotated_partner(value) * sine[...]

        wide_g[rows, lanes(0)] = unturn(grad_q).astype(BF)
        wide_g[rows, lanes(1024)] = unturn(grad_k).astype(BF)
        wide_g[rows, lanes(2048)] = grad_v.astype(BF)

    def heads_step(index, carry):
        heads(index // 8, index % 8)
        return carry

    for part in range(4):
        lax.fori_loop(8 * part, 8 * part + 8, heads_step, 0)
        pump("attn%d" % part)

    load(11, normed_one_in, normed).wait()
    wait_sent(range(5, 8))

    def qkv_step(p, carry):
        columns = pl.ds(pl.multiple_of(p * 384, 128), 384)
        value = mm(wide_g[:, columns], normed[...], 0, 0)
        for j in range(3):
            low = value[j * 64 : (j + 1) * 64]
            high = value[192 + j * 64 : 192 + (j + 1) * 64]
            place_block(jnp.concatenate([low, high], axis=0), UNIT_QKV + j, p % 2, p // 2)
        return carry

    lax.fori_loop(0, 8, qkv_step, 0)
    pump("qkv")

    for tile in range(9, 12):
        load_weight(tile).wait()
        columns = slice((tile - 9) * 1024, (tile - 8) * 1024)

        def first_step(m, carry, tile=tile, columns=columns):
            rows = pl.ds(pl.multiple_of(m * 256, 256), 256)
            add = mm(wide_g[rows, columns], weight[tile % 2], 1, 1)
            total[rows, :] = add if tile == 9 else total[rows, :] + add
            return carry

        lax.fori_loop(0, 2, first_step, 0)
        if tile == 9:
            load_weight(11).start()
    load(9, hidden_zero_in, hidden_z).wait()
    gain_sum, shift_sum = none, none
    for seq in range(4):

        def norm_one_step(m, carry, seq=seq):
            rows = pl.ds(pl.multiple_of(seq * 128 + m * 32, 32), 32)
            grad, gain_add, shift_add = norm_back(hidden_z, vectors[0:1, :], rows)
            grad = grad + hidden[rows, :]
            inc[rows, :] = grad.astype(BF)
            return (
                carry[0] + gain_add,
                carry[1] + shift_add,
                carry[2] + jnp.sum(grad, axis=0, keepdims=True),
            )

        gain_sum, shift_sum, embed_sum = lax.fori_loop(
            0, 4, norm_one_step, (gain_sum, shift_sum, none)
        )
        vec_rows[seq : seq + 1, :] = embed_sum
    vec_rows[4:5, :] = gain_sum
    vec_rows[5:6, :] = shift_sum
    for pair in range(8):
        message[pair, 0:16, :] = vec_rows[:, pair * 128 : (pair + 1) * 128]

    def small_copy(step, other):
        del step
        return remote(
            message.at[other // 4],
            small_recv.at[me],
            small_ssem.at[other],
            small_rsem.at[me],
            (other // 2, other % 2),
        )

    def small_start(step, carry):
        small_copy(step, lax.rem(me + step, devices)).start()
        return carry

    lax.fori_loop(1, devices, small_start, 0)
    small_recv[me] = message[place // 2]

    def mixed_back_copies():
        local = pltpu.make_async_copy(
            mixed.at[:, pl.ds(yy * 64, 64)], mixed_out.at[pl.ds(yy * 4, 4)], load_sem.at[12]
        )
        away = remote(
            mixed.at[:, pl.ds((1 - yy) * 64, 64)],
            mixed_out.at[pl.ds(yy * 4, 4)],
            back_ssem.at[0],
            back_rsem.at[0],
            y_peer,
        )
        return local, away

    def tokens_back_copies(seq):
        local = pltpu.make_async_copy(
            inc.at[pl.ds(seq * 128 + yy * 64, 64)], tokens_out.at[yy * 4 + seq], load_sem.at[13 + seq]
        )
        away = remote(
            inc.at[pl.ds(seq * 128 + (1 - yy) * 64, 64)],
            tokens_out.at[yy * 4 + seq],
            back_ssem.at[1 + seq],
            back_rsem.at[1 + seq],
            y_peer,
        )
        return local, away

    back = [mixed_back_copies()] + [tokens_back_copies(seq) for seq in range(4)]
    for local, away in back:
        local.start()
        away.start()

    pump("end")

    def small_wait(step, carry):
        source = lax.rem(me + step, devices)
        pltpu.make_async_remote_copy(
            src_ref=message.at[0],
            dst_ref=small_recv.at[source],
            send_sem=small_ssem.at[source],
            recv_sem=small_rsem.at[source],
            device_id=(source // 2, source % 2),
            device_id_type=MESH_ID,
        ).wait()
        return carry

    lax.fori_loop(1, devices, small_wait, 0)
    small_out[...] = small_recv[...]
    for local, away in back:
        local.wait()
        away.wait()
    wait_sent(range(8, 12))
    for unit in range(UNITS):
        one_copy(unit).wait_send()
        two_copy(unit).wait_send()
        for step in (1, 2, 3):
            three_copy(unit, step).wait_send()
        gather_copy(unit).wait_send()


def schedule():
    link = 2 / 0.091
    free = {"x": 0.0, "y": 0.0, "z": 0.0}
    order, waiting, now = [], [], 0.0

    def send(axis, mbytes, start):
        free[axis] = max(free[axis], start) + mbytes * link
        return free[axis] + 1.5

    def run(stage, unit):
        nonlocal now
        order.append(("step", stage, unit))
        now += (0.8, 0.5, 0.3, 0.2, 0.0)[stage]
        first, second = ("x", "y") if ORDERS[unit] == "x" else ("y", "x")
        if stage == 0:
            ready = send(first, 0.524, now)
        elif stage == 1:
            ready = send(second, 0.262, now)
        elif stage == 2:
            ready = send("z", 0.262, now)
        elif stage == 3:
            ready = send("y", 0.0655, now)
        else:
            return
        waiting.append((ready, stage + 1, unit))

    def drain(until):
        nonlocal now
        while waiting:
            waiting.sort()
            ready, stage, unit = waiting[0]
            if ready > max(now, until):
                return
            waiting.pop(0)
            now = max(now, ready)
            run(stage, unit)

    def core(units):
        for unit in units:
            order.append(("step", -1, unit))
            waiting.append((now + 2.5, 0, unit))

    def piece(label, length, units=()):
        nonlocal now
        now += length
        core(units)
        drain(now)
        order.append(("mark", label, 0))

    for part in range(4):
        piece("down%d" % part, 2.0, (UNIT_DOWN + part,))
    for tile in range(4):
        piece("mix%d" % tile, 3.6)
    piece("up0", 3.5)
    piece("up1", 3.5, range(UNIT_UP, UNIT_UP + 4))
    for tile in range(4):
        piece("gn%d" % tile, 1.7)
    piece("ln2", 2.0)
    piece("out", 1.8, (UNIT_OUT,))
    for part in range(4):
        piece("attn%d" % part, 3.0)
    piece("qkv", 6.0, range(UNIT_QKV, UNIT_QKV + 3))
    now += 9.0
    drain(1e9)
    order.append(("mark", "end", 0))
    return order


def backward_call(operands, vectors, cosine, sine):
    vmem = pl.BlockSpec(memory_space=pltpu.VMEM)
    hbm = pl.BlockSpec(memory_space=pl.ANY)
    dma = pltpu.SemaphoreType.DMA
    return pl.pallas_call(
        backward_kernel,
        name="backward",
        out_shape=(
            jax.ShapeDtypeStruct((8, 64, 1024), BF),
            jax.ShapeDtypeStruct((8, 64, 1024), BF),
            jax.ShapeDtypeStruct((UNITS, 2, 64, 512), BF),
            jax.ShapeDtypeStruct((32, 24, 128), F32),
        ),
        in_specs=[hbm] * 13 + [vmem] * 3,
        out_specs=(hbm, hbm, vmem, vmem),
        scratch_shapes=[
            pltpu.VMEM((2 * UNITS, 2, 4, 64, 512), BF),
            pltpu.VMEM((4, 2, 2, 4, 64, 512), BF),
            pltpu.VMEM((4, 2, 2, 4, 64, 512), BF),
            pltpu.VMEM((UNITS, 2, 4, 64, 512), BF),
            pltpu.VMEM((UNITS, 4, 64, 512), BF),
            pltpu.VMEM((UNITS, 3, 64, 512), BF),
            pltpu.VMEM((2, 1024, 1024), BF),
            pltpu.VMEM((512, 4096), BF),
            pltpu.VMEM((512, 4096), BF),
            pltpu.VMEM((512, 1024), BF),
            pltpu.VMEM((512, 1024), BF),
            pltpu.VMEM((512, 1024), F32),
            pltpu.VMEM((512, 1024), F32),
            pltpu.VMEM((512, 1024), F32),
            pltpu.VMEM((512, 1024), BF),
            pltpu.VMEM((512, 1024), BF),
            pltpu.VMEM((512, 1024), BF),
            pltpu.VMEM((4, 128, 1024), BF),
            pltpu.VMEM((8, 24, 128), F32),
            pltpu.VMEM((32, 24, 128), F32),
            pltpu.VMEM((16, 1024), F32),
            dma((17,)),
            dma((2,)),
            dma((4,)),
            dma((4,)),
            pltpu.SemaphoreType.REGULAR((4,)),
            dma((UNITS,)),
            dma((UNITS,)),
            dma((UNITS,)),
            dma((UNITS,)),
            dma((3 * UNITS,)),
            dma((3 * UNITS,)),
            dma((UNITS,)),
            dma((UNITS,)),
            dma((32,)),
            dma((32,)),
            dma((5,)),
            dma((5,)),
        ],
        compiler_params=pltpu.CompilerParams(
            collective_id=1, has_side_effects=True, vmem_limit_bytes=VMEM_LIMIT
        ),
    )(*operands, vectors, cosine, sine)


def body(
    tokens,
    noise_times,
    time_proj,
    time_bias,
    gain_one,
    shift_one,
    w_qkv,
    w_out,
    gain_two,
    shift_two,
    w_up,
    b_up,
    w_down,
    b_down,
    cotangent,
):
    seq_ways, tok_ways = lax.axis_size("seq"), lax.axis_size("tok")
    model_width = tokens.shape[-1]
    seq_count, length = tokens.shape[0] // tok_ways, tokens.shape[1] * tok_ways
    row_count = seq_count * length
    all_times = lax.all_gather(noise_times, "seq", tiled=True)
    own_times = lax.dynamic_slice_in_dim(
        noise_times, lax.axis_index("tok") * seq_count, seq_count
    )
    embed_table = noise_table(own_times).astype(jnp.bfloat16)
    time_embed = product(embed_table, time_proj) + time_bias.astype(jnp.float32)
    tokens = gather_sequences(tokens)
    incoming = gather_sequences(cotangent).reshape(row_count, model_width)
    hidden_zero = (tokens.astype(jnp.float32) + time_embed[:, None, :]).reshape(
        row_count, model_width
    )
    normed_one, pull_one = jax.vjp(
        layer_norm, hidden_zero, gain_one.astype(jnp.float32), shift_one.astype(jnp.float32)
    )
    normed_one = normed_one.astype(jnp.bfloat16)
    projected = product(normed_one, w_qkv).astype(jnp.bfloat16)
    received, attended, log_total = attend_items(
        projected.reshape(seq_count, length, 3, 1, model_width)
    )
    attended = attended.reshape(row_count, model_width)
    hidden_one = hidden_zero + product(attended, w_out)
    normed_two, pull_two = jax.vjp(
        layer_norm, hidden_one, gain_two.astype(jnp.float32), shift_two.astype(jnp.float32)
    )
    normed_two = normed_two.astype(jnp.bfloat16)
    upward = product(normed_two, w_up) + b_up.astype(jnp.float32)
    active, pull_gelu = jax.vjp(jax.nn.gelu, upward)
    active = active.astype(jnp.bfloat16)
    out_wdown = scatter_sum(contract_rows(incoming, active))
    result = hidden_one + (product(active, w_down) + b_down.astype(jnp.float32))
    mixed_out = return_positions(
        result.astype(jnp.bfloat16).reshape(seq_count, length, model_width)
    )
    sum_down = jnp.sum(incoming, axis=0, dtype=jnp.float32)
    grad_active = times_transpose(incoming, w_down)
    (grad_upward,) = pull_gelu(grad_active)
    grad_upward = grad_upward.astype(jnp.bfloat16)
    sum_up = jnp.sum(grad_upward, axis=0, dtype=jnp.float32)
    out_wup = scatter_sum(contract_rows(grad_upward, normed_two))
    grad_norm_two = times_transpose(grad_upward, w_up)
    grad_hidden_two, grad_gain_two, grad_shift_two = pull_two(grad_norm_two)
    grad_hidden_one = incoming.astype(jnp.float32) + grad_hidden_two
    grad_attn = grad_hidden_one.astype(jnp.bfloat16)
    out_wout = scatter_sum(contract_rows(grad_attn, attended))
    grad_mixed = times_transpose(grad_attn, w_out).astype(jnp.bfloat16)
    grad_parts = attention_grad(
        received, log_total, grad_mixed.reshape(seq_count, length, 1, model_width)
    ).reshape(row_count, 3 * model_width)
    out_wqkv = scatter_sum(contract_rows(grad_parts, normed_one))
    grad_norm_one = times_transpose(grad_parts, w_qkv)
    grad_hidden_zero, grad_gain_one, grad_shift_one = pull_one(grad_norm_one)
    grad_total = grad_hidden_one + grad_hidden_zero
    grad_tokens = return_positions(
        grad_total.astype(jnp.bfloat16).reshape(seq_count, length, model_width)
    )
    grad_embed = jnp.sum(grad_total.reshape(seq_count, length, model_width), axis=1)
    wide = sum_up.shape[0] // model_width
    small = jnp.concatenate(
        [
            grad_embed.reshape(seq_count, seq_ways, -1).swapaxes(0, 1),
            grad_gain_one.reshape(seq_ways, 1, -1),
            grad_shift_one.reshape(seq_ways, 1, -1),
            grad_gain_two.reshape(seq_ways, 1, -1),
            grad_shift_two.reshape(seq_ways, 1, -1),
            sum_down.reshape(seq_ways, 1, -1),
            sum_up.reshape(seq_ways, wide, -1),
        ],
        axis=1,
    )
    small = lax.all_to_all(small, "seq", split_axis=0, concat_axis=0, tiled=True)
    small = lax.all_gather(small, "tok", axis=1)
    embeds = small[:, :, :seq_count].reshape(-1, small.shape[-1])
    out_proj = jnp.dot(
        noise_table(all_times).astype(jnp.bfloat16).astype(jnp.float32).T,
        embeds,
        precision=lax.Precision.HIGHEST,
    )
    out_bias = jnp.sum(embeds, axis=0)
    sums = jnp.sum(small[:, :, seq_count:], axis=(0, 1))
    return (
        mixed_out,
        grad_tokens,
        out_proj,
        out_bias,
        sums[0],
        sums[1],
        out_wqkv,
        out_wout,
        sums[2],
        sums[3],
        out_wup,
        sums[5:].reshape(-1),
        out_wdown,
        sums[4],
    )


def rotary_lanes():
    cosine, sine = rotary_tables(128)
    cosine = jnp.tile(cosine[:, 0], (1, 2))
    sine = jnp.tile(sine[:, 0], (1, 2))
    sign = jnp.where(jnp.arange(128) % 64 < 32, -1.0, 1.0)
    return cosine, sine * sign


def fast_body(
    tokens,
    noise_times,
    time_proj,
    time_bias,
    gain_one,
    shift_one,
    w_qkv,
    w_out,
    gain_two,
    shift_two,
    w_up,
    b_up,
    w_down,
    b_down,
    cotangent,
):
    tok_ways = lax.axis_size("tok")
    model_width = tokens.shape[-1]
    seq_count, length = tokens.shape[0] // tok_ways, tokens.shape[1] * tok_ways
    row_count = seq_count * length
    all_times = lax.all_gather(noise_times, "seq", tiled=True)
    own_times = lax.dynamic_slice_in_dim(
        noise_times, lax.axis_index("tok") * seq_count, seq_count
    )
    embed_table = noise_table(own_times).astype(jnp.bfloat16)
    time_embed = product(embed_table, time_proj) + time_bias.astype(jnp.float32)
    tokens = gather_sequences(tokens)
    incoming = gather_sequences(cotangent).reshape(row_count, model_width)
    hidden_zero = (tokens.astype(jnp.float32) + time_embed[:, None, :]).reshape(
        row_count, model_width
    )
    normed_one = layer_norm(
        hidden_zero, gain_one.astype(jnp.float32), shift_one.astype(jnp.float32)
    ).astype(jnp.bfloat16)
    projected = product(normed_one, w_qkv).astype(jnp.bfloat16)
    projected = projected.reshape(seq_count, length, 3, 1, model_width)
    queries, keys_rot, values, _, _ = split_heads(projected)
    _, attended, _ = attend_items(projected)
    attended = attended.reshape(row_count, model_width)
    qkv = jnp.concatenate(
        [part.reshape(row_count, model_width) for part in (queries, keys_rot, values)], axis=1
    )
    hidden_one = hidden_zero + product(attended, w_out)
    normed_two = layer_norm(
        hidden_one, gain_two.astype(jnp.float32), shift_two.astype(jnp.float32)
    ).astype(jnp.bfloat16)
    upward = product(normed_two, w_up) + b_up.astype(jnp.float32)
    factor = math.sqrt(2.0 / math.pi)
    bend = jnp.tanh(factor * (upward + 0.044715 * upward**3))
    active = (0.5 * upward * (1.0 + bend)).astype(jnp.bfloat16)
    slope = 0.5 * (1.0 + bend) + 0.5 * upward * (1.0 - bend * bend) * factor * (
        1.0 + 3.0 * 0.044715 * upward * upward
    )
    slope = slope.astype(jnp.bfloat16)
    vectors = jnp.concatenate(
        [
            gain_one[None, :],
            gain_two[None, :],
            b_down[None, :],
            jnp.zeros((5, model_width), jnp.bfloat16),
        ]
    ).astype(jnp.float32)
    cosine, sine = rotary_lanes()
    mixed_out, grad_tokens, shares, small = backward_call(
        (
            incoming,
            active,
            slope,
            normed_two,
            hidden_one,
            attended,
            qkv,
            normed_one,
            hidden_zero,
            w_down,
            w_up,
            w_out,
            w_qkv,
        ),
        vectors,
        cosine,
        sine,
    )
    core = lax.axis_index("seq") % 2
    shares = jnp.swapaxes(shares, 1, 2).reshape(UNITS, 64, model_width)
    out_wdown = jnp.swapaxes(shares[0:4], 1, 2).reshape(4 * model_width, 64)
    out_wup = shares[4:8].reshape(256, model_width).T
    out_wout = shares[8].T
    out_wqkv = shares[9:12].reshape(192, model_width).T
    wide = small[:, 16:20]
    small = lax.dynamic_slice_in_dim(small[:, :9], core * 64, 64, axis=2)
    embeds = small[:, :4].reshape(-1, 64)
    sums = jnp.sum(small[:, 4:], axis=0)
    out_proj = jnp.dot(
        noise_table(all_times).astype(jnp.bfloat16).astype(jnp.float32).T,
        embeds,
        precision=lax.Precision.HIGHEST,
    )
    out_bias = jnp.sum(embeds, axis=0)
    out_bup = lax.dynamic_slice_in_dim(jnp.sum(wide, axis=0), core * 2, 2, axis=0).reshape(-1)
    return (
        mixed_out,
        grad_tokens,
        out_proj,
        out_bias,
        sums[0],
        sums[1],
        out_wqkv.astype(jnp.float32),
        out_wout.astype(jnp.float32),
        sums[2],
        sums[3],
        out_wup.astype(jnp.float32),
        out_bup,
        out_wdown.astype(jnp.float32),
        sums[4],
    )


def solution(mesh):
    chosen = fast_body if (mesh.shape["seq"], mesh.shape["tok"]) == (16, 2) else body
    in_specs = (
        P("seq", "tok", None),
        P("seq"),
        P(),
        P(),
        P(),
        P(),
        P(),
        P(),
        P(),
        P(),
        P(),
        P(),
        P(),
        P(),
        P("seq", "tok", None),
    )
    out_specs = (
        P("seq", "tok", None),
        P("seq", "tok", None),
        P(None, "seq"),
        P("seq"),
        P("seq"),
        P("seq"),
        P(None, "seq"),
        P(None, "seq"),
        P("seq"),
        P("seq"),
        P(None, "seq"),
        P("seq"),
        P(None, "seq"),
        P("seq"),
    )
    return jax.shard_map(chosen, mesh=mesh, in_specs=in_specs, out_specs=out_specs, check_vma=False)
```

```python
import math

import jax
import jax.numpy as jnp
import numpy as np
from jax import lax
from jax.experimental import pallas as pl
from jax.experimental.pallas import tpu as pltpu
from jax.sharding import PartitionSpec as P

HD = 64
TEMB = 256
VMEM_LIMIT = 64 * 1024 * 1024 - 65536


def layer_norm(hidden, gain_vec, shift_vec):
    center = hidden - jnp.mean(hidden, axis=-1, keepdims=True)
    spread = jnp.mean(center * center, axis=-1, keepdims=True)
    return center * lax.rsqrt(spread + 1e-05) * gain_vec + shift_vec


def noise_table(noise_steps):
    halves = TEMB // 2
    frequency = jnp.exp(-math.log(10000.0) * jnp.arange(halves, dtype=jnp.float32) / halves)
    angles = noise_steps.astype(jnp.float32)[:, None] * frequency[None, :]
    return jnp.concatenate([jnp.sin(angles), jnp.cos(angles)], axis=-1)


def rotary_tables(length):
    halves = HD // 2
    frequency = jnp.exp(-math.log(10000.0) * jnp.arange(halves, dtype=jnp.float32) / halves)
    angles = jnp.arange(length, dtype=jnp.float32)[:, None] * frequency[None, :]
    angles = jnp.concatenate([angles, angles], axis=-1)[:, None, :]
    return (jnp.cos(angles), jnp.sin(angles))


def rotate(values, cosine, sine_tab):
    halves = values.shape[-1] // 2
    turned = jnp.concatenate([-values[..., halves:], values[..., :halves]], axis=-1)
    return values * cosine + turned * sine_tab


def unrotate(gradient, cosine, sine_tab):
    halves = gradient.shape[-1] // 2
    scaled = gradient * sine_tab
    turned = jnp.concatenate([scaled[..., halves:], -scaled[..., :halves]], axis=-1)
    return gradient * cosine + turned


def product(left_side, right_side):
    return jnp.dot(left_side, right_side, preferred_element_type=jnp.float32)


def contract_rows(left_side, right_side):
    return jnp.einsum("ra,rb->ab", left_side, right_side, preferred_element_type=jnp.float32)


def times_transpose(left_side, right_side):
    return jnp.einsum("rb,ab->ra", left_side, right_side, preferred_element_type=jnp.float32)


def split_heads(received):
    batch_size, length = (received.shape[0], received.shape[1])
    local_heads = received.shape[-1] // HD
    split_view = received.reshape(batch_size, length, 3, local_heads, HD)
    cosine, sine_tab = rotary_tables(length)
    queries = rotate(split_view[:, :, 0].astype(jnp.float32), cosine, sine_tab).astype(jnp.bfloat16)
    keys_rot = rotate(split_view[:, :, 1].astype(jnp.float32), cosine, sine_tab).astype(
        jnp.bfloat16
    )
    return (queries, keys_rot, split_view[:, :, 2], cosine, sine_tab)


def attend_items(received):
    batch_size, length = (received.shape[0], received.shape[1])
    scaling = 1.0 / math.sqrt(HD)
    queries, keys_rot, values, cosine, sine_tab = split_heads(received)
    scores = (
        jnp.einsum("gqhd,gkhd->ghqk", queries, keys_rot, preferred_element_type=jnp.float32)
        * scaling
    )
    highest = jnp.max(scores, axis=-1, keepdims=True)
    exponent = jnp.exp(scores - highest)
    totals = jnp.sum(exponent, axis=-1, keepdims=True)
    prob_rows = (exponent / totals).astype(jnp.bfloat16)
    log_total = (highest + jnp.log(totals))[..., 0]
    attended = jnp.einsum("ghqk,gkhd->gqhd", prob_rows, values, preferred_element_type=jnp.float32)
    attended = attended.astype(jnp.bfloat16).reshape(batch_size, length, 1, -1)
    return (received, attended, log_total)


def attention_grad(received, log_total, grad_heads):
    batch_size, length = (received.shape[0], received.shape[1])
    scaling = 1.0 / math.sqrt(HD)
    queries, keys_rot, values, cosine, sine_tab = split_heads(received)
    scores = (
        jnp.einsum("gqhd,gkhd->ghqk", queries, keys_rot, preferred_element_type=jnp.float32)
        * scaling
    )
    prob_rows = jnp.exp(scores - log_total[..., None])
    grad_out = grad_heads.reshape(batch_size, length, values.shape[2], HD)
    grad_probs = jnp.einsum("gqhd,gkhd->ghqk", grad_out, values, preferred_element_type=jnp.float32)
    grad_values = jnp.einsum(
        "ghqk,gqhd->gkhd",
        prob_rows.astype(jnp.bfloat16),
        grad_out,
        preferred_element_type=jnp.float32,
    )
    inner_sum = jnp.sum(prob_rows * grad_probs, axis=-1, keepdims=True)
    grad_scores = (prob_rows * (grad_probs - inner_sum)).astype(jnp.bfloat16)
    grad_queries = (
        jnp.einsum("ghqk,gkhd->gqhd", grad_scores, keys_rot, preferred_element_type=jnp.float32)
        * scaling
    )
    grad_keys = (
        jnp.einsum("ghqk,gqhd->gkhd", grad_scores, queries, preferred_element_type=jnp.float32)
        * scaling
    )
    stacked = jnp.stack(
        [
            unrotate(grad_queries, cosine, sine_tab),
            unrotate(grad_keys, cosine, sine_tab),
            grad_values,
        ],
        axis=2,
    )
    return stacked.astype(jnp.bfloat16).reshape(batch_size, length, 3, 1, -1)


def gather_sequences(values):
    return lax.all_to_all(values, "tok", split_axis=0, concat_axis=1, tiled=True)


def return_positions(values):
    return lax.all_to_all(values, "tok", split_axis=1, concat_axis=0, tiled=True)


def group_scatter(parts, own, size, axis, perm_of):
    total = lax.dynamic_index_in_dim(parts, own, 0, keepdims=False).astype(jnp.float32)
    for shift in range(1, size):
        piece = lax.dynamic_index_in_dim(parts, (own + shift) % size, 0, keepdims=False)
        total = total + lax.ppermute(piece, axis, perm_of(shift)).astype(jnp.float32)
    return total.astype(jnp.bfloat16)


def group_gather(piece, own, size, axis, perm_of):
    held = jnp.zeros((size,) + piece.shape, piece.dtype)
    held = lax.dynamic_update_index_in_dim(held, piece, own, 0)
    for shift in range(1, size):
        other = lax.ppermute(piece, axis, perm_of(shift))
        held = lax.dynamic_update_index_in_dim(held, other, (own - shift) % size, 0)
    return held


def scatter_sum(gradient):
    seq_ways, tok_ways = lax.axis_size("seq"), lax.axis_size("tok")
    outer, middle = 4, seq_ways // 8
    place, turn = lax.axis_index("seq"), lax.axis_index("tok")
    core, mid, out = place % 2, (place // 2) % middle, place // (2 * middle)

    def core_perm(shift):
        return [(i, i ^ 1) for i in range(seq_ways)]

    def mid_perm(shift):
        return [
            (i, (i // (2 * middle)) * 2 * middle + ((i // 2 + shift) % middle) * 2 + i % 2)
            for i in range(seq_ways)
        ]

    def out_perm(shift):
        return [(i, (i + shift * 2 * middle) % seq_ways) for i in range(seq_ways)]

    def tok_perm(shift):
        return [(i, (i + shift) % tok_ways) for i in range(tok_ways)]

    rows, width = gradient.shape[0] // seq_ways, gradient.shape[1]
    parts = gradient.astype(jnp.bfloat16).reshape(outer * middle, 2, rows, width)
    parts = group_scatter(jnp.swapaxes(parts, 0, 1), core, 2, "seq", core_perm)
    parts = parts.reshape(outer, middle, rows, 2, tok_ways, width // (2 * tok_ways))
    first = jnp.transpose(parts[:, :, :, 0], (1, 3, 0, 2, 4))
    second = jnp.transpose(parts[:, :, :, 1], (3, 1, 0, 2, 4))
    first = group_scatter(first, mid, middle, "seq", mid_perm)
    second = group_scatter(second, turn, tok_ways, "tok", tok_perm)
    first = group_scatter(first, turn, tok_ways, "tok", tok_perm)
    second = group_scatter(second, mid, middle, "seq", mid_perm)
    both = jnp.stack([first, second], axis=1)
    both = group_scatter(both, out, outer, "seq", out_perm)
    both = group_gather(both, turn, tok_ways, "tok", tok_perm)
    return jnp.transpose(both, (2, 1, 0, 3)).reshape(rows, width).T.astype(jnp.float32)


MESH_ID = pl.DeviceIdType.MESH
BF = jnp.bfloat16
F32 = jnp.float32
UNITS = 12
UNIT_DOWN, UNIT_UP, UNIT_OUT, UNIT_QKV = 0, 4, 8, 9
ORDERS = "xyxyxzzyxzxzyzyxyxyyxxzz"
GELU_A = math.sqrt(2.0 / math.pi)
GELU_B = 0.044715


def mm(left, right, left_dim, right_dim):
    return lax.dot_general(
        left, right, (((left_dim,), (right_dim,)), ((), ())), preferred_element_type=F32
    )


def rotated_partner(values):
    lane = lax.broadcasted_iota(jnp.int32, values.shape, 1)
    return jnp.where(lane % 64 < 32, pltpu.roll(values, 96, 1), pltpu.roll(values, 32, 1))


def lane_index(rows):
    return lax.broadcasted_iota(jnp.int32, (rows, 128), 1)


def two_heads(value):
    first = lane_index(128) < 64
    zero = jnp.zeros_like(value)
    return jnp.concatenate([jnp.where(first, value, zero), jnp.where(first, zero, value)], axis=0)


def head_mask(count):
    lane = lane_index(256)
    row = lax.broadcasted_iota(jnp.int32, (256, 128), 0)
    return jnp.where((lane // 64 == row // 128) & (lane % 64 < count), 1.0, 0.0)


def in_terms(value):
    lane = lane_index(value.shape[0]) % 64
    out, rest = jnp.zeros(value.shape, BF), value
    for index in range(3):
        term = rest.astype(BF)
        rest = rest - term.astype(F32)
        out = jnp.where(lane == index, term, out)
    return out


def layer_kernel(
    tokens_in,
    cotangent_in,
    w_qkv,
    w_out,
    w_up,
    w_down,
    time_proj,
    time_bias,
    gain_one,
    shift_one,
    gain_two,
    shift_two,
    b_up,
    b_down,
    cosine,
    sine,
    noise_times,
    mixed_out,
    tokens_out,
    shares_out,
    small_out,
    normed_one_out,
    partial,
    core_recv,
    recv_one,
    recv_two,
    recv_three,
    weight,
    wide_a,
    wide_g,
    qkv,
    tokens,
    inc,
    normed,
    hidden,
    total,
    grad_attn,
    attended,
    mixed,
    message,
    small_recv,
    vec_rows,
    embeds,
    tables,
    time_embed,
    load_sem,
    weight_sem,
    token_ssem,
    token_rsem,
    cot_ssem,
    cot_rsem,
    core_ssem,
    core_rsem,
    credit,
    one_ssem,
    one_rsem,
    two_ssem,
    two_rsem,
    three_ssem,
    three_rsem,
    gather_ssem,
    gather_rsem,
    small_ssem,
    small_rsem,
    back_ssem,
    back_rsem,
):
    place, turn = lax.axis_index("seq"), lax.axis_index("tok")
    core, xx, zz = place % 2, (place // 2) % 2, place // 4
    yy = turn
    me = place * 2 + turn
    devices = 32

    def at_seq(z, x, c):
        return ((z * 2 + x) * 2 + c, turn)

    core_peer = at_seq(zz, xx, 1 - core)
    x_peer = at_seq(zz, 1 - xx, core)
    y_peer = (place, 1 - turn)

    def load(index, source, target):
        return pltpu.make_async_copy(source, target, load_sem.at[index])

    def load_weight(tile):
        if tile == 0 or tile == 13:
            source = w_out
        elif tile < 5:
            source = w_up.at[:, pl.ds((tile - 1) * 1024, 1024)]
        elif tile < 9:
            source = w_down.at[pl.ds((tile - 5) * 1024, 1024), :]
        elif tile < 13:
            source = w_up.at[:, pl.ds((tile - 9) * 1024, 1024)]
        else:
            source = w_qkv.at[:, pl.ds((tile - 14) * 1024, 1024)]
        return pltpu.make_async_copy(source, weight.at[tile % 2], weight_sem.at[tile % 2])

    def row_of(vector):
        return vector[...].astype(F32).reshape(1, vector.shape[0])

    own_half = pl.ds(turn * 64, 64)

    def load_qkv(part):
        index, half = part // 2, part % 2
        columns = pl.ds(index * 1024, 1024)
        target = (wide_a, wide_g)[half]
        return load(
            1 + part, w_qkv.at[pl.ds(half * 512, 512), columns], target.at[:, columns]
        )

    def load_cot(seq):
        return load(
            8 + seq,
            cotangent_in.at[turn * 4 + seq],
            inc.at[pl.ds(seq * 128 + turn * 64, 64)],
        )

    load_tokens = load(0, tokens_in.at[pl.ds(turn * 4, 4)], tokens.at[:, own_half])
    load_tokens.start()
    for part in range(6):
        load_qkv(part).start()
    load_weight(0).start()
    load_weight(1).start()
    for seq in range(4):
        load_cot(seq).start()

    barrier = pltpu.get_barrier_semaphore()

    def greet(step, carry):
        other = lax.rem(me + step, devices)
        pl.semaphore_signal(
            barrier, inc=1, device_id=(other // 2, other % 2), device_id_type=MESH_ID
        )
        return carry

    lax.fori_loop(1, devices, greet, 0)
    pl.semaphore_wait(barrier, devices - 1)

    def remote(source, target, send, recv, device):
        return pltpu.make_async_remote_copy(
            src_ref=source,
            dst_ref=target,
            send_sem=send,
            recv_sem=recv,
            device_id=device,
            device_id_type=MESH_ID,
        )

    parity, high = zz % 2, zz // 2

    def core_copy(unit):
        slot = unit % 4
        return remote(
            partial.at[pl.ds(2 * UNITS + 2 * slot, 2)],
            core_recv.at[slot],
            core_ssem.at[slot],
            core_rsem.at[slot],
            core_peer,
        )

    def half_of(chain):
        return chain // 2, pl.ds(32 * (chain % 2), 32)

    def one_copy(chain):
        unit, rows = half_of(chain)
        if ORDERS[chain] == "x":
            source, device = partial.at[2 * unit + 1 - xx, :, :, :, rows], x_peer
        elif ORDERS[chain] == "y":
            source, device = partial.at[pl.ds(2 * unit, 2), 1 - yy, :, :, rows], y_peer
        else:
            source = partial.at[pl.ds(2 * unit, 2), :, 1 - parity, :, rows]
            device = at_seq(2 * high + 1 - parity, xx, core)
        target = recv_one.at[unit, :, :, :, rows]
        return remote(source, target, one_ssem.at[chain], one_rsem.at[chain], device)

    def two_copy(chain):
        unit, rows = half_of(chain)
        if ORDERS[chain] == "x":
            source, device = partial.at[2 * unit + xx, 1 - yy, :, :, rows], y_peer
        elif ORDERS[chain] == "y":
            source, device = partial.at[2 * unit + 1 - xx, yy, :, :, rows], x_peer
        else:
            source = partial.at[pl.ds(2 * unit, 2), :, parity, 1 - high, rows]
            device = at_seq(2 * (1 - high) + parity, xx, core)
        target = recv_two.at[unit, :, :, rows]
        return remote(source, target, two_ssem.at[chain], two_rsem.at[chain], device)

    def three_copy(chain, step):
        unit, rows = half_of(chain)
        index = 3 * chain + step - 1
        if ORDERS[chain] != "z":
            other = (zz + step) % 4
            source = partial.at[2 * unit + xx, yy, other % 2, other // 2, rows]
            target, device = recv_three.at[unit, step - 1, rows], at_seq(other, xx, core)
        elif step == 1:
            source = partial.at[2 * unit + 1 - xx, :, parity, high, rows]
            target, device = recv_three.at[unit, pl.ds(0, 2), rows], x_peer
        else:
            source = partial.at[2 * unit + xx, 1 - yy, parity, high, rows]
            target, device = recv_three.at[unit, 2, rows], y_peer
        return remote(source, target, three_ssem.at[index], three_rsem.at[index], device)

    def gather_copy(chain):
        unit, rows = half_of(chain)
        view = shares_out.at[unit, yy, rows]
        return remote(view, view, gather_ssem.at[chain], gather_rsem.at[chain], y_peer)

    def start_core(unit):
        if unit >= 4:
            pl.semaphore_wait(credit.at[unit % 4], 1)
        core_copy(unit).start()

    def add_core(unit):
        core_copy(unit).wait_recv()

        def add(index, carry):
            x, h, p = index // 4, (index // 2) % 2, index % 2
            partial[2 * unit + x, h, p] = (
                partial[2 * unit + x, h, p] + core_recv[unit % 4, x, h, p]
            )
            return carry

        lax.fori_loop(0, 8, add, 0)
        if unit < UNITS - 4:
            pl.semaphore_signal(
                credit.at[unit % 4], inc=1, device_id=core_peer, device_id_type=MESH_ID
            )

    def add_one(chain):
        one_copy(chain).wait_recv()
        unit, rows = half_of(chain)
        for a in range(2):
            for b in range(2):
                for c in range(2):
                    if ORDERS[chain] == "x":
                        at = (2 * unit + xx, a, b, c, rows)
                    elif ORDERS[chain] == "y":
                        at = (2 * unit + a, yy, b, c, rows)
                    else:
                        at = (2 * unit + a, b, parity, c, rows)
                    partial[at] = partial[at] + recv_one[unit, a, b, c, rows]

    def add_two(chain):
        two_copy(chain).wait_recv()
        unit, rows = half_of(chain)
        for a in range(2):
            for b in range(2):
                if ORDERS[chain] == "z":
                    at = (2 * unit + a, b, parity, high, rows)
                else:
                    at = (2 * unit + xx, yy, a, b, rows)
                partial[at] = partial[at] + recv_two[unit, a, b, rows]

    def add_three(chain):
        unit, rows = half_of(chain)
        value = partial[2 * unit + xx, yy, parity, high, rows].astype(F32)
        for step in (1, 2, 3):
            three_copy(chain, step).wait_recv()
        for step in (1, 2, 3):
            value = value + recv_three[unit, step - 1, rows].astype(F32)
        shares_out[unit, yy, rows] = value.astype(BF)

    def add_last_x(chain):
        three_copy(chain, 1).wait_recv()
        unit, rows = half_of(chain)
        for h in range(2):
            at = (2 * unit + xx, h, parity, high, rows)
            partial[at] = partial[at] + recv_three[unit, h, rows]

    def add_last_y(chain):
        three_copy(chain, 2).wait_recv()
        unit, rows = half_of(chain)
        value = partial[2 * unit + xx, yy, parity, high, rows].astype(F32)
        value = value + recv_three[unit, 2, rows].astype(F32)
        shares_out[unit, yy, rows] = value.astype(BF)

    def start_three(chain):
        for step in (2, 1, 3):
            three_copy(chain, step).start()

    actions = {
        "core": (start_core, add_core),
        "one": (lambda unit: one_copy(unit).start(), add_one),
        "two": (lambda unit: two_copy(unit).start(), add_two),
        "three": (start_three, add_three),
        "last_x": (lambda unit: three_copy(unit, 1).start(), add_last_x),
        "last_y": (lambda unit: three_copy(unit, 2).start(), add_last_y),
        "gather": (
            lambda unit: gather_copy(unit).start(),
            lambda unit: gather_copy(unit).wait_recv(),
        ),
    }
    def row_copies(part):
        if part == 0:
            source, target = mixed, mixed_out
            at = pl.ds(yy * 4, 4)
            views = [source.at[:, pl.ds(y * 64, 64)] for y in (yy, 1 - yy)]
        else:
            source, target = inc, tokens_out
            at = yy * 4 + part - 1
            views = [
                source.at[pl.ds((part - 1) * 128 + y * 64, 64)] for y in (yy, 1 - yy)
            ]
        local = pltpu.make_async_copy(views[0], target.at[at], load_sem.at[12 + part])
        away = remote(views[1], target.at[at], back_ssem.at[part], back_rsem.at[part], y_peer)
        return local, away

    def start_rows(part):
        for copy in row_copies(part):
            copy.start()

    plan = schedule(ORDERS)
    cursor = [0]

    def pump(label):
        while True:
            kind, stage, unit = plan[cursor[0]]
            cursor[0] += 1
            if kind == "mark":
                assert stage == label
                return
            if stage == "rows":
                start_rows(unit)
            else:
                actions[stage][0 if kind == "start" else 1](unit)

    def wait_sent(units):
        for unit in units:
            core_copy(unit).wait_send()

    def place_block(low, high_rows, unit, x, p, q):
        own, away = 2 * unit + x, 2 * UNITS + 2 * (unit % 4) + x
        for value, at in (
            (low, own * (1 - core) + away * core),
            (high_rows, away * (1 - core) + own * core),
        ):
            value = value.astype(BF)
            for h in range(2):
                partial[at, h, p, q] = value[:, h * 512 : (h + 1) * 512]

    def send_tokens(batch):
        return remote(
            tokens_in.at[pl.ds((1 - turn) * 4 + 2 * batch, 2)],
            tokens.at[pl.ds(2 * batch, 2), own_half],
            token_ssem.at[batch],
            token_rsem.at[batch],
            y_peer,
        )

    def send_cot(seq):
        return remote(
            cotangent_in.at[(1 - turn) * 4 + seq],
            inc.at[pl.ds(seq * 128 + turn * 64, 64)],
            cot_ssem.at[seq],
            cot_rsem.at[seq],
            y_peer,
        )

    send_tokens(0).start()
    message[...] = jnp.zeros_like(message)
    vec_rows[...] = jnp.zeros_like(vec_rows)
    lane = lax.broadcasted_iota(jnp.int32, (1, 128), 1).astype(F32)
    frequency = jnp.exp((-math.log(10000.0) * lane) / 128)
    steps = [jnp.where(turn == 0, noise_times[j], noise_times[4 + j]) for j in range(4)]
    angles = jnp.concatenate([frequency * step.astype(F32) for step in steps] * 2, axis=0)
    sine_rows = jnp.sin(angles).astype(BF)
    cosine_rows = jnp.cos(angles).astype(BF)
    time_embed[...] = (
        mm(jnp.concatenate([sine_rows, cosine_rows], axis=1), time_proj[...], 1, 0)
        + row_of(time_bias)
    )
    for pair in range(8):
        message[pair, 20:24, :] = sine_rows.astype(F32)[0:4]
        message[pair, 24:28, :] = cosine_rows.astype(F32)[0:4]
    load_tokens.wait()

    def norm(value, gain, shift):
        center = value - jnp.mean(value, axis=1, keepdims=True)
        spread = jnp.mean(center * center, axis=1, keepdims=True)
        return (center * lax.rsqrt(spread + 1e-05) * gain + shift).astype(BF)

    def first_norm(seqs, side):
        starts = [pl.multiple_of(seq * 128 + side * 64, 64) for seq in seqs]
        for seq, start in zip(seqs, starts):

            def step(m, carry, seq=seq, start=start):
                rows = pl.ds(pl.multiple_of(start + m * 32, 32), 32)
                inner = pl.ds(pl.multiple_of(side * 64 + m * 32, 32), 32)
                value = tokens[seq, inner, :].astype(F32) + time_embed[seq : seq + 1, :]
                hidden[rows, :] = value
                grad_attn[rows, :] = norm(value, row_of(gain_one), row_of(shift_one))
                return carry

            lax.fori_loop(0, 2, step, 0)
        rows = jnp.concatenate([grad_attn[pl.ds(start, 64), :] for start in starts], axis=0)
        for part in range(3):
            columns = slice(part * 1024, (part + 1) * 1024)
            if len(seqs) == 4:
                load_qkv(2 * part).wait()
                load_qkv(2 * part + 1).wait()
            value = mm(rows[:, :512], wide_a[:, columns], 1, 0)
            value = (value + mm(rows[:, 512:], wide_g[:, columns], 1, 0)).astype(BF)
            for index, start in enumerate(starts):
                qkv[pl.ds(start, 64), columns] = value[index * 64 : (index + 1) * 64]

    def forward_heads(seq, pair):
        rows = pl.ds(pl.multiple_of(seq * 128, 128), 128)

        def lanes(base):
            return pl.ds(pl.multiple_of(base + pair * 128, 128), 128)

        def turned(value):
            value = value.astype(F32)
            return value * cosine[...] + rotated_partner(value) * sine[...]

        first = lane_index(128) < 64
        q = (turned(qkv[rows, lanes(0)]) * 0.125).astype(BF)
        k = turned(qkv[rows, lanes(1024)]).astype(BF)
        qkv[rows, lanes(0)] = q
        qkv[rows, lanes(1024)] = k
        scores = mm(q, two_heads(k), 1, 1)
        highest, exponent = [], []
        for part in range(2):
            s = scores[:, part * 128 : (part + 1) * 128]
            highest.append(jnp.max(s, axis=1, keepdims=True))
            exponent.append(jnp.exp(s - highest[part]))
        sums = mm(
            jnp.concatenate(exponent, axis=1).astype(BF),
            jnp.concatenate(
                [two_heads(qkv[rows, lanes(2048)]), head_mask(64).astype(BF)], axis=1
            ),
            1,
            0,
        )
        attended[rows, lanes(0)] = (sums[:, :128] / sums[:, 128:]).astype(BF)
        log_total = jnp.where(first, highest[0], highest[1]) + jnp.log(sums[:, 128:])
        qkv[rows, lanes(3072)] = in_terms(log_total)

    first_norm((0, 1, 2, 3), turn)
    for batch in range(2):
        send_tokens(batch).wait_recv()
        if batch == 0:
            send_tokens(1).start()
        else:
            for seq in range(4):
                send_cot(seq).start()
        first_norm((2 * batch, 2 * batch + 1), 1 - turn)

        def forward_step(index, carry, batch=batch):
            for pair in range(4):
                forward_heads(2 * batch + index // 2, (index % 2) * 4 + pair)
            return carry

        lax.fori_loop(0, 4, forward_step, 0)
        if batch == 0:
            load_weight(0).wait()
        rows = slice(batch * 256, (batch + 1) * 256)
        hidden[rows, :] = hidden[rows, :] + mm(attended[rows, :], weight[0], 1, 0)

        def second_step(m, carry, batch=batch):
            rows = pl.ds(pl.multiple_of(batch * 256 + m * 32, 32), 32)
            normed[rows, :] = norm(hidden[rows, :], row_of(gain_two), row_of(shift_two))
            return carry

        lax.fori_loop(0, 8, second_step, 0)
    spill_normed = load(7, grad_attn, normed_one_out)
    spill_normed.start()
    load_weight(2).start()
    pump("start")

    def up_tile(tile):
        columns = slice(tile * 1024, (tile + 1) * 1024)
        bias = row_of(b_up)

        def step(m, carry):
            for half in range(2):
                rows = pl.ds(pl.multiple_of(m * 256 + half * 128, 128), 128)
                u = mm(normed[rows, :], weight[(tile + 1) % 2], 1, 0) + bias[:, columns]
                square = u * u
                bend = jnp.tanh(u * (GELU_A + (GELU_A * GELU_B) * square))
                side = 0.5 * (1.0 + bend)
                wide_a[rows, columns] = (u * side).astype(BF)
                slope = side + (0.5 * u) * (1.0 - bend * bend) * (
                    GELU_A + (3.0 * GELU_A * GELU_B) * square
                )
                wide_g[rows, columns] = slope.astype(BF)
            return carry

        lax.fori_loop(0, 2, step, 0)

    def down_unit(unit):
        def step(m, carry):
            rows = pl.ds(pl.multiple_of(m * 512, 512), 512)
            value = mm(inc[:, rows], wide_a[:, unit * 1024 : (unit + 1) * 1024], 0, 0)
            for q in range(4):
                at = q * 128
                place_block(
                    value[at : at + 64], value[at + 64 : at + 128], unit, q % 2, q // 2, m
                )
            return carry

        lax.fori_loop(0, 2, step, 0)

    for part in range(5):
        if part < 4:
            load_weight(1 + part).wait()
            up_tile(part)
            load_weight(part + 3).start()
            pump("up%d" % part)
        if part == 1:
            for seq in range(4):
                load_cot(seq).wait()
                send_cot(seq).wait_recv()
        if part > 0:
            down_unit(UNIT_DOWN + part - 1)
            pump("down%d" % (part - 1))

    for tile in range(4):
        load_weight(5 + tile).wait()
        columns = slice(tile * 1024, (tile + 1) * 1024)

        for part in range(2):
            at = tile * 1024 + part * 512
            grad = mm(inc[...], weight[(tile + 1) % 2, part * 512 : (part + 1) * 512, :], 1, 1)
            grad = (grad * wide_g[:, at : at + 512].astype(F32)).astype(BF)
            wide_g[:, at : at + 512] = grad
            sums = jnp.sum(grad.astype(F32), axis=0, keepdims=True)
            for row in range(4):
                message[2 * tile + part, 16 + row : 17 + row, :] = sums[
                    :, row * 128 : (row + 1) * 128
                ]
        pump("gu%d" % tile)

        def mixed_step(m, carry, tile=tile, columns=columns):
            rows = pl.ds(pl.multiple_of(m * 256, 256), 256)
            add = mm(wide_a[rows, columns], weight[(tile + 1) % 2], 1, 0)
            if tile == 0:
                total[rows, :] = hidden[rows, :] + row_of(b_down) + add
            elif tile < 3:
                total[rows, :] = total[rows, :] + add
            else:
                mixed[pl.ds(2 * m, 2)] = (total[rows, :] + add).astype(BF).reshape(2, 128, 1024)
            return carry

        lax.fori_loop(0, 2, mixed_step, 0)
        load_weight(tile + 7).start()
        pump("mx%d" % tile)

    wait_sent(range(0, 4))

    def up_step(p, carry):
        columns = pl.ds(pl.multiple_of(p * 512, 512), 512)
        value = mm(wide_g[:, columns], normed[...], 0, 0)
        for j in range(4):
            low = value[j * 64 : (j + 1) * 64]
            high_rows = value[256 + j * 64 : 256 + (j + 1) * 64]
            place_block(low, high_rows, UNIT_UP + j, p % 2, (p // 2) % 2, p // 4)
        return carry

    for part in range(4):
        lax.fori_loop(2 * part, 2 * part + 2, up_step, 0)
        pump("gup%d" % part)

    for tile in range(9, 13):
        load_weight(tile).wait()
        columns = slice((tile - 9) * 1024, (tile - 8) * 1024)

        def norm_step(m, carry, tile=tile, columns=columns):
            rows = pl.ds(pl.multiple_of(m * 256, 256), 256)
            add = mm(wide_g[rows, columns], weight[tile % 2], 1, 1)
            total[rows, :] = add if tile == 9 else total[rows, :] + add
            return carry

        lax.fori_loop(0, 2, norm_step, 0)
        load_weight(tile + 2).start()
        pump("gn%d" % (tile - 9))

    spill_normed.wait()

    def norm_back(h, gain, rows):
        center = h - jnp.mean(h, axis=1, keepdims=True)
        scale = lax.rsqrt(jnp.mean(center * center, axis=1, keepdims=True) + 1e-05)
        xh = center * scale
        q = total[rows, :]
        e = q * gain
        grad = (
            e - jnp.mean(e, axis=1, keepdims=True) - xh * jnp.mean(e * xh, axis=1, keepdims=True)
        ) * scale
        return (
            grad,
            jnp.sum(q * xh, axis=0, keepdims=True),
            jnp.sum(q, axis=0, keepdims=True),
        )

    def norm_two_step(m, carry):
        rows = pl.ds(pl.multiple_of(m * 32, 32), 32)
        grad, gain_sum, shift_sum = norm_back(hidden[rows, :], row_of(gain_two), rows)
        cot = inc[rows, :].astype(F32)
        grad = cot + grad
        hidden[rows, :] = grad
        grad_attn[rows, :] = grad.astype(BF)
        return (
            carry[0] + gain_sum,
            carry[1] + shift_sum,
            carry[2] + jnp.sum(cot, axis=0, keepdims=True),
        )

    none = jnp.zeros((1, 1024), F32)
    gain_sum, shift_sum, down_sum = lax.fori_loop(0, 16, norm_two_step, (none, none, none))
    vec_rows[6:7, :] = gain_sum
    vec_rows[7:8, :] = shift_sum
    vec_rows[8:9, :] = down_sum
    pump("ln2")

    wait_sent(range(4, 5))

    def out_step(m, carry):
        rows = pl.ds(pl.multiple_of(m * 512, 512), 512)
        value = mm(grad_attn[:, rows], attended[...], 0, 0)
        for q in range(4):
            at = q * 128
            place_block(
                value[at : at + 64], value[at + 64 : at + 128], UNIT_OUT, q % 2, q // 2, m
            )
        return carry

    lax.fori_loop(0, 2, out_step, 0)
    pump("out")
    load_weight(13).wait()

    def mixed_back(m, carry):
        rows = pl.ds(pl.multiple_of(m * 256, 256), 256)
        normed[rows, :] = mm(grad_attn[rows, :], weight[1], 1, 1).astype(BF)
        return carry

    lax.fori_loop(0, 2, mixed_back, 0)
    load_weight(15).start()
    fill_normed = load(7, normed_one_out, grad_attn)
    fill_normed.start()
    pump("mb")


    def heads(seq, pair):
        rows = pl.ds(pl.multiple_of(seq * 128, 128), 128)

        def lanes(base):
            return pl.ds(pl.multiple_of(base + pair * 128, 128), 128)

        first = lane_index(128) < 64
        minus = (-head_mask(3)).astype(BF)
        both = jnp.where(
            (lax.broadcasted_iota(jnp.int32, (256, 128), 0) % 128) // 64 == lane_index(256) // 64,
            1.0,
            0.0,
        ).astype(BF)
        q = qkv[rows, lanes(0)]
        k_two = two_heads(qkv[rows, lanes(1024)])
        v_two = two_heads(qkv[rows, lanes(2048)])
        grad_out = normed[rows, lanes(0)]
        product_rows = grad_out.astype(F32) * attended[rows, lanes(0)].astype(F32)
        head_part = product_rows.astype(BF)
        tail_part = (product_rows - head_part.astype(F32)).astype(BF)
        inner = mm(jnp.concatenate([head_part, tail_part], axis=1), both, 1, 0)
        scores = mm(
            jnp.concatenate([q, qkv[rows, lanes(3072)]], axis=1),
            jnp.concatenate([k_two, minus], axis=1),
            1,
            1,
        )
        grad_probs = mm(
            jnp.concatenate([grad_out, in_terms(inner)], axis=1),
            jnp.concatenate([v_two, minus], axis=1),
            1,
            1,
        )
        soft = jnp.exp(scores)
        grad_scores = (soft * grad_probs).astype(BF)
        grad_q = mm(grad_scores, k_two, 1, 0) * 0.125
        grad_k = mm(grad_scores, q, 0, 0)
        grad_v = mm(soft.astype(BF), grad_out, 0, 0)
        grad_k = jnp.where(first, grad_k[:128], grad_k[128:])
        grad_v = jnp.where(first, grad_v[:128], grad_v[128:])

        def unturn(value):
            return value * cosine[...] - rotated_partner(value) * sine[...]

        wide_g[rows, lanes(0)] = unturn(grad_q).astype(BF)
        wide_g[rows, lanes(1024)] = unturn(grad_k).astype(BF)
        wide_g[rows, lanes(2048)] = grad_v.astype(BF)

    def heads_step(index, carry):
        for pair in range(4):
            heads(index // 2, (index % 2) * 4 + pair)
        return carry

    for part in range(4):
        lax.fori_loop(2 * part, 2 * part + 2, heads_step, 0)
        pump("attn%d" % part)

    fill_normed.wait()
    wait_sent(range(5, 8))

    def qkv_step(p, carry):
        columns = pl.ds(pl.multiple_of(p * 384, 128), 384)
        value = mm(wide_g[:, columns], grad_attn[...], 0, 0)
        for j in range(3):
            low = value[j * 64 : (j + 1) * 64]
            high_rows = value[192 + j * 64 : 192 + (j + 1) * 64]
            place_block(low, high_rows, UNIT_QKV + j, p % 2, (p // 2) % 2, p // 4)
        return carry

    lax.fori_loop(0, 4, qkv_step, 0)
    pump("qkv0")
    lax.fori_loop(4, 8, qkv_step, 0)
    pump("qkv1")

    for tile in range(14, 17):
        load_weight(tile).wait()
        columns = slice((tile - 14) * 1024, (tile - 13) * 1024)

        def first_step(m, carry, tile=tile, columns=columns):
            rows = pl.ds(pl.multiple_of(m * 256, 256), 256)
            add = mm(wide_g[rows, columns], weight[tile % 2], 1, 1)
            total[rows, :] = add if tile == 14 else total[rows, :] + add
            return carry

        lax.fori_loop(0, 2, first_step, 0)
        if tile == 14:
            load_weight(16).start()
        pump("gf%d" % (tile - 14))
    gain_sum, shift_sum = none, none
    for seq in range(4):

        def norm_one_step(m, carry, seq=seq):
            rows = pl.ds(pl.multiple_of(seq * 128 + m * 32, 32), 32)
            inner = pl.ds(pl.multiple_of(m * 32, 32), 32)
            value = tokens[seq, inner, :].astype(F32) + time_embed[seq : seq + 1, :]
            grad, gain_add, shift_add = norm_back(value, row_of(gain_one), rows)
            grad = grad + hidden[rows, :]
            inc[rows, :] = grad.astype(BF)
            return (
                carry[0] + gain_add,
                carry[1] + shift_add,
                carry[2] + jnp.sum(grad, axis=0, keepdims=True),
            )

        gain_sum, shift_sum, embed_sum = lax.fori_loop(
            0, 4, norm_one_step, (gain_sum, shift_sum, none)
        )
        vec_rows[seq : seq + 1, :] = embed_sum
    vec_rows[4:5, :] = gain_sum
    vec_rows[5:6, :] = shift_sum
    for pair in range(8):
        message[pair, 0:16, :] = vec_rows[:, pair * 128 : (pair + 1) * 128]

    def small_copy(other):
        return remote(
            message.at[other // 4],
            small_recv.at[me],
            small_ssem.at[other],
            small_rsem.at[me],
            (other // 2, other % 2),
        )

    def small_start(step, carry):
        small_copy(lax.rem(me + step, devices)).start()
        return carry

    lax.fori_loop(1, devices, small_start, 0)
    small_recv[me] = message[place // 2]
    pump("rows")
    pump("small")

    def small_wait(step, carry):
        source = lax.rem(me + step, devices)
        pltpu.make_async_remote_copy(
            src_ref=message.at[0],
            dst_ref=small_recv.at[source],
            send_sem=small_ssem.at[source],
            recv_sem=small_rsem.at[source],
            device_id=(source // 2, source % 2),
            device_id_type=MESH_ID,
        ).wait()
        return carry

    lax.fori_loop(1, devices, small_wait, 0)

    def spread(source, carry):
        for row in range(4):
            at = 4 * source + row
            embeds[pl.ds(at, 1), :] = small_recv[source, row : row + 1, :]
            tables[0, pl.ds(at, 1), :] = small_recv[source, 20 + row : 21 + row, :]
            tables[1, pl.ds(at, 1), :] = small_recv[source, 24 + row : 25 + row, :]
        return carry + small_recv[source, 0:24, :]

    sums = lax.fori_loop(0, devices, spread, jnp.zeros((24, 128), F32))
    rest, terms = embeds[...], []
    for _ in range(3):
        terms.append(rest.astype(BF))
        rest = rest - terms[-1].astype(F32)

    def own_lanes(value):
        return jnp.where(core == 0, value, pltpu.roll(value, 64, 1))

    for part in range(2):
        turned = tables[part].astype(BF)
        value = sum(mm(turned, term, 0, 0) for term in terms)
        small_out[part * 128 : (part + 1) * 128, :] = own_lanes(value)
    small_out[256:280, :] = own_lanes(sums)
    wide = jnp.where(core == 0, sums[16:18], sums[18:20])
    small_out[280:282, :] = wide
    pump("end")

    for part in range(5):
        for copy in row_copies(part):
            copy.wait()
    wait_sent(range(8, 12))
    for batch in range(2):
        send_tokens(batch).wait_send()
    for seq in range(4):
        send_cot(seq).wait_send()
    for chain in range(2 * UNITS):
        one_copy(chain).wait_send()
        two_copy(chain).wait_send()
        for step in (1, 2, 3) if ORDERS[chain] != "z" else (1, 2):
            three_copy(chain, step).wait_send()
        gather_copy(chain).wait_send()


LAST_STEPS = 16
WINDOW = 0.2
LENGTHS = {
    "start": 24.0,
    "up": 2.5,
    "down": 1.7,
    "gu": 2.0,
    "mx": 1.7,
    "gup": 1.4,
    "gn": 1.7,
    "ln": 3.0,
    "out": 1.8,
    "mb": 1.9,
    "attn": 3.6,
    "qkv": 2.6,
    "gf": 1.7,
    "rows": 6.0,
}
PIECES = (
    ("start", ()),
    ("up0", ()),
    ("up1", ()),
    ("down0", (0,)),
    ("up2", ()),
    ("down1", (1,)),
    ("up3", ()),
    ("down2", (2,)),
    ("down3", (3,)),
    ("gu0", ()),
    ("mx0", ()),
    ("gu1", ()),
    ("mx1", ()),
    ("gu2", ()),
    ("mx2", ()),
    ("gu3", ()),
    ("mx3", ()),
    ("gup0", ()),
    ("gup1", ()),
    ("gup2", ()),
    ("gup3", (4, 5, 6, 7)),
    ("gn0", ()),
    ("gn1", ()),
    ("gn2", ()),
    ("gn3", ()),
    ("ln2", ()),
    ("out", (8,)),
    ("mb", ()),
    ("attn0", ()),
    ("attn1", ()),
    ("attn2", ()),
    ("attn3", ()),
    ("qkv0", ()),
    ("qkv1", (9, 10, 11)),
    ("gf0", ()),
    ("gf1", ()),
    ("gf2", ()),
    ("rows", ()),
)
CHAINS = {
    "x": ("one", "two", "three", "gather"),
    "y": ("one", "two", "three", "gather"),
    "z": ("one", "two", "last_x", "last_y", "gather"),
}
COSTS = {"core": 0.5, "one": 0.2, "two": 0.15, "three": 0.25, "last_x": 0.15, "last_y": 0.15, "gather": 0.05, "rows": 0.0}
FIRST = {"x": "x", "y": "y", "z": "a"}
SECOND = {"x": "y", "y": "x", "z": "b"}


def transfer(stage, kind):
    if stage == "one":
        return FIRST[kind], 0.262
    if stage == "two":
        return SECOND[kind], 0.262 if kind == "z" else 0.131
    if stage == "three":
        return "b", 0.131
    if stage == "last_x":
        return "x", 0.0655
    return "y", 0.0328


def schedule(orders):
    rate, lag = 0.094 / 2, 1.4
    flying = {axis: [] for axis in "xyab"}
    queues = {axis: [] for axis in "xyab"}
    arrived, order = [], []
    now, clock = 0.0, 0.0
    core = []

    def advance(until):
        nonlocal now
        while now < until:
            step = until - now
            for fly in flying.values():
                if fly:
                    step = min(step, min(f[0] for f in fly) * len(fly) / rate)
            now += step
            for axis, fly in flying.items():
                if fly:
                    part = step * rate / len(fly)
                    for f in fly:
                        f[0] -= part
                    for f in [f for f in fly if f[0] < 1e-9]:
                        fly.remove(f)
                        if f[1] is None:
                            continue
                        arrived.append((now + lag, f[1]))
            if step <= 0:
                now = until

    def issue():
        for axis in "baxy":
            queue = queues[axis]
            while queue and sum(f[0] for f in flying[axis] if f[1] is not None) < WINDOW:
                queue.sort()
                _, key, size = queue.pop(0)
                flying[axis].append([size, key, clock])
                if axis == "b":
                    flying["a"].append([size * (0.5 if key[0] == "two" else 0.75), None, clock])
                order.append(("start",) + key)

    def ready(stage, chain):
        axis, size = transfer(stage, orders[chain])
        queues[axis].append((chain, (stage, chain), size))

    def take(when, key):
        nonlocal clock
        clock = max(clock, when)
        advance(clock)
        stage, chain = key
        if stage == "rows":
            issue()
            return
        order.append(("add",) + key)
        clock += COSTS[stage]
        advance(clock)
        if stage == "core":
            ready("one", 2 * chain)
            ready("one", 2 * chain + 1)
        else:
            names = CHAINS[orders[chain]]
            if stage != names[-1]:
                ready(names[names.index(stage) + 1], chain)
        issue()

    def due():
        while True:
            arrived.sort()
            if not arrived or arrived[0][0] > clock:
                return
            take(*arrived.pop(0))

    for label, units in PIECES:
        clock += LENGTHS[label.rstrip("0123456789")]
        advance(clock)
        for unit in units:
            order.append(("start", "core", unit))
            arrived.append((clock + 2.3 + 0.3 * units.index(unit), ("core", unit)))
        if label == "mx3":
            queues["y"].append((100, ("rows", 0), 0.524))
        if label == "rows":
            for seq in range(4):
                queues["y"].append((50, ("rows", 1 + seq), 0.131))
        issue()
        due()
        order.append(("mark", label, 0))
    while arrived or any(flying.values()):
        if arrived:
            arrived.sort()
            if arrived[0][0] <= now or not any(flying.values()):
                take(*arrived.pop(0))
                continue
        advance(now + 0.1)
    order.insert(len(order) - LAST_STEPS, ("mark", "small", 0))
    order.append(("mark", "end", 0))
    return order


def layer_call(operands, constants, times):
    vmem = pl.BlockSpec(memory_space=pltpu.VMEM)
    hbm = pl.BlockSpec(memory_space=pl.ANY)
    dma = pltpu.SemaphoreType.DMA
    chains = 2 * UNITS
    return pl.pallas_call(
        layer_kernel,
        name="layer",
        out_shape=(
            jax.ShapeDtypeStruct((8, 64, 1024), BF),
            jax.ShapeDtypeStruct((8, 64, 1024), BF),
            jax.ShapeDtypeStruct((UNITS, 2, 64, 512), BF),
            jax.ShapeDtypeStruct((288, 128), F32),
            jax.ShapeDtypeStruct((512, 1024), BF),
        ),
        in_specs=[hbm] * 6 + [vmem] * 10 + [pl.BlockSpec(memory_space=pltpu.SMEM)],
        out_specs=(hbm, hbm, vmem, vmem, hbm),
        scratch_shapes=[
            pltpu.VMEM((2 * UNITS + 8, 2, 2, 2, 64, 512), BF),
            pltpu.VMEM((4, 2, 2, 2, 2, 64, 512), BF),
            pltpu.VMEM((UNITS, 2, 2, 2, 64, 512), BF),
            pltpu.VMEM((UNITS, 2, 2, 64, 512), BF),
            pltpu.VMEM((UNITS, 3, 64, 512), BF),
            pltpu.VMEM((2, 1024, 1024), BF),
            pltpu.VMEM((512, 4096), BF),
            pltpu.VMEM((512, 4096), BF),
            pltpu.VMEM((512, 4096), BF),
            pltpu.VMEM((4, 128, 1024), BF),
            pltpu.VMEM((512, 1024), BF),
            pltpu.VMEM((512, 1024), BF),
            pltpu.VMEM((512, 1024), F32),
            pltpu.VMEM((512, 1024), F32),
            pltpu.VMEM((512, 1024), BF),
            pltpu.VMEM((512, 1024), BF),
            pltpu.VMEM((4, 128, 1024), BF),
            pltpu.VMEM((8, 32, 128), F32),
            pltpu.VMEM((32, 32, 128), F32),
            pltpu.VMEM((16, 1024), F32),
            pltpu.VMEM((128, 128), F32),
            pltpu.VMEM((2, 128, 128), F32),
            pltpu.VMEM((8, 1024), F32),
            dma((17,)),
            dma((2,)),
            dma((2,)),
            dma((2,)),
            dma((4,)),
            dma((4,)),
            dma((4,)),
            dma((4,)),
            pltpu.SemaphoreType.REGULAR((4,)),
            dma((chains,)),
            dma((chains,)),
            dma((chains,)),
            dma((chains,)),
            dma((3 * chains,)),
            dma((3 * chains,)),
            dma((chains,)),
            dma((chains,)),
            dma((32,)),
            dma((32,)),
            dma((5,)),
            dma((5,)),
        ],
        compiler_params=pltpu.CompilerParams(
            collective_id=0, has_side_effects=True, vmem_limit_bytes=VMEM_LIMIT
        ),
    )(*operands, *constants, times)


def body(
    tokens,
    noise_times,
    time_proj,
    time_bias,
    gain_one,
    shift_one,
    w_qkv,
    w_out,
    gain_two,
    shift_two,
    w_up,
    b_up,
    w_down,
    b_down,
    cotangent,
):
    seq_ways, tok_ways = lax.axis_size("seq"), lax.axis_size("tok")
    model_width = tokens.shape[-1]
    seq_count, length = tokens.shape[0] // tok_ways, tokens.shape[1] * tok_ways
    row_count = seq_count * length
    all_times = lax.all_gather(noise_times, "seq", tiled=True)
    own_times = lax.dynamic_slice_in_dim(
        noise_times, lax.axis_index("tok") * seq_count, seq_count
    )
    embed_table = noise_table(own_times).astype(jnp.bfloat16)
    time_embed = product(embed_table, time_proj) + time_bias.astype(jnp.float32)
    tokens = gather_sequences(tokens)
    incoming = gather_sequences(cotangent).reshape(row_count, model_width)
    hidden_zero = (tokens.astype(jnp.float32) + time_embed[:, None, :]).reshape(
        row_count, model_width
    )
    normed_one, pull_one = jax.vjp(
        layer_norm, hidden_zero, gain_one.astype(jnp.float32), shift_one.astype(jnp.float32)
    )
    normed_one = normed_one.astype(jnp.bfloat16)
    projected = product(normed_one, w_qkv).astype(jnp.bfloat16)
    received, attended, log_total = attend_items(
        projected.reshape(seq_count, length, 3, 1, model_width)
    )
    attended = attended.reshape(row_count, model_width)
    hidden_one = hidden_zero + product(attended, w_out)
    normed_two, pull_two = jax.vjp(
        layer_norm, hidden_one, gain_two.astype(jnp.float32), shift_two.astype(jnp.float32)
    )
    normed_two = normed_two.astype(jnp.bfloat16)
    upward = product(normed_two, w_up) + b_up.astype(jnp.float32)
    active, pull_gelu = jax.vjp(jax.nn.gelu, upward)
    active = active.astype(jnp.bfloat16)
    out_wdown = scatter_sum(contract_rows(incoming, active))
    result = hidden_one + (product(active, w_down) + b_down.astype(jnp.float32))
    mixed_out = return_positions(
        result.astype(jnp.bfloat16).reshape(seq_count, length, model_width)
    )
    sum_down = jnp.sum(incoming, axis=0, dtype=jnp.float32)
    grad_active = times_transpose(incoming, w_down)
    (grad_upward,) = pull_gelu(grad_active)
    grad_upward = grad_upward.astype(jnp.bfloat16)
    sum_up = jnp.sum(grad_upward, axis=0, dtype=jnp.float32)
    out_wup = scatter_sum(contract_rows(grad_upward, normed_two))
    grad_norm_two = times_transpose(grad_upward, w_up)
    grad_hidden_two, grad_gain_two, grad_shift_two = pull_two(grad_norm_two)
    grad_hidden_one = incoming.astype(jnp.float32) + grad_hidden_two
    grad_attn = grad_hidden_one.astype(jnp.bfloat16)
    out_wout = scatter_sum(contract_rows(grad_attn, attended))
    grad_mixed = times_transpose(grad_attn, w_out).astype(jnp.bfloat16)
    grad_parts = attention_grad(
        received, log_total, grad_mixed.reshape(seq_count, length, 1, model_width)
    ).reshape(row_count, 3 * model_width)
    out_wqkv = scatter_sum(contract_rows(grad_parts, normed_one))
    grad_norm_one = times_transpose(grad_parts, w_qkv)
    grad_hidden_zero, grad_gain_one, grad_shift_one = pull_one(grad_norm_one)
    grad_total = grad_hidden_one + grad_hidden_zero
    grad_tokens = return_positions(
        grad_total.astype(jnp.bfloat16).reshape(seq_count, length, model_width)
    )
    grad_embed = jnp.sum(grad_total.reshape(seq_count, length, model_width), axis=1)
    wide = sum_up.shape[0] // model_width
    small = jnp.concatenate(
        [
            grad_embed.reshape(seq_count, seq_ways, -1).swapaxes(0, 1),
            grad_gain_one.reshape(seq_ways, 1, -1),
            grad_shift_one.reshape(seq_ways, 1, -1),
            grad_gain_two.reshape(seq_ways, 1, -1),
            grad_shift_two.reshape(seq_ways, 1, -1),
            sum_down.reshape(seq_ways, 1, -1),
            sum_up.reshape(seq_ways, wide, -1),
        ],
        axis=1,
    )
    small = lax.all_to_all(small, "seq", split_axis=0, concat_axis=0, tiled=True)
    small = lax.all_gather(small, "tok", axis=1)
    embeds = small[:, :, :seq_count].reshape(-1, small.shape[-1])
    out_proj = jnp.dot(
        noise_table(all_times).astype(jnp.bfloat16).astype(jnp.float32).T,
        embeds,
        precision=lax.Precision.HIGHEST,
    )
    out_bias = jnp.sum(embeds, axis=0)
    sums = jnp.sum(small[:, :, seq_count:], axis=(0, 1))
    return (
        mixed_out,
        grad_tokens,
        out_proj,
        out_bias,
        sums[0],
        sums[1],
        out_wqkv,
        out_wout,
        sums[2],
        sums[3],
        out_wup,
        sums[5:].reshape(-1),
        out_wdown,
        sums[4],
    )


def rotary_lanes():
    halves = HD // 2
    frequency = np.exp(-math.log(10000.0) * np.arange(halves, dtype=np.float32) / halves)
    angles = np.arange(128, dtype=np.float32)[:, None] * frequency.astype(np.float32)[None, :]
    cosine, sine = np.cos(angles), np.sin(angles)
    return (
        jnp.asarray(np.tile(cosine, (1, 4)), jnp.float32),
        jnp.asarray(np.concatenate([-sine, sine] * 2, axis=1), jnp.float32),
    )


def fast_body(
    tokens,
    noise_times,
    time_proj,
    time_bias,
    gain_one,
    shift_one,
    w_qkv,
    w_out,
    gain_two,
    shift_two,
    w_up,
    b_up,
    w_down,
    b_down,
    cotangent,
):
    model_width = tokens.shape[-1]
    cosine, sine = rotary_lanes()
    mixed_out, grad_tokens, shares, small, _ = layer_call(
        (tokens, cotangent, w_qkv, w_out, w_up, w_down),
        (
            time_proj,
            time_bias,
            gain_one,
            shift_one,
            gain_two,
            shift_two,
            b_up,
            b_down,
            cosine,
            sine,
        ),
        noise_times,
    )
    shares = jnp.swapaxes(shares, 1, 2).reshape(UNITS, 64, model_width)
    out_wdown = jnp.swapaxes(shares[0:4], 1, 2).reshape(4 * model_width, 64)
    out_wup = shares[4:8].reshape(256, model_width).T
    out_wout = shares[8].T
    out_wqkv = shares[9:12].reshape(192, model_width).T
    out_proj = small[0:256, 0:64]
    sums = small[256:280, 0:64]
    return (
        mixed_out,
        grad_tokens,
        out_proj,
        sums[0] + sums[1] + sums[2] + sums[3],
        sums[4],
        sums[5],
        out_wqkv.astype(jnp.float32),
        out_wout.astype(jnp.float32),
        sums[6],
        sums[7],
        out_wup.astype(jnp.float32),
        small[280:282].reshape(-1),
        out_wdown.astype(jnp.float32),
        sums[8],
    )


def solution(mesh):
    chosen = fast_body if (mesh.shape["seq"], mesh.shape["tok"]) == (16, 2) else body
    in_specs = (
        P("seq", "tok", None),
        P("seq"),
        P(),
        P(),
        P(),
        P(),
        P(),
        P(),
        P(),
        P(),
        P(),
        P(),
        P(),
        P(),
        P("seq", "tok", None),
    )
    out_specs = (
        P("seq", "tok", None),
        P("seq", "tok", None),
        P(None, "seq"),
        P("seq"),
        P("seq"),
        P("seq"),
        P(None, "seq"),
        P(None, "seq"),
        P("seq"),
        P("seq"),
        P(None, "seq"),
        P("seq"),
        P(None, "seq"),
        P("seq"),
    )
    return jax.shard_map(chosen, mesh=mesh, in_specs=in_specs, out_specs=out_specs, check_vma=False)
```

```python
import math

import jax
import jax.numpy as jnp
import numpy as np
from jax import lax
from jax.experimental import pallas as pl
from jax.experimental.pallas import tpu as pltpu
from jax.sharding import PartitionSpec as P

HD = 64
TEMB = 256
VMEM_LIMIT = 64 * 1024 * 1024 - 65536


def layer_norm(hidden, gain_vec, shift_vec):
    center = hidden - jnp.mean(hidden, axis=-1, keepdims=True)
    spread = jnp.mean(center * center, axis=-1, keepdims=True)
    return center * lax.rsqrt(spread + 1e-05) * gain_vec + shift_vec


def noise_table(noise_steps):
    halves = TEMB // 2
    frequency = jnp.exp(-math.log(10000.0) * jnp.arange(halves, dtype=jnp.float32) / halves)
    angles = noise_steps.astype(jnp.float32)[:, None] * frequency[None, :]
    return jnp.concatenate([jnp.sin(angles), jnp.cos(angles)], axis=-1)


def rotary_tables(length):
    halves = HD // 2
    frequency = jnp.exp(-math.log(10000.0) * jnp.arange(halves, dtype=jnp.float32) / halves)
    angles = jnp.arange(length, dtype=jnp.float32)[:, None] * frequency[None, :]
    angles = jnp.concatenate([angles, angles], axis=-1)[:, None, :]
    return (jnp.cos(angles), jnp.sin(angles))


def rotate(values, cosine, sine_tab):
    halves = values.shape[-1] // 2
    turned = jnp.concatenate([-values[..., halves:], values[..., :halves]], axis=-1)
    return values * cosine + turned * sine_tab


def unrotate(gradient, cosine, sine_tab):
    halves = gradient.shape[-1] // 2
    scaled = gradient * sine_tab
    turned = jnp.concatenate([scaled[..., halves:], -scaled[..., :halves]], axis=-1)
    return gradient * cosine + turned


def product(left_side, right_side):
    return jnp.dot(left_side, right_side, preferred_element_type=jnp.float32)


def contract_rows(left_side, right_side):
    return jnp.einsum("ra,rb->ab", left_side, right_side, preferred_element_type=jnp.float32)


def times_transpose(left_side, right_side):
    return jnp.einsum("rb,ab->ra", left_side, right_side, preferred_element_type=jnp.float32)


def split_heads(received):
    batch_size, length = (received.shape[0], received.shape[1])
    local_heads = received.shape[-1] // HD
    split_view = received.reshape(batch_size, length, 3, local_heads, HD)
    cosine, sine_tab = rotary_tables(length)
    queries = rotate(split_view[:, :, 0].astype(jnp.float32), cosine, sine_tab).astype(jnp.bfloat16)
    keys_rot = rotate(split_view[:, :, 1].astype(jnp.float32), cosine, sine_tab).astype(
        jnp.bfloat16
    )
    return (queries, keys_rot, split_view[:, :, 2], cosine, sine_tab)


def attend_items(received):
    batch_size, length = (received.shape[0], received.shape[1])
    scaling = 1.0 / math.sqrt(HD)
    queries, keys_rot, values, cosine, sine_tab = split_heads(received)
    scores = (
        jnp.einsum("gqhd,gkhd->ghqk", queries, keys_rot, preferred_element_type=jnp.float32)
        * scaling
    )
    highest = jnp.max(scores, axis=-1, keepdims=True)
    exponent = jnp.exp(scores - highest)
    totals = jnp.sum(exponent, axis=-1, keepdims=True)
    prob_rows = (exponent / totals).astype(jnp.bfloat16)
    log_total = (highest + jnp.log(totals))[..., 0]
    attended = jnp.einsum("ghqk,gkhd->gqhd", prob_rows, values, preferred_element_type=jnp.float32)
    attended = attended.astype(jnp.bfloat16).reshape(batch_size, length, 1, -1)
    return (received, attended, log_total)


def attention_grad(received, log_total, grad_heads):
    batch_size, length = (received.shape[0], received.shape[1])
    scaling = 1.0 / math.sqrt(HD)
    queries, keys_rot, values, cosine, sine_tab = split_heads(received)
    scores = (
        jnp.einsum("gqhd,gkhd->ghqk", queries, keys_rot, preferred_element_type=jnp.float32)
        * scaling
    )
    prob_rows = jnp.exp(scores - log_total[..., None])
    grad_out = grad_heads.reshape(batch_size, length, values.shape[2], HD)
    grad_probs = jnp.einsum("gqhd,gkhd->ghqk", grad_out, values, preferred_element_type=jnp.float32)
    grad_values = jnp.einsum(
        "ghqk,gqhd->gkhd",
        prob_rows.astype(jnp.bfloat16),
        grad_out,
        preferred_element_type=jnp.float32,
    )
    inner_sum = jnp.sum(prob_rows * grad_probs, axis=-1, keepdims=True)
    grad_scores = (prob_rows * (grad_probs - inner_sum)).astype(jnp.bfloat16)
    grad_queries = (
        jnp.einsum("ghqk,gkhd->gqhd", grad_scores, keys_rot, preferred_element_type=jnp.float32)
        * scaling
    )
    grad_keys = (
        jnp.einsum("ghqk,gqhd->gkhd", grad_scores, queries, preferred_element_type=jnp.float32)
        * scaling
    )
    stacked = jnp.stack(
        [
            unrotate(grad_queries, cosine, sine_tab),
            unrotate(grad_keys, cosine, sine_tab),
            grad_values,
        ],
        axis=2,
    )
    return stacked.astype(jnp.bfloat16).reshape(batch_size, length, 3, 1, -1)


def gather_sequences(values):
    return lax.all_to_all(values, "tok", split_axis=0, concat_axis=1, tiled=True)


def return_positions(values):
    return lax.all_to_all(values, "tok", split_axis=1, concat_axis=0, tiled=True)


def group_scatter(parts, own, size, axis, perm_of):
    total = lax.dynamic_index_in_dim(parts, own, 0, keepdims=False).astype(jnp.float32)
    for shift in range(1, size):
        piece = lax.dynamic_index_in_dim(parts, (own + shift) % size, 0, keepdims=False)
        total = total + lax.ppermute(piece, axis, perm_of(shift)).astype(jnp.float32)
    return total.astype(jnp.bfloat16)


def group_gather(piece, own, size, axis, perm_of):
    held = jnp.zeros((size,) + piece.shape, piece.dtype)
    held = lax.dynamic_update_index_in_dim(held, piece, own, 0)
    for shift in range(1, size):
        other = lax.ppermute(piece, axis, perm_of(shift))
        held = lax.dynamic_update_index_in_dim(held, other, (own - shift) % size, 0)
    return held


def scatter_sum(gradient):
    seq_ways, tok_ways = lax.axis_size("seq"), lax.axis_size("tok")
    outer, middle = 4, seq_ways // 8
    place, turn = lax.axis_index("seq"), lax.axis_index("tok")
    core, mid, out = place % 2, (place // 2) % middle, place // (2 * middle)

    def core_perm(shift):
        return [(i, i ^ 1) for i in range(seq_ways)]

    def mid_perm(shift):
        return [
            (i, (i // (2 * middle)) * 2 * middle + ((i // 2 + shift) % middle) * 2 + i % 2)
            for i in range(seq_ways)
        ]

    def out_perm(shift):
        return [(i, (i + shift * 2 * middle) % seq_ways) for i in range(seq_ways)]

    def tok_perm(shift):
        return [(i, (i + shift) % tok_ways) for i in range(tok_ways)]

    rows, width = gradient.shape[0] // seq_ways, gradient.shape[1]
    parts = gradient.astype(jnp.bfloat16).reshape(outer * middle, 2, rows, width)
    parts = group_scatter(jnp.swapaxes(parts, 0, 1), core, 2, "seq", core_perm)
    parts = parts.reshape(outer, middle, rows, 2, tok_ways, width // (2 * tok_ways))
    first = jnp.transpose(parts[:, :, :, 0], (1, 3, 0, 2, 4))
    second = jnp.transpose(parts[:, :, :, 1], (3, 1, 0, 2, 4))
    first = group_scatter(first, mid, middle, "seq", mid_perm)
    second = group_scatter(second, turn, tok_ways, "tok", tok_perm)
    first = group_scatter(first, turn, tok_ways, "tok", tok_perm)
    second = group_scatter(second, mid, middle, "seq", mid_perm)
    both = jnp.stack([first, second], axis=1)
    both = group_scatter(both, out, outer, "seq", out_perm)
    both = group_gather(both, turn, tok_ways, "tok", tok_perm)
    return jnp.transpose(both, (2, 1, 0, 3)).reshape(rows, width).T.astype(jnp.float32)


MESH_ID = pl.DeviceIdType.MESH
BF = jnp.bfloat16
F32 = jnp.float32
UNITS = 12
UNIT_DOWN, UNIT_UP, UNIT_OUT, UNIT_QKV = 0, 4, 8, 9
ORDERS = "wzywywywwwyzwyyyywwwzwwy"
GELU_A = math.sqrt(2.0 / math.pi)
GELU_B = 0.044715


def mm(left, right, left_dim, right_dim):
    return lax.dot_general(
        left, right, (((left_dim,), (right_dim,)), ((), ())), preferred_element_type=F32
    )


def rotated_partner(values):
    lane = lax.broadcasted_iota(jnp.int32, values.shape, 1)
    return jnp.where(lane % 64 < 32, pltpu.roll(values, 96, 1), pltpu.roll(values, 32, 1))


def lane_index(rows):
    return lax.broadcasted_iota(jnp.int32, (rows, 128), 1)


def two_heads(value):
    first = lane_index(128) < 64
    zero = jnp.zeros_like(value)
    return jnp.concatenate([jnp.where(first, value, zero), jnp.where(first, zero, value)], axis=0)


def head_mask(count):
    lane = lane_index(256)
    row = lax.broadcasted_iota(jnp.int32, (256, 128), 0)
    return jnp.where((lane // 64 == row // 128) & (lane % 64 < count), 1.0, 0.0)


def in_terms(value):
    lane = lane_index(value.shape[0]) % 64
    out, rest = jnp.zeros(value.shape, BF), value
    for index in range(3):
        term = rest.astype(BF)
        rest = rest - term.astype(F32)
        out = jnp.where(lane == index, term, out)
    return out


def layer_kernel(
    tokens_in,
    cotangent_in,
    w_qkv,
    w_out,
    w_up,
    w_down,
    time_proj,
    time_bias,
    gain_one,
    shift_one,
    gain_two,
    shift_two,
    b_up,
    b_down,
    cosine,
    sine,
    noise_times,
    mixed_out,
    tokens_out,
    shares_out,
    small_out,
    normed_one_out,
    hidden_one_out,
    partial,
    core_recv,
    recv_one,
    recv_two,
    recv_three,
    weight,
    wide_a,
    wide_g,
    q_held,
    k_held,
    v_held,
    log_held,
    tokens,
    inc,
    normed,
    hidden,
    total,
    grad_attn,
    attended,
    message,
    small_recv,
    vec_rows,
    embeds,
    tables,
    time_embed,
    load_sem,
    weight_sem,
    token_ssem,
    token_rsem,
    cot_ssem,
    cot_rsem,
    core_ssem,
    core_rsem,
    credit,
    one_ssem,
    one_rsem,
    two_ssem,
    two_rsem,
    three_ssem,
    three_rsem,
    gather_ssem,
    gather_rsem,
    small_ssem,
    small_rsem,
    back_ssem,
    back_rsem,
):
    place, turn = lax.axis_index("seq"), lax.axis_index("tok")
    core, xx, zz = place % 2, (place // 2) % 2, place // 4
    yy = turn
    me = place * 2 + turn
    devices = 32

    def at_seq(z, x, c):
        return ((z * 2 + x) * 2 + c, turn)

    core_peer = at_seq(zz, xx, 1 - core)
    x_peer = at_seq(zz, 1 - xx, core)
    y_peer = (place, 1 - turn)

    def load(index, source, target):
        return pltpu.make_async_copy(source, target, load_sem.at[index])

    def load_weight(tile):
        if tile == 0 or tile == 13:
            source = w_out
        elif tile < 5:
            source = w_up.at[:, pl.ds((tile - 1) * 1024, 1024)]
        elif tile < 9:
            source = w_down.at[pl.ds((tile - 5) * 1024, 1024), :]
        elif tile < 13:
            source = w_up.at[:, pl.ds((tile - 9) * 1024, 1024)]
        elif tile < 17:
            source = w_qkv.at[:, pl.ds((tile - 14) * 1024, 1024)]
        else:
            source = w_down.at[pl.ds((tile - 17) * 1024, 1024), :]
        return pltpu.make_async_copy(source, weight.at[tile % 2], weight_sem.at[tile % 2])

    def row_of(vector):
        return vector[...].astype(F32).reshape(1, vector.shape[0])

    own_half = pl.ds(turn * 64, 64)

    def load_qkv(part):
        index, half = part // 2, part % 2
        columns = pl.ds(index * 1024, 1024)
        target = (wide_a, wide_g)[half]
        return load(
            1 + part, w_qkv.at[pl.ds(half * 512, 512), columns], target.at[:, columns]
        )

    def load_cot(seq):
        return load(
            8 + seq,
            cotangent_in.at[turn * 4 + seq],
            inc.at[pl.ds(seq * 128 + turn * 64, 64)],
        )

    load_tokens = load(0, tokens_in.at[pl.ds(turn * 4, 4)], tokens.at[:, own_half])
    load_tokens.start()
    for part in range(6):
        load_qkv(part).start()
    load_weight(0).start()
    load_weight(1).start()
    for seq in range(4):
        load_cot(seq).start()

    barrier = pltpu.get_barrier_semaphore()

    def greet(step, carry):
        other = lax.rem(me + step, devices)
        pl.semaphore_signal(
            barrier, inc=1, device_id=(other // 2, other % 2), device_id_type=MESH_ID
        )
        return carry

    lax.fori_loop(1, devices, greet, 0)
    message[...] = jnp.zeros_like(message)
    vec_rows[...] = jnp.zeros_like(vec_rows)
    lane = lax.broadcasted_iota(jnp.int32, (1, 128), 1).astype(F32)
    frequency = jnp.exp((-math.log(10000.0) * lane) / 128)
    steps = [jnp.where(turn == 0, noise_times[j], noise_times[4 + j]) for j in range(4)]
    angles = jnp.concatenate([frequency * step.astype(F32) for step in steps] * 2, axis=0)
    sine_rows = jnp.sin(angles).astype(BF)
    cosine_rows = jnp.cos(angles).astype(BF)
    time_embed[...] = (
        mm(jnp.concatenate([sine_rows, cosine_rows], axis=1), time_proj[...], 1, 0)
        + row_of(time_bias)
    )
    for pair in range(8):
        message[pair, 20:24, :] = sine_rows.astype(F32)[0:4]
        message[pair, 24:28, :] = cosine_rows.astype(F32)[0:4]
    pl.semaphore_wait(barrier, devices - 1)

    def remote(source, target, send, recv, device):
        return pltpu.make_async_remote_copy(
            src_ref=source,
            dst_ref=target,
            send_sem=send,
            recv_sem=recv,
            device_id=device,
            device_id_type=MESH_ID,
        )

    parity, high = zz % 2, zz // 2

    def core_copy(unit):
        slot = unit % 4
        return remote(
            partial.at[pl.ds(2 * UNITS + 2 * slot, 2)],
            core_recv.at[slot],
            core_ssem.at[slot],
            core_rsem.at[slot],
            core_peer,
        )

    def half_of(chain):
        return chain // 2, pl.ds(32 * (chain % 2), 32)

    def one_copy(chain):
        unit, rows = half_of(chain)
        if ORDERS[chain] in "xw":
            source, device = partial.at[2 * unit + 1 - xx, :, :, :, rows], x_peer
        elif ORDERS[chain] == "y":
            source, device = partial.at[pl.ds(2 * unit, 2), 1 - yy, :, :, rows], y_peer
        else:
            source = partial.at[pl.ds(2 * unit, 2), :, 1 - parity, :, rows]
            device = at_seq(2 * high + 1 - parity, xx, core)
        target = recv_one.at[unit, :, :, :, rows]
        return remote(source, target, one_ssem.at[chain], one_rsem.at[chain], device)

    def two_copy(chain):
        unit, rows = half_of(chain)
        if ORDERS[chain] == "x":
            source, device = partial.at[2 * unit + xx, 1 - yy, :, :, rows], y_peer
        elif ORDERS[chain] == "y":
            source, device = partial.at[2 * unit + 1 - xx, yy, :, :, rows], x_peer
        elif ORDERS[chain] == "w":
            source = partial.at[2 * unit + xx, :, 1 - parity, :, rows]
            device = at_seq(2 * high + 1 - parity, xx, core)
        else:
            source = partial.at[pl.ds(2 * unit, 2), :, parity, 1 - high, rows]
            device = at_seq(2 * (1 - high) + parity, xx, core)
        target = recv_two.at[unit, :, :, rows]
        return remote(source, target, two_ssem.at[chain], two_rsem.at[chain], device)

    def three_copy(chain, step):
        unit, rows = half_of(chain)
        index = 3 * chain + step - 1
        if ORDERS[chain] in "xy":
            other = (zz + step) % 4
            source = partial.at[2 * unit + xx, yy, other % 2, other // 2, rows]
            target, device = recv_three.at[unit, step - 1, rows], at_seq(other, xx, core)
        elif step == 1 and ORDERS[chain] == "w":
            source = partial.at[2 * unit + xx, :, parity, 1 - high, rows]
            target = recv_three.at[unit, pl.ds(0, 2), rows]
            device = at_seq(2 * (1 - high) + parity, xx, core)
        elif step == 1:
            source = partial.at[2 * unit + 1 - xx, :, parity, high, rows]
            target, device = recv_three.at[unit, pl.ds(0, 2), rows], x_peer
        else:
            source = partial.at[2 * unit + xx, :, parity, high, rows]
            target, device = recv_three.at[unit, pl.ds(2, 2), rows], y_peer
        return remote(source, target, three_ssem.at[index], three_rsem.at[index], device)

    def gather_copy(chain):
        unit, rows = half_of(chain)
        view = shares_out.at[unit, yy, rows]
        return remote(view, view, gather_ssem.at[chain], gather_rsem.at[chain], y_peer)

    def start_core(unit):
        if unit >= 4:
            pl.semaphore_wait(credit.at[unit % 4], 1)
        core_copy(unit).start()

    def add_core(unit):
        core_copy(unit).wait_recv()

        def add(index, carry):
            x, h, p = index // 4, (index // 2) % 2, index % 2
            partial[2 * unit + x, h, p] = (
                partial[2 * unit + x, h, p] + core_recv[unit % 4, x, h, p]
            )
            return carry

        lax.fori_loop(0, 8, add, 0)
        if unit < UNITS - 4:
            pl.semaphore_signal(
                credit.at[unit % 4], inc=1, device_id=core_peer, device_id_type=MESH_ID
            )

    def add_one(chain):
        one_copy(chain).wait_recv()
        unit, rows = half_of(chain)
        for a in range(2):
            for b in range(2):
                for c in range(2):
                    if ORDERS[chain] in "xw":
                        at = (2 * unit + xx, a, b, c, rows)
                    elif ORDERS[chain] == "y":
                        at = (2 * unit + a, yy, b, c, rows)
                    else:
                        at = (2 * unit + a, b, parity, c, rows)
                    partial[at] = partial[at] + recv_one[unit, a, b, c, rows]

    def add_two(chain):
        two_copy(chain).wait_recv()
        unit, rows = half_of(chain)
        for a in range(2):
            for b in range(2):
                if ORDERS[chain] == "z":
                    at = (2 * unit + a, b, parity, high, rows)
                elif ORDERS[chain] == "w":
                    at = (2 * unit + xx, a, parity, b, rows)
                else:
                    at = (2 * unit + xx, yy, a, b, rows)
                partial[at] = partial[at] + recv_two[unit, a, b, rows]

    def add_three(chain):
        unit, rows = half_of(chain)
        value = partial[2 * unit + xx, yy, parity, high, rows].astype(F32)
        for step in (1, 2, 3):
            three_copy(chain, step).wait_recv()
        for step in (1, 2, 3):
            value = value + recv_three[unit, step - 1, rows].astype(F32)
        shares_out[unit, yy, rows] = value.astype(BF)

    def add_last_x(chain):
        three_copy(chain, 1).wait_recv()
        unit, rows = half_of(chain)
        for h in range(2):
            at = (2 * unit + xx, h, parity, high, rows)
            partial[at] = partial[at] + recv_three[unit, h, rows]

    def add_swap(chain):
        three_copy(chain, 2).wait_recv()
        unit, rows = half_of(chain)
        for h in range(2):
            value = partial[2 * unit + xx, h, parity, high, rows].astype(F32)
            value = value + recv_three[unit, 2 + h, rows].astype(F32)
            shares_out[unit, h, rows] = value.astype(BF)

    def start_three(chain):
        for step in (2, 1, 3):
            three_copy(chain, step).start()

    actions = {
        "core": (start_core, add_core),
        "one": (lambda unit: one_copy(unit).start(), add_one),
        "two": (lambda unit: two_copy(unit).start(), add_two),
        "three": (start_three, add_three),
        "last_x": (lambda unit: three_copy(unit, 1).start(), add_last_x),
        "swap": (lambda unit: three_copy(unit, 2).start(), add_swap),
        "gather": (
            lambda unit: gather_copy(unit).start(),
            lambda unit: gather_copy(unit).wait_recv(),
        ),
    }
    def row_copies(part, seq):
        source, target = (attended, mixed_out) if part == 0 else (inc, tokens_out)
        views = [source.at[pl.ds(seq * 128 + y * 64, 64)] for y in (yy, 1 - yy)]
        index, at = 4 * part + seq, yy * 4 + seq
        local = pltpu.make_async_copy(views[0], target.at[at], load_sem.at[13 + index])
        away = remote(views[1], target.at[at], back_ssem.at[index], back_rsem.at[index], y_peer)
        return local, away

    def start_rows(part):
        for seq in range(4) if part == 0 else (part - 1,):
            for copy in row_copies(min(part, 1), seq):
                copy.start()

    plan = schedule(ORDERS)
    cursor = [0]

    def pump(label):
        while True:
            kind, stage, unit = plan[cursor[0]]
            cursor[0] += 1
            if kind == "mark":
                assert stage == label
                return
            if stage == "rows":
                start_rows(unit)
            else:
                actions[stage][0 if kind == "start" else 1](unit)

    def wait_sent(units):
        for unit in units:
            core_copy(unit).wait_send()

    def place_block(low, high_rows, unit, x, p, q):
        own, away = 2 * unit + x, 2 * UNITS + 2 * (unit % 4) + x
        for value, at in (
            (low, own * (1 - core) + away * core),
            (high_rows, away * (1 - core) + own * core),
        ):
            value = value.astype(BF)
            for h in range(2):
                partial[at, h, p, q] = value[:, h * 512 : (h + 1) * 512]

    def send_tokens(batch):
        return remote(
            tokens_in.at[pl.ds((1 - turn) * 4 + 2 * batch, 2)],
            tokens.at[pl.ds(2 * batch, 2), own_half],
            token_ssem.at[batch],
            token_rsem.at[batch],
            y_peer,
        )

    def send_cot(seq):
        return remote(
            cotangent_in.at[(1 - turn) * 4 + seq],
            inc.at[pl.ds(seq * 128 + turn * 64, 64)],
            cot_ssem.at[seq],
            cot_rsem.at[seq],
            y_peer,
        )

    send_tokens(0).start()
    load_tokens.wait()

    def norm(value, gain, shift):
        center = value - jnp.mean(value, axis=1, keepdims=True)
        spread = jnp.mean(center * center, axis=1, keepdims=True)
        return (center * lax.rsqrt(spread + 1e-05) * gain + shift).astype(BF)

    def first_norm(seqs, side):
        starts = [pl.multiple_of(seq * 128 + side * 64, 64) for seq in seqs]
        for seq, start in zip(seqs, starts):

            def step(m, carry, seq=seq, start=start):
                rows = pl.ds(pl.multiple_of(start + m * 32, 32), 32)
                inner = pl.ds(pl.multiple_of(side * 64 + m * 32, 32), 32)
                value = tokens[seq, inner, :].astype(F32) + time_embed[seq : seq + 1, :]
                hidden[rows, :] = value
                grad_attn[rows, :] = norm(value, row_of(gain_one), row_of(shift_one))
                return carry

            lax.fori_loop(0, 2, step, 0)
        if len(seqs) == 4:
            send_tokens(1).start()
        rows = jnp.concatenate([grad_attn[pl.ds(start, 64), :] for start in starts], axis=0)
        for part in range(3):
            columns = slice(part * 1024, (part + 1) * 1024)
            if len(seqs) == 4:
                load_qkv(2 * part).wait()
                load_qkv(2 * part + 1).wait()
            value = mm(rows[:, :512], wide_a[:, columns], 1, 0)
            value = (value + mm(rows[:, 512:], wide_g[:, columns], 1, 0)).astype(BF)
            for index, start in enumerate(starts):
                piece = value[index * 64 : (index + 1) * 64]
                if part == 0:
                    wide_a[pl.ds(start, 64), 3072:4096] = piece
                else:
                    (normed, v_held)[part - 1][pl.ds(start, 64), :] = piece

    def forward_heads(seq, pair):
        rows = pl.ds(pl.multiple_of(seq * 128, 128), 128)
        lanes = pl.ds(pl.multiple_of(pair * 128, 128), 128)

        def turned(value):
            value = value.astype(F32)
            return value * cosine[...] + rotated_partner(value) * sine[...]

        first = lane_index(128) < 64
        q = (turned(wide_a[rows, pl.ds(pl.multiple_of(3072 + pair * 128, 128), 128)]) * 0.125).astype(BF)
        k = turned(normed[rows, lanes]).astype(BF)
        q_held[rows, lanes] = q
        k_held[rows, lanes] = k
        scores = mm(q, two_heads(k), 1, 1)
        highest, exponent = [], []
        for part in range(2):
            s = scores[:, part * 128 : (part + 1) * 128]
            highest.append(jnp.max(s, axis=1, keepdims=True))
            exponent.append(jnp.exp(s - highest[part]))
        sums = mm(
            jnp.concatenate(exponent, axis=1).astype(BF),
            jnp.concatenate(
                [two_heads(v_held[rows, lanes]), head_mask(64).astype(BF)], axis=1
            ),
            1,
            0,
        )
        attended[rows, lanes] = (sums[:, :128] / sums[:, 128:]).astype(BF)
        log_total = jnp.where(first, highest[0], highest[1]) + jnp.log(sums[:, 128:])
        log_held[rows, lanes] = in_terms(log_total)

    first_norm((0, 1, 2, 3), turn)
    for batch in range(2):
        send_tokens(batch).wait_recv()
        if batch == 1:
            for seq in range(4):
                send_cot(seq).start()
        first_norm((2 * batch, 2 * batch + 1), 1 - turn)

        def forward_step(index, carry, batch=batch):
            for pair in range(4):
                forward_heads(2 * batch + index // 2, (index % 2) * 4 + pair)
            return carry

        lax.fori_loop(0, 4, forward_step, 0)
        if batch == 0:
            load_weight(0).wait()
        rows = slice(batch * 256, (batch + 1) * 256)
        hidden[rows, :] = hidden[rows, :] + mm(attended[rows, :], weight[0], 1, 0)

        def second_step(m, carry, batch=batch):
            rows = pl.ds(pl.multiple_of(batch * 256 + m * 32, 32), 32)
            normed[rows, :] = norm(hidden[rows, :], row_of(gain_two), row_of(shift_two))
            return carry

        lax.fori_loop(0, 8, second_step, 0)
    spill_normed = load(7, grad_attn, normed_one_out)
    spill_hidden = load(12, hidden, hidden_one_out)
    spill_normed.start()
    spill_hidden.start()
    load_weight(2).start()
    pump("start")

    def up_tile(tile):
        columns = slice(tile * 1024, (tile + 1) * 1024)
        bias = row_of(b_up)

        def step(m, carry):
            for half in range(2):
                rows = pl.ds(pl.multiple_of(m * 256 + half * 128, 128), 128)
                u = mm(normed[rows, :], weight[(tile + 1) % 2], 1, 0) + bias[:, columns]
                square = u * u
                bend = jnp.tanh(u * (GELU_A + (GELU_A * GELU_B) * square))
                side = 0.5 * (1.0 + bend)
                wide_a[rows, columns] = (u * side).astype(BF)
                slope = side + (0.5 * u) * (1.0 - bend * bend) * (
                    GELU_A + (3.0 * GELU_A * GELU_B) * square
                )
                wide_g[rows, columns] = slope.astype(BF)
            return carry

        lax.fori_loop(0, 2, step, 0)

    def down_unit(unit):
        def step(m, carry):
            rows = pl.ds(pl.multiple_of(m * 512, 512), 512)
            value = mm(inc[:, rows], wide_a[:, unit * 1024 : (unit + 1) * 1024], 0, 0)
            for q in range(4):
                at = q * 128
                place_block(
                    value[at : at + 64], value[at + 64 : at + 128], unit, q % 2, q // 2, m
                )
            return carry

        lax.fori_loop(0, 2, step, 0)

    for part in range(4):
        load_weight(1 + part).wait()
        up_tile(part)
        load_weight(part + 3).start()
        pump("up%d" % part)
        if part == 0:
            for seq in range(4):
                load_cot(seq).wait()
                send_cot(seq).wait_recv()
        down_unit(UNIT_DOWN + part)
        pump("down%d" % part)

    for tile in range(4):
        load_weight(5 + tile).wait()
        columns = slice(tile * 1024, (tile + 1) * 1024)

        for part in range(2):
            at = tile * 1024 + part * 512
            grad = mm(inc[...], weight[(tile + 1) % 2, part * 512 : (part + 1) * 512, :], 1, 1)
            grad = (grad * wide_g[:, at : at + 512].astype(F32)).astype(BF)
            wide_g[:, at : at + 512] = grad
            sums = jnp.sum(grad.astype(F32), axis=0, keepdims=True)
            for row in range(4):
                message[2 * tile + part, 16 + row : 17 + row, :] = sums[
                    :, row * 128 : (row + 1) * 128
                ]
        load_weight(tile + 7).start()
        pump("gu%d" % tile)

    wait_sent(range(0, 4))

    def up_step(p, carry):
        columns = pl.ds(pl.multiple_of(p * 512, 512), 512)
        value = mm(wide_g[:, columns], normed[...], 0, 0)
        for j in range(4):
            low = value[j * 64 : (j + 1) * 64]
            high_rows = value[256 + j * 64 : 256 + (j + 1) * 64]
            place_block(low, high_rows, UNIT_UP + j, p % 2, (p // 2) % 2, p // 4)
        return carry

    for part in range(4):
        lax.fori_loop(2 * part, 2 * part + 2, up_step, 0)
        pump("gup%d" % part)

    for tile in range(9, 13):
        load_weight(tile).wait()
        columns = slice((tile - 9) * 1024, (tile - 8) * 1024)

        def norm_step(m, carry, tile=tile, columns=columns):
            rows = pl.ds(pl.multiple_of(m * 256, 256), 256)
            add = mm(wide_g[rows, columns], weight[tile % 2], 1, 1)
            total[rows, :] = add if tile == 9 else total[rows, :] + add
            return carry

        lax.fori_loop(0, 2, norm_step, 0)
        load_weight(tile + 2).start()
        pump("gn%d" % (tile - 9))

    spill_normed.wait()
    spill_hidden.wait()

    def norm_back(h, gain, rows):
        center = h - jnp.mean(h, axis=1, keepdims=True)
        scale = lax.rsqrt(jnp.mean(center * center, axis=1, keepdims=True) + 1e-05)
        xh = center * scale
        q = total[rows, :]
        e = q * gain
        grad = (
            e - jnp.mean(e, axis=1, keepdims=True) - xh * jnp.mean(e * xh, axis=1, keepdims=True)
        ) * scale
        return (
            grad,
            jnp.sum(q * xh, axis=0, keepdims=True),
            jnp.sum(q, axis=0, keepdims=True),
        )

    def norm_two_step(m, carry):
        rows = pl.ds(pl.multiple_of(m * 32, 32), 32)
        grad, gain_sum, shift_sum = norm_back(hidden[rows, :], row_of(gain_two), rows)
        cot = inc[rows, :].astype(F32)
        grad = cot + grad
        hidden[rows, :] = grad
        grad_attn[rows, :] = grad.astype(BF)
        return (
            carry[0] + gain_sum,
            carry[1] + shift_sum,
            carry[2] + jnp.sum(cot, axis=0, keepdims=True),
        )

    none = jnp.zeros((1, 1024), F32)
    gain_sum, shift_sum, down_sum = lax.fori_loop(0, 16, norm_two_step, (none, none, none))
    vec_rows[6:7, :] = gain_sum
    vec_rows[7:8, :] = shift_sum
    vec_rows[8:9, :] = down_sum
    pump("ln2")

    wait_sent(range(4, 5))

    def out_step(m, carry):
        rows = pl.ds(pl.multiple_of(m * 512, 512), 512)
        value = mm(grad_attn[:, rows], attended[...], 0, 0)
        for q in range(4):
            at = q * 128
            place_block(
                value[at : at + 64], value[at + 64 : at + 128], UNIT_OUT, q % 2, q // 2, m
            )
        return carry

    lax.fori_loop(0, 2, out_step, 0)
    pump("out")
    load_weight(13).wait()

    def mixed_back(m, carry):
        rows = pl.ds(pl.multiple_of(m * 256, 256), 256)
        normed[rows, :] = mm(grad_attn[rows, :], weight[1], 1, 1).astype(BF)
        return carry

    lax.fori_loop(0, 2, mixed_back, 0)
    load_weight(15).start()
    fill_normed = load(7, normed_one_out, grad_attn)
    fill_normed.start()
    pump("mb")


    def heads(seq, pair):
        rows = pl.ds(pl.multiple_of(seq * 128, 128), 128)

        def lanes(base):
            return pl.ds(pl.multiple_of(base + pair * 128, 128), 128)

        first = lane_index(128) < 64
        minus = (-head_mask(3)).astype(BF)
        both = jnp.where(
            (lax.broadcasted_iota(jnp.int32, (256, 128), 0) % 128) // 64 == lane_index(256) // 64,
            1.0,
            0.0,
        ).astype(BF)
        q = q_held[rows, lanes(0)]
        k_two = two_heads(k_held[rows, lanes(0)])
        v_two = two_heads(v_held[rows, lanes(0)])
        grad_out = normed[rows, lanes(0)]
        product_rows = grad_out.astype(F32) * attended[rows, lanes(0)].astype(F32)
        head_part = product_rows.astype(BF)
        tail_part = (product_rows - head_part.astype(F32)).astype(BF)
        inner = mm(jnp.concatenate([head_part, tail_part], axis=1), both, 1, 0)
        scores = mm(
            jnp.concatenate([q, log_held[rows, lanes(0)]], axis=1),
            jnp.concatenate([k_two, minus], axis=1),
            1,
            1,
        )
        grad_probs = mm(
            jnp.concatenate([grad_out, in_terms(inner)], axis=1),
            jnp.concatenate([v_two, minus], axis=1),
            1,
            1,
        )
        soft = jnp.exp(scores)
        grad_scores = (soft * grad_probs).astype(BF)
        grad_q = mm(grad_scores, k_two, 1, 0) * 0.125
        grad_k = mm(grad_scores, q, 0, 0)
        grad_v = mm(soft.astype(BF), grad_out, 0, 0)
        grad_k = jnp.where(first, grad_k[:128], grad_k[128:])
        grad_v = jnp.where(first, grad_v[:128], grad_v[128:])

        def unturn(value):
            return value * cosine[...] - rotated_partner(value) * sine[...]

        wide_g[rows, lanes(0)] = unturn(grad_q).astype(BF)
        wide_g[rows, lanes(1024)] = unturn(grad_k).astype(BF)
        wide_g[rows, lanes(2048)] = grad_v.astype(BF)

    def heads_step(index, carry):
        for pair in range(4):
            heads(index // 2, (index % 2) * 4 + pair)
        return carry

    for part in range(4):
        lax.fori_loop(2 * part, 2 * part + 2, heads_step, 0)
        pump("attn%d" % part)

    fill_normed.wait()
    wait_sent(range(5, 8))

    def qkv_step(p, carry):
        columns = pl.ds(pl.multiple_of(p * 384, 128), 384)
        value = mm(wide_g[:, columns], grad_attn[...], 0, 0)
        for j in range(3):
            low = value[j * 64 : (j + 1) * 64]
            high_rows = value[192 + j * 64 : 192 + (j + 1) * 64]
            place_block(low, high_rows, UNIT_QKV + j, p % 2, (p // 2) % 2, p // 4)
        return carry

    lax.fori_loop(0, 4, qkv_step, 0)
    pump("qkv0")
    lax.fori_loop(4, 8, qkv_step, 0)
    pump("qkv1")

    for tile in range(14, 17):
        load_weight(tile).wait()
        columns = slice((tile - 14) * 1024, (tile - 13) * 1024)

        def first_step(m, carry, tile=tile, columns=columns):
            rows = pl.ds(pl.multiple_of(m * 256, 256), 256)
            add = mm(wide_g[rows, columns], weight[tile % 2], 1, 1)
            total[rows, :] = add if tile == 14 else total[rows, :] + add
            return carry

        lax.fori_loop(0, 2, first_step, 0)
        load_weight(tile + 2).start()
        pump("gf%d" % (tile - 14))
    gain_sum, shift_sum = none, none
    for seq in range(4):

        def norm_one_step(m, carry, seq=seq):
            rows = pl.ds(pl.multiple_of(seq * 128 + m * 32, 32), 32)
            inner = pl.ds(pl.multiple_of(m * 32, 32), 32)
            value = tokens[seq, inner, :].astype(F32) + time_embed[seq : seq + 1, :]
            grad, gain_add, shift_add = norm_back(value, row_of(gain_one), rows)
            grad = grad + hidden[rows, :]
            inc[rows, :] = grad.astype(BF)
            return (
                carry[0] + gain_add,
                carry[1] + shift_add,
                carry[2] + jnp.sum(grad, axis=0, keepdims=True),
            )

        gain_sum, shift_sum, embed_sum = lax.fori_loop(
            0, 4, norm_one_step, (gain_sum, shift_sum, none)
        )
        vec_rows[seq : seq + 1, :] = embed_sum
    vec_rows[4:5, :] = gain_sum
    vec_rows[5:6, :] = shift_sum
    fill_hidden = load(12, hidden_one_out, hidden)
    fill_hidden.start()
    for pair in range(8):
        message[pair, 0:16, :] = vec_rows[:, pair * 128 : (pair + 1) * 128]

    def small_copy(other):
        return remote(
            message.at[other // 4],
            small_recv.at[me],
            small_ssem.at[other],
            small_rsem.at[me],
            (other // 2, other % 2),
        )

    def small_start(step, carry):
        small_copy(lax.rem(me + step, devices)).start()
        return carry

    lax.fori_loop(1, devices, small_start, 0)
    small_recv[me] = message[place // 2]
    pump("rows")
    fill_hidden.wait()
    for tile in range(4):
        load_weight(17 + tile).wait()
        columns = slice(tile * 1024, (tile + 1) * 1024)

        def mixed_step(m, carry, tile=tile, columns=columns):
            rows = pl.ds(pl.multiple_of(m * 256, 256), 256)
            add = mm(wide_a[rows, columns], weight[(tile + 1) % 2], 1, 0)
            if tile == 0:
                total[rows, :] = hidden[rows, :] + row_of(b_down) + add
            elif tile < 3:
                total[rows, :] = total[rows, :] + add
            else:
                attended[rows, :] = (total[rows, :] + add).astype(BF)
            return carry

        lax.fori_loop(0, 2, mixed_step, 0)
        if tile < 2:
            load_weight(19 + tile).start()
        pump("mx%d" % tile)
    pump("small")

    def small_wait(step, carry):
        source = lax.rem(me + step, devices)
        pltpu.make_async_remote_copy(
            src_ref=message.at[0],
            dst_ref=small_recv.at[source],
            send_sem=small_ssem.at[source],
            recv_sem=small_rsem.at[source],
            device_id=(source // 2, source % 2),
            device_id_type=MESH_ID,
        ).wait()
        return carry

    lax.fori_loop(1, devices, small_wait, 0)

    def spread(source, carry):
        for row in range(4):
            at = 4 * source + row
            embeds[pl.ds(at, 1), :] = small_recv[source, row : row + 1, :]
            tables[0, pl.ds(at, 1), :] = small_recv[source, 20 + row : 21 + row, :]
            tables[1, pl.ds(at, 1), :] = small_recv[source, 24 + row : 25 + row, :]
        return carry + small_recv[source, 0:24, :]

    sums = lax.fori_loop(0, devices, spread, jnp.zeros((24, 128), F32))
    rest, terms = embeds[...], []
    for _ in range(3):
        terms.append(rest.astype(BF))
        rest = rest - terms[-1].astype(F32)

    def own_lanes(value):
        return jnp.where(core == 0, value, pltpu.roll(value, 64, 1))

    for part in range(2):
        turned = tables[part].astype(BF)
        value = sum(mm(turned, term, 0, 0) for term in terms)
        small_out[part * 128 : (part + 1) * 128, :] = own_lanes(value)
    small_out[256:280, :] = own_lanes(sums)
    wide = jnp.where(core == 0, sums[16:18], sums[18:20])
    small_out[280:282, :] = wide
    pump("end")

    for part in range(2):
        for seq in range(4):
            for copy in row_copies(part, seq):
                copy.wait()
    wait_sent(range(8, 12))
    for batch in range(2):
        send_tokens(batch).wait_send()
    for seq in range(4):
        send_cot(seq).wait_send()
    for chain in range(2 * UNITS):
        one_copy(chain).wait_send()
        two_copy(chain).wait_send()
        for step in (1, 2, 3) if ORDERS[chain] in "xy" else (1, 2):
            three_copy(chain, step).wait_send()
        if ORDERS[chain] in "xy":
            gather_copy(chain).wait_send()


LAST_STEPS = 16
WINDOW = 0.14
BIAS = {"one": 0, "two": 0, "three": -12, "last_x": -12, "swap": 2, "gather": 8}
ROWS_RANK = (-10, 100)
LENGTHS = {
    "start": 25.0,
    "up": 2.5,
    "down": 1.9,
    "gu": 2.1,
    "mx": 1.8,
    "gup": 1.5,
    "gn": 1.9,
    "ln": 3.0,
    "out": 1.9,
    "mb": 2.0,
    "attn": 3.8,
    "qkv": 2.8,
    "gf": 1.9,
    "rows": 6.0,
}
PIECES = (
    ("start", ()),
    ("up0", ()),
    ("down0", (0,)),
    ("up1", ()),
    ("down1", (1,)),
    ("up2", ()),
    ("down2", (2,)),
    ("up3", ()),
    ("down3", (3,)),
    ("gu0", ()),
    ("gu1", ()),
    ("gu2", ()),
    ("gu3", ()),
    ("gup0", ()),
    ("gup1", ()),
    ("gup2", ()),
    ("gup3", (4, 5, 6, 7)),
    ("gn0", ()),
    ("gn1", ()),
    ("gn2", ()),
    ("gn3", ()),
    ("ln2", ()),
    ("out", (8,)),
    ("mb", ()),
    ("attn0", ()),
    ("attn1", ()),
    ("attn2", ()),
    ("attn3", ()),
    ("qkv0", ()),
    ("qkv1", (9, 10, 11)),
    ("gf0", ()),
    ("gf1", ()),
    ("gf2", ()),
    ("rows", ()),
    ("mx0", ()),
    ("mx1", ()),
    ("mx2", ()),
    ("mx3", ()),
)
CHAINS = {
    "x": ("one", "two", "three", "gather"),
    "y": ("one", "two", "three", "gather"),
    "z": ("one", "two", "last_x", "swap"),
    "w": ("one", "two", "last_x", "swap"),
}
COSTS = {"core": 0.5, "one": 0.2, "two": 0.15, "three": 0.25, "last_x": 0.15, "swap": 0.15, "gather": 0.05, "rows": 0.0}
FIRST = {"x": "x", "y": "y", "z": "a", "w": "x"}
SECOND = {"x": "y", "y": "x", "z": "b", "w": "a"}


def transfer(stage, kind):
    if stage == "one":
        return FIRST[kind], 0.262
    if stage == "two":
        return SECOND[kind], 0.262 if kind == "z" else 0.131
    if stage == "three":
        return "b", 0.131
    if stage == "last_x" and kind == "w":
        return "b", 0.131
    if stage in ("last_x", "swap"):
        return ("x" if stage == "last_x" else "y"), 0.0655
    return "y", 0.0328


def schedule(orders):
    rate, lag = 0.086 / 2, 1.4
    flying = {axis: [] for axis in "xyab"}
    queues = {axis: [] for axis in "xyab"}
    arrived, order = [], []
    now, clock = 0.0, 0.0
    core = []

    def advance(until):
        nonlocal now
        while now < until:
            step = until - now
            for fly in flying.values():
                if fly:
                    step = min(step, min(f[0] for f in fly) * len(fly) / rate)
            now += step
            for axis, fly in flying.items():
                if fly:
                    part = step * rate / len(fly)
                    for f in fly:
                        f[0] -= part
                    for f in [f for f in fly if f[0] < 1e-9]:
                        fly.remove(f)
                        if f[1] is None:
                            continue
                        arrived.append((now + lag, f[1]))
            if step <= 0:
                now = until

    def issue():
        for axis in "baxy":
            queue = queues[axis]
            while queue and sum(f[0] for f in flying[axis] if f[1] is not None) < WINDOW:
                queue.sort()
                _, key, size = queue.pop(0)
                flying[axis].append([size, key, clock])
                if axis == "b":
                    flying["a"].append([size * (0.75 if key[0] == "three" else 0.5), None, clock])
                order.append(("start",) + key)

    def ready(stage, chain):
        axis, size = transfer(stage, orders[chain])
        queues[axis].append((chain + BIAS[stage], (stage, chain), size))

    def take(when, key):
        nonlocal clock
        clock = max(clock, when)
        advance(clock)
        stage, chain = key
        if stage == "rows":
            issue()
            return
        order.append(("add",) + key)
        clock += COSTS[stage]
        advance(clock)
        if stage == "core":
            ready("one", 2 * chain)
            ready("one", 2 * chain + 1)
        else:
            names = CHAINS[orders[chain]]
            if stage != names[-1]:
                ready(names[names.index(stage) + 1], chain)
        issue()

    def due():
        while True:
            arrived.sort()
            if not arrived or arrived[0][0] > clock:
                return
            take(*arrived.pop(0))

    for label, units in PIECES:
        clock += LENGTHS[label.rstrip("0123456789")]
        advance(clock)
        for unit in units:
            order.append(("start", "core", unit))
            arrived.append((clock + 2.3 + 0.3 * units.index(unit), ("core", unit)))
        if label == "mx3":
            queues["y"].append((ROWS_RANK[0], ("rows", 0), 0.524))
        if label == "rows":
            for seq in range(4):
                queues["y"].append((ROWS_RANK[1], ("rows", 1 + seq), 0.131))
        issue()
        due()
        order.append(("mark", label, 0))
    while arrived or any(flying.values()):
        if arrived:
            arrived.sort()
            if arrived[0][0] <= now or not any(flying.values()):
                take(*arrived.pop(0))
                continue
        advance(now + 0.1)
    order.insert(len(order) - LAST_STEPS, ("mark", "small", 0))
    order.append(("mark", "end", 0))
    return order


def layer_call(operands, constants, times):
    vmem = pl.BlockSpec(memory_space=pltpu.VMEM)
    hbm = pl.BlockSpec(memory_space=pl.ANY)
    dma = pltpu.SemaphoreType.DMA
    chains = 2 * UNITS
    return pl.pallas_call(
        layer_kernel,
        name="layer",
        out_shape=(
            jax.ShapeDtypeStruct((8, 64, 1024), BF),
            jax.ShapeDtypeStruct((8, 64, 1024), BF),
            jax.ShapeDtypeStruct((UNITS, 2, 64, 512), BF),
            jax.ShapeDtypeStruct((288, 128), F32),
            jax.ShapeDtypeStruct((512, 1024), BF),
            jax.ShapeDtypeStruct((512, 1024), F32),
        ),
        in_specs=[hbm] * 6 + [vmem] * 10 + [pl.BlockSpec(memory_space=pltpu.SMEM)],
        out_specs=(hbm, hbm, vmem, vmem, hbm, hbm),
        scratch_shapes=[
            pltpu.VMEM((2 * UNITS + 8, 2, 2, 2, 64, 512), BF),
            pltpu.VMEM((4, 2, 2, 2, 2, 64, 512), BF),
            pltpu.VMEM((UNITS, 2, 2, 2, 64, 512), BF),
            pltpu.VMEM((UNITS, 2, 2, 64, 512), BF),
            pltpu.VMEM((UNITS, 4, 64, 512), BF),
            pltpu.VMEM((2, 1024, 1024), BF),
            pltpu.VMEM((512, 4096), BF),
            pltpu.VMEM((512, 4096), BF),
            pltpu.VMEM((512, 1024), BF),
            pltpu.VMEM((512, 1024), BF),
            pltpu.VMEM((512, 1024), BF),
            pltpu.VMEM((512, 1024), BF),
            pltpu.VMEM((4, 128, 1024), BF),
            pltpu.VMEM((512, 1024), BF),
            pltpu.VMEM((512, 1024), BF),
            pltpu.VMEM((512, 1024), F32),
            pltpu.VMEM((512, 1024), F32),
            pltpu.VMEM((512, 1024), BF),
            pltpu.VMEM((512, 1024), BF),
            pltpu.VMEM((8, 32, 128), F32),
            pltpu.VMEM((32, 32, 128), F32),
            pltpu.VMEM((16, 1024), F32),
            pltpu.VMEM((128, 128), F32),
            pltpu.VMEM((2, 128, 128), F32),
            pltpu.VMEM((8, 1024), F32),
            dma((21,)),
            dma((2,)),
            dma((2,)),
            dma((2,)),
            dma((4,)),
            dma((4,)),
            dma((4,)),
            dma((4,)),
            pltpu.SemaphoreType.REGULAR((4,)),
            dma((chains,)),
            dma((chains,)),
            dma((chains,)),
            dma((chains,)),
            dma((3 * chains,)),
            dma((3 * chains,)),
            dma((chains,)),
            dma((chains,)),
            dma((32,)),
            dma((32,)),
            dma((8,)),
            dma((8,)),
        ],
        compiler_params=pltpu.CompilerParams(
            collective_id=0, has_side_effects=True, vmem_limit_bytes=VMEM_LIMIT
        ),
    )(*operands, *constants, times)


def finish_kernel(
    mixed_in,
    tokens_in,
    shares,
    small,
    mixed_out,
    tokens_out,
    down_out,
    up_out,
    w_out_out,
    qkv_out,
    proj_out,
    time_bias,
    gain_one,
    shift_one,
    gain_two,
    shift_two,
    b_down,
    b_up,
    mixed_held,
    tokens_held,
    sem,
):
    copies = []
    for index, (source, held, target) in enumerate(
        ((mixed_in, mixed_held, mixed_out), (tokens_in, tokens_held, tokens_out))
    ):
        inward = pltpu.make_async_copy(source, held, sem.at[index])
        outward = pltpu.make_async_copy(held, target, sem.at[2 + index])
        inward.start()
        copies.append((inward, outward))

    def share(unit, h):
        return shares[unit, h].astype(F32)

    for h in range(2):
        columns = slice(h * 512, (h + 1) * 512)
        for j in range(4):
            down_out[:, j * 1024 + h * 512 : j * 1024 + (h + 1) * 512] = share(UNIT_DOWN + j, h)
        for j in range(3):
            qkv_out[j * 64 : (j + 1) * 64, columns] = share(UNIT_QKV + j, h)
        w_out_out[:, columns] = share(UNIT_OUT, h)
        for j in range(0, 4, 2):
            both = jnp.concatenate([share(UNIT_UP + j, h), share(UNIT_UP + j + 1, h)], axis=0)
            up_out[columns, j * 64 : (j + 2) * 64] = both.T
    for inward, outward in copies:
        inward.wait()
        outward.start()
    for part in range(2):
        proj_out[:, part * 128 : (part + 1) * 128] = small[part * 128 : (part + 1) * 128, :].T[:64]
    rows = small[256:288, :]
    time_bias[...] = jnp.sum(rows[0:4], axis=0)[:64]
    for index, target in enumerate((gain_one, shift_one, gain_two, shift_two, b_down)):
        target[...] = rows[4 + index, :64]
    for index in range(2):
        b_up[index * 128 : (index + 1) * 128] = rows[24 + index, :]
    for _, outward in copies:
        outward.wait()


def finish_call(mixed, tokens, shares, small):
    vmem = pl.BlockSpec(memory_space=pltpu.VMEM)
    hbm = pl.BlockSpec(memory_space=pl.ANY)
    like = jax.ShapeDtypeStruct
    vector = like((64,), F32)
    return pl.pallas_call(
        finish_kernel,
        name="finish",
        out_shape=(
            like((8, 64, 1024), BF),
            like((8, 64, 1024), BF),
            like((64, 4096), F32),
            like((1024, 256), F32),
            like((64, 1024), F32),
            like((192, 1024), F32),
            like((64, 256), F32),
            vector,
            vector,
            vector,
            vector,
            vector,
            vector,
            like((256,), F32),
        ),
        in_specs=[hbm, hbm, vmem, vmem],
        out_specs=(hbm, hbm) + (vmem,) * 12,
        scratch_shapes=[
            pltpu.VMEM((8, 64, 1024), BF),
            pltpu.VMEM((8, 64, 1024), BF),
            pltpu.SemaphoreType.DMA((4,)),
        ],
        compiler_params=pltpu.CompilerParams(vmem_limit_bytes=VMEM_LIMIT),
    )(mixed, tokens, shares, small)


def body(
    tokens,
    noise_times,
    time_proj,
    time_bias,
    gain_one,
    shift_one,
    w_qkv,
    w_out,
    gain_two,
    shift_two,
    w_up,
    b_up,
    w_down,
    b_down,
    cotangent,
):
    seq_ways, tok_ways = lax.axis_size("seq"), lax.axis_size("tok")
    model_width = tokens.shape[-1]
    seq_count, length = tokens.shape[0] // tok_ways, tokens.shape[1] * tok_ways
    row_count = seq_count * length
    all_times = lax.all_gather(noise_times, "seq", tiled=True)
    own_times = lax.dynamic_slice_in_dim(
        noise_times, lax.axis_index("tok") * seq_count, seq_count
    )
    embed_table = noise_table(own_times).astype(jnp.bfloat16)
    time_embed = product(embed_table, time_proj) + time_bias.astype(jnp.float32)
    tokens = gather_sequences(tokens)
    incoming = gather_sequences(cotangent).reshape(row_count, model_width)
    hidden_zero = (tokens.astype(jnp.float32) + time_embed[:, None, :]).reshape(
        row_count, model_width
    )
    normed_one, pull_one = jax.vjp(
        layer_norm, hidden_zero, gain_one.astype(jnp.float32), shift_one.astype(jnp.float32)
    )
    normed_one = normed_one.astype(jnp.bfloat16)
    projected = product(normed_one, w_qkv).astype(jnp.bfloat16)
    received, attended, log_total = attend_items(
        projected.reshape(seq_count, length, 3, 1, model_width)
    )
    attended = attended.reshape(row_count, model_width)
    hidden_one = hidden_zero + product(attended, w_out)
    normed_two, pull_two = jax.vjp(
        layer_norm, hidden_one, gain_two.astype(jnp.float32), shift_two.astype(jnp.float32)
    )
    normed_two = normed_two.astype(jnp.bfloat16)
    upward = product(normed_two, w_up) + b_up.astype(jnp.float32)
    active, pull_gelu = jax.vjp(jax.nn.gelu, upward)
    active = active.astype(jnp.bfloat16)
    out_wdown = scatter_sum(contract_rows(incoming, active))
    result = hidden_one + (product(active, w_down) + b_down.astype(jnp.float32))
    mixed_out = return_positions(
        result.astype(jnp.bfloat16).reshape(seq_count, length, model_width)
    )
    sum_down = jnp.sum(incoming, axis=0, dtype=jnp.float32)
    grad_active = times_transpose(incoming, w_down)
    (grad_upward,) = pull_gelu(grad_active)
    grad_upward = grad_upward.astype(jnp.bfloat16)
    sum_up = jnp.sum(grad_upward, axis=0, dtype=jnp.float32)
    out_wup = scatter_sum(contract_rows(grad_upward, normed_two))
    grad_norm_two = times_transpose(grad_upward, w_up)
    grad_hidden_two, grad_gain_two, grad_shift_two = pull_two(grad_norm_two)
    grad_hidden_one = incoming.astype(jnp.float32) + grad_hidden_two
    grad_attn = grad_hidden_one.astype(jnp.bfloat16)
    out_wout = scatter_sum(contract_rows(grad_attn, attended))
    grad_mixed = times_transpose(grad_attn, w_out).astype(jnp.bfloat16)
    grad_parts = attention_grad(
        received, log_total, grad_mixed.reshape(seq_count, length, 1, model_width)
    ).reshape(row_count, 3 * model_width)
    out_wqkv = scatter_sum(contract_rows(grad_parts, normed_one))
    grad_norm_one = times_transpose(grad_parts, w_qkv)
    grad_hidden_zero, grad_gain_one, grad_shift_one = pull_one(grad_norm_one)
    grad_total = grad_hidden_one + grad_hidden_zero
    grad_tokens = return_positions(
        grad_total.astype(jnp.bfloat16).reshape(seq_count, length, model_width)
    )
    grad_embed = jnp.sum(grad_total.reshape(seq_count, length, model_width), axis=1)
    wide = sum_up.shape[0] // model_width
    small = jnp.concatenate(
        [
            grad_embed.reshape(seq_count, seq_ways, -1).swapaxes(0, 1),
            grad_gain_one.reshape(seq_ways, 1, -1),
            grad_shift_one.reshape(seq_ways, 1, -1),
            grad_gain_two.reshape(seq_ways, 1, -1),
            grad_shift_two.reshape(seq_ways, 1, -1),
            sum_down.reshape(seq_ways, 1, -1),
            sum_up.reshape(seq_ways, wide, -1),
        ],
        axis=1,
    )
    small = lax.all_to_all(small, "seq", split_axis=0, concat_axis=0, tiled=True)
    small = lax.all_gather(small, "tok", axis=1)
    embeds = small[:, :, :seq_count].reshape(-1, small.shape[-1])
    out_proj = jnp.dot(
        noise_table(all_times).astype(jnp.bfloat16).astype(jnp.float32).T,
        embeds,
        precision=lax.Precision.HIGHEST,
    )
    out_bias = jnp.sum(embeds, axis=0)
    sums = jnp.sum(small[:, :, seq_count:], axis=(0, 1))
    return (
        mixed_out,
        grad_tokens,
        out_proj,
        out_bias,
        sums[0],
        sums[1],
        out_wqkv,
        out_wout,
        sums[2],
        sums[3],
        out_wup,
        sums[5:].reshape(-1),
        out_wdown,
        sums[4],
    )


def rotary_lanes():
    halves = HD // 2
    frequency = np.exp(-math.log(10000.0) * np.arange(halves, dtype=np.float32) / halves)
    angles = np.arange(128, dtype=np.float32)[:, None] * frequency.astype(np.float32)[None, :]
    cosine, sine = np.cos(angles), np.sin(angles)
    return (
        jnp.asarray(np.tile(cosine, (1, 4)), jnp.float32),
        jnp.asarray(np.concatenate([-sine, sine] * 2, axis=1), jnp.float32),
    )


def fast_body(
    tokens,
    noise_times,
    time_proj,
    time_bias,
    gain_one,
    shift_one,
    w_qkv,
    w_out,
    gain_two,
    shift_two,
    w_up,
    b_up,
    w_down,
    b_down,
    cotangent,
):
    cosine, sine = rotary_lanes()
    mixed_out, grad_tokens, shares, small, _, _ = layer_call(
        (tokens, cotangent, w_qkv, w_out, w_up, w_down),
        (
            time_proj,
            time_bias,
            gain_one,
            shift_one,
            gain_two,
            shift_two,
            b_up,
            b_down,
            cosine,
            sine,
        ),
        noise_times,
    )
    (
        mixed_out,
        grad_tokens,
        out_wdown,
        out_wup,
        out_wout,
        out_wqkv,
        out_proj,
        out_bias,
        out_gain_one,
        out_shift_one,
        out_gain_two,
        out_shift_two,
        out_bdown,
        out_bup,
    ) = finish_call(mixed_out, grad_tokens, shares, small)
    return (
        mixed_out,
        grad_tokens,
        out_proj.T,
        out_bias,
        out_gain_one,
        out_shift_one,
        out_wqkv.T,
        out_wout.T,
        out_gain_two,
        out_shift_two,
        out_wup,
        out_bup,
        out_wdown.T,
        out_bdown,
    )


def solution(mesh):
    chosen = fast_body if (mesh.shape["seq"], mesh.shape["tok"]) == (16, 2) else body
    in_specs = (
        P("seq", "tok", None),
        P("seq"),
        P(),
        P(),
        P(),
        P(),
        P(),
        P(),
        P(),
        P(),
        P(),
        P(),
        P(),
        P(),
        P("seq", "tok", None),
    )
    out_specs = (
        P("seq", "tok", None),
        P("seq", "tok", None),
        P(None, "seq"),
        P("seq"),
        P("seq"),
        P("seq"),
        P(None, "seq"),
        P(None, "seq"),
        P("seq"),
        P("seq"),
        P(None, "seq"),
        P("seq"),
        P(None, "seq"),
        P("seq"),
    )
    return jax.shard_map(chosen, mesh=mesh, in_specs=in_specs, out_specs=out_specs, check_vma=False)
```

```python
import math

import jax
import jax.numpy as jnp
import numpy as np
from jax import lax
from jax.experimental import pallas as pl
from jax.experimental.pallas import tpu as pltpu
from jax.sharding import PartitionSpec as P

HD = 64
TEMB = 256
VMEM_LIMIT = 64 * 1024 * 1024 - 65536


def layer_norm(hidden, gain_vec, shift_vec):
    center = hidden - jnp.mean(hidden, axis=-1, keepdims=True)
    spread = jnp.mean(center * center, axis=-1, keepdims=True)
    return center * lax.rsqrt(spread + 1e-05) * gain_vec + shift_vec


def noise_table(noise_steps):
    halves = TEMB // 2
    frequency = jnp.exp(-math.log(10000.0) * jnp.arange(halves, dtype=jnp.float32) / halves)
    angles = noise_steps.astype(jnp.float32)[:, None] * frequency[None, :]
    return jnp.concatenate([jnp.sin(angles), jnp.cos(angles)], axis=-1)


def rotary_tables(length):
    halves = HD // 2
    frequency = jnp.exp(-math.log(10000.0) * jnp.arange(halves, dtype=jnp.float32) / halves)
    angles = jnp.arange(length, dtype=jnp.float32)[:, None] * frequency[None, :]
    angles = jnp.concatenate([angles, angles], axis=-1)[:, None, :]
    return (jnp.cos(angles), jnp.sin(angles))


def rotate(values, cosine, sine_tab):
    halves = values.shape[-1] // 2
    turned = jnp.concatenate([-values[..., halves:], values[..., :halves]], axis=-1)
    return values * cosine + turned * sine_tab


def unrotate(gradient, cosine, sine_tab):
    halves = gradient.shape[-1] // 2
    scaled = gradient * sine_tab
    turned = jnp.concatenate([scaled[..., halves:], -scaled[..., :halves]], axis=-1)
    return gradient * cosine + turned


def product(left_side, right_side):
    return jnp.dot(left_side, right_side, preferred_element_type=jnp.float32)


def contract_rows(left_side, right_side):
    return jnp.einsum("ra,rb->ab", left_side, right_side, preferred_element_type=jnp.float32)


def times_transpose(left_side, right_side):
    return jnp.einsum("rb,ab->ra", left_side, right_side, preferred_element_type=jnp.float32)


def split_heads(received):
    batch_size, length = (received.shape[0], received.shape[1])
    local_heads = received.shape[-1] // HD
    split_view = received.reshape(batch_size, length, 3, local_heads, HD)
    cosine, sine_tab = rotary_tables(length)
    queries = rotate(split_view[:, :, 0].astype(jnp.float32), cosine, sine_tab).astype(jnp.bfloat16)
    keys_rot = rotate(split_view[:, :, 1].astype(jnp.float32), cosine, sine_tab).astype(
        jnp.bfloat16
    )
    return (queries, keys_rot, split_view[:, :, 2], cosine, sine_tab)


def attend_items(received):
    batch_size, length = (received.shape[0], received.shape[1])
    scaling = 1.0 / math.sqrt(HD)
    queries, keys_rot, values, cosine, sine_tab = split_heads(received)
    scores = (
        jnp.einsum("gqhd,gkhd->ghqk", queries, keys_rot, preferred_element_type=jnp.float32)
        * scaling
    )
    highest = jnp.max(scores, axis=-1, keepdims=True)
    exponent = jnp.exp(scores - highest)
    totals = jnp.sum(exponent, axis=-1, keepdims=True)
    prob_rows = (exponent / totals).astype(jnp.bfloat16)
    log_total = (highest + jnp.log(totals))[..., 0]
    attended = jnp.einsum("ghqk,gkhd->gqhd", prob_rows, values, preferred_element_type=jnp.float32)
    attended = attended.astype(jnp.bfloat16).reshape(batch_size, length, 1, -1)
    return (received, attended, log_total)


def attention_grad(received, log_total, grad_heads):
    batch_size, length = (received.shape[0], received.shape[1])
    scaling = 1.0 / math.sqrt(HD)
    queries, keys_rot, values, cosine, sine_tab = split_heads(received)
    scores = (
        jnp.einsum("gqhd,gkhd->ghqk", queries, keys_rot, preferred_element_type=jnp.float32)
        * scaling
    )
    prob_rows = jnp.exp(scores - log_total[..., None])
    grad_out = grad_heads.reshape(batch_size, length, values.shape[2], HD)
    grad_probs = jnp.einsum("gqhd,gkhd->ghqk", grad_out, values, preferred_element_type=jnp.float32)
    grad_values = jnp.einsum(
        "ghqk,gqhd->gkhd",
        prob_rows.astype(jnp.bfloat16),
        grad_out,
        preferred_element_type=jnp.float32,
    )
    inner_sum = jnp.sum(prob_rows * grad_probs, axis=-1, keepdims=True)
    grad_scores = (prob_rows * (grad_probs - inner_sum)).astype(jnp.bfloat16)
    grad_queries = (
        jnp.einsum("ghqk,gkhd->gqhd", grad_scores, keys_rot, preferred_element_type=jnp.float32)
        * scaling
    )
    grad_keys = (
        jnp.einsum("ghqk,gqhd->gkhd", grad_scores, queries, preferred_element_type=jnp.float32)
        * scaling
    )
    stacked = jnp.stack(
        [
            unrotate(grad_queries, cosine, sine_tab),
            unrotate(grad_keys, cosine, sine_tab),
            grad_values,
        ],
        axis=2,
    )
    return stacked.astype(jnp.bfloat16).reshape(batch_size, length, 3, 1, -1)


def gather_sequences(values):
    return lax.all_to_all(values, "tok", split_axis=0, concat_axis=1, tiled=True)


def return_positions(values):
    return lax.all_to_all(values, "tok", split_axis=1, concat_axis=0, tiled=True)


def group_scatter(parts, own, size, axis, perm_of):
    total = lax.dynamic_index_in_dim(parts, own, 0, keepdims=False).astype(jnp.float32)
    for shift in range(1, size):
        piece = lax.dynamic_index_in_dim(parts, (own + shift) % size, 0, keepdims=False)
        total = total + lax.ppermute(piece, axis, perm_of(shift)).astype(jnp.float32)
    return total.astype(jnp.bfloat16)


def group_gather(piece, own, size, axis, perm_of):
    held = jnp.zeros((size,) + piece.shape, piece.dtype)
    held = lax.dynamic_update_index_in_dim(held, piece, own, 0)
    for shift in range(1, size):
        other = lax.ppermute(piece, axis, perm_of(shift))
        held = lax.dynamic_update_index_in_dim(held, other, (own - shift) % size, 0)
    return held


def scatter_sum(gradient):
    seq_ways, tok_ways = lax.axis_size("seq"), lax.axis_size("tok")
    outer, middle = 4, seq_ways // 8
    place, turn = lax.axis_index("seq"), lax.axis_index("tok")
    core, mid, out = place % 2, (place // 2) % middle, place // (2 * middle)

    def core_perm(shift):
        return [(i, i ^ 1) for i in range(seq_ways)]

    def mid_perm(shift):
        return [
            (i, (i // (2 * middle)) * 2 * middle + ((i // 2 + shift) % middle) * 2 + i % 2)
            for i in range(seq_ways)
        ]

    def out_perm(shift):
        return [(i, (i + shift * 2 * middle) % seq_ways) for i in range(seq_ways)]

    def tok_perm(shift):
        return [(i, (i + shift) % tok_ways) for i in range(tok_ways)]

    rows, width = gradient.shape[0] // seq_ways, gradient.shape[1]
    parts = gradient.astype(jnp.bfloat16).reshape(outer * middle, 2, rows, width)
    parts = group_scatter(jnp.swapaxes(parts, 0, 1), core, 2, "seq", core_perm)
    parts = parts.reshape(outer, middle, rows, 2, tok_ways, width // (2 * tok_ways))
    first = jnp.transpose(parts[:, :, :, 0], (1, 3, 0, 2, 4))
    second = jnp.transpose(parts[:, :, :, 1], (3, 1, 0, 2, 4))
    first = group_scatter(first, mid, middle, "seq", mid_perm)
    second = group_scatter(second, turn, tok_ways, "tok", tok_perm)
    first = group_scatter(first, turn, tok_ways, "tok", tok_perm)
    second = group_scatter(second, mid, middle, "seq", mid_perm)
    both = jnp.stack([first, second], axis=1)
    both = group_scatter(both, out, outer, "seq", out_perm)
    both = group_gather(both, turn, tok_ways, "tok", tok_perm)
    return jnp.transpose(both, (2, 1, 0, 3)).reshape(rows, width).T.astype(jnp.float32)


MESH_ID = pl.DeviceIdType.MESH
BF = jnp.bfloat16
F32 = jnp.float32
UNITS = 12
UNIT_DOWN, UNIT_UP, UNIT_OUT, UNIT_QKV = 0, 4, 8, 9
ORDERS = "wzywywywwwyzwyyyywwwzwwy"
GELU_A = math.sqrt(2.0 / math.pi)
GELU_B = 0.044715


def mm(left, right, left_dim, right_dim):
    return lax.dot_general(
        left, right, (((left_dim,), (right_dim,)), ((), ())), preferred_element_type=F32
    )


def rotated_partner(values):
    lane = lax.broadcasted_iota(jnp.int32, values.shape, 1)
    return jnp.where(lane % 64 < 32, pltpu.roll(values, 96, 1), pltpu.roll(values, 32, 1))


def lane_index(rows):
    return lax.broadcasted_iota(jnp.int32, (rows, 128), 1)


def two_heads(value):
    first = lane_index(128) < 64
    zero = jnp.zeros_like(value)
    return jnp.concatenate([jnp.where(first, value, zero), jnp.where(first, zero, value)], axis=0)


def head_mask(count):
    lane = lane_index(256)
    row = lax.broadcasted_iota(jnp.int32, (256, 128), 0)
    return jnp.where((lane // 64 == row // 128) & (lane % 64 < count), 1.0, 0.0)


def in_terms(value):
    lane = lane_index(value.shape[0]) % 64
    out, rest = jnp.zeros(value.shape, BF), value
    for index in range(3):
        term = rest.astype(BF)
        rest = rest - term.astype(F32)
        out = jnp.where(lane == index, term, out)
    return out


def layer_kernel(
    tokens_in,
    cotangent_in,
    w_qkv,
    w_out,
    w_up,
    w_down,
    time_proj,
    time_bias,
    gain_one,
    shift_one,
    gain_two,
    shift_two,
    b_up,
    b_down,
    cosine,
    sine,
    noise_times,
    mixed_out,
    tokens_out,
    shares_out,
    small_out,
    normed_one_out,
    hidden_one_out,
    partial,
    core_recv,
    recv_one,
    recv_two,
    recv_three,
    weight,
    wide_a,
    wide_g,
    q_held,
    k_held,
    v_held,
    log_held,
    tokens,
    inc,
    normed,
    hidden,
    total,
    grad_attn,
    attended,
    message,
    small_recv,
    vec_rows,
    embeds,
    tables,
    time_embed,
    load_sem,
    weight_sem,
    token_ssem,
    token_rsem,
    cot_ssem,
    cot_rsem,
    core_ssem,
    core_rsem,
    credit,
    one_ssem,
    one_rsem,
    two_ssem,
    two_rsem,
    three_ssem,
    three_rsem,
    gather_ssem,
    gather_rsem,
    small_ssem,
    small_rsem,
    back_ssem,
    back_rsem,
):
    place, turn = lax.axis_index("seq"), lax.axis_index("tok")
    core, xx, zz = place % 2, (place // 2) % 2, place // 4
    yy = turn
    me = place * 2 + turn
    devices = 32

    def at_seq(z, x, c):
        return ((z * 2 + x) * 2 + c, turn)

    core_peer = at_seq(zz, xx, 1 - core)
    x_peer = at_seq(zz, 1 - xx, core)
    y_peer = (place, 1 - turn)

    def load(index, source, target):
        return pltpu.make_async_copy(source, target, load_sem.at[index])

    def load_weight(tile):
        if tile == 0 or tile == 13:
            source = w_out
        elif tile < 5:
            source = w_up.at[:, pl.ds((tile - 1) * 1024, 1024)]
        elif tile < 9:
            source = w_down.at[pl.ds((tile - 5) * 1024, 1024), :]
        elif tile < 13:
            source = w_up.at[:, pl.ds((tile - 9) * 1024, 1024)]
        elif tile < 17:
            source = w_qkv.at[:, pl.ds((tile - 14) * 1024, 1024)]
        else:
            source = w_down.at[pl.ds((tile - 17) * 1024, 1024), :]
        return pltpu.make_async_copy(source, weight.at[tile % 2], weight_sem.at[tile % 2])

    def row_of(vector):
        return vector[...].astype(F32).reshape(1, vector.shape[0])

    own_half = pl.ds(turn * 64, 64)

    def load_qkv(part):
        index, half = part // 2, part % 2
        columns = pl.ds(index * 1024, 1024)
        target = (wide_a, wide_g)[half]
        return load(
            1 + part, w_qkv.at[pl.ds(half * 512, 512), columns], target.at[:, columns]
        )

    def load_cot(seq):
        return load(
            8 + seq,
            cotangent_in.at[turn * 4 + seq],
            inc.at[pl.ds(seq * 128 + turn * 64, 64)],
        )

    load_tokens = load(0, tokens_in.at[pl.ds(turn * 4, 4)], tokens.at[:, own_half])
    load_tokens.start()
    for part in range(6):
        load_qkv(part).start()
    load_weight(0).start()
    load_weight(1).start()
    for seq in range(4):
        load_cot(seq).start()

    barrier = pltpu.get_barrier_semaphore()

    def greet(step, carry):
        other = lax.rem(me + step, devices)
        pl.semaphore_signal(
            barrier, inc=1, device_id=(other // 2, other % 2), device_id_type=MESH_ID
        )
        return carry

    lax.fori_loop(1, devices, greet, 0)
    message[...] = jnp.zeros_like(message)
    vec_rows[...] = jnp.zeros_like(vec_rows)
    lane = lax.broadcasted_iota(jnp.int32, (1, 128), 1).astype(F32)
    frequency = jnp.exp((-math.log(10000.0) * lane) / 128)
    steps = [jnp.where(turn == 0, noise_times[j], noise_times[4 + j]) for j in range(4)]
    angles = jnp.concatenate([frequency * step.astype(F32) for step in steps] * 2, axis=0)
    sine_rows = jnp.sin(angles).astype(BF)
    cosine_rows = jnp.cos(angles).astype(BF)
    time_embed[...] = (
        mm(jnp.concatenate([sine_rows, cosine_rows], axis=1), time_proj[...], 1, 0)
        + row_of(time_bias)
    )
    for pair in range(8):
        message[pair, 20:24, :] = sine_rows.astype(F32)[0:4]
        message[pair, 24:28, :] = cosine_rows.astype(F32)[0:4]
    pl.semaphore_wait(barrier, devices - 1)

    def remote(source, target, send, recv, device):
        return pltpu.make_async_remote_copy(
            src_ref=source,
            dst_ref=target,
            send_sem=send,
            recv_sem=recv,
            device_id=device,
            device_id_type=MESH_ID,
        )

    parity, high = zz % 2, zz // 2

    def core_copy(unit):
        slot = unit % 4
        return remote(
            partial.at[pl.ds(2 * UNITS + 2 * slot, 2)],
            core_recv.at[slot],
            core_ssem.at[slot],
            core_rsem.at[slot],
            core_peer,
        )

    def half_of(chain):
        return chain // 2, pl.ds(32 * (chain % 2), 32)

    def one_copy(chain):
        unit, rows = half_of(chain)
        if ORDERS[chain] in "xw":
            source, device = partial.at[2 * unit + 1 - xx, :, :, :, rows], x_peer
        elif ORDERS[chain] == "y":
            source, device = partial.at[pl.ds(2 * unit, 2), 1 - yy, :, :, rows], y_peer
        else:
            source = partial.at[pl.ds(2 * unit, 2), :, 1 - parity, :, rows]
            device = at_seq(2 * high + 1 - parity, xx, core)
        target = recv_one.at[unit, :, :, :, rows]
        return remote(source, target, one_ssem.at[chain], one_rsem.at[chain], device)

    def two_copy(chain):
        unit, rows = half_of(chain)
        if ORDERS[chain] == "x":
            source, device = partial.at[2 * unit + xx, 1 - yy, :, :, rows], y_peer
        elif ORDERS[chain] == "y":
            source, device = partial.at[2 * unit + 1 - xx, yy, :, :, rows], x_peer
        elif ORDERS[chain] == "w":
            source = partial.at[2 * unit + xx, :, 1 - parity, :, rows]
            device = at_seq(2 * high + 1 - parity, xx, core)
        else:
            source = partial.at[pl.ds(2 * unit, 2), :, parity, 1 - high, rows]
            device = at_seq(2 * (1 - high) + parity, xx, core)
        target = recv_two.at[unit, :, :, rows]
        return remote(source, target, two_ssem.at[chain], two_rsem.at[chain], device)

    def three_copy(chain, step):
        unit, rows = half_of(chain)
        index = 3 * chain + step - 1
        if ORDERS[chain] in "xy":
            other = (zz + step) % 4
            source = partial.at[2 * unit + xx, yy, other % 2, other // 2, rows]
            target, device = recv_three.at[unit, step - 1, rows], at_seq(other, xx, core)
        elif step == 1 and ORDERS[chain] == "w":
            source = partial.at[2 * unit + xx, :, parity, 1 - high, rows]
            target = recv_three.at[unit, pl.ds(0, 2), rows]
            device = at_seq(2 * (1 - high) + parity, xx, core)
        elif step == 1:
            source = partial.at[2 * unit + 1 - xx, :, parity, high, rows]
            target, device = recv_three.at[unit, pl.ds(0, 2), rows], x_peer
        else:
            source = partial.at[2 * unit + xx, :, parity, high, rows]
            target, device = recv_three.at[unit, pl.ds(2, 2), rows], y_peer
        return remote(source, target, three_ssem.at[index], three_rsem.at[index], device)

    def gather_copy(chain):
        unit, rows = half_of(chain)
        view = shares_out.at[unit, yy, rows]
        return remote(view, view, gather_ssem.at[chain], gather_rsem.at[chain], y_peer)

    def start_core(unit):
        if unit >= 4:
            pl.semaphore_wait(credit.at[unit % 4], 1)
        core_copy(unit).start()

    def add_core(unit):
        core_copy(unit).wait_recv()

        def add(index, carry):
            x, h, p = index // 4, (index // 2) % 2, index % 2
            partial[2 * unit + x, h, p] = (
                partial[2 * unit + x, h, p] + core_recv[unit % 4, x, h, p]
            )
            return carry

        lax.fori_loop(0, 8, add, 0)
        if unit < UNITS - 4:
            pl.semaphore_signal(
                credit.at[unit % 4], inc=1, device_id=core_peer, device_id_type=MESH_ID
            )

    def add_one(chain):
        one_copy(chain).wait_recv()
        unit, rows = half_of(chain)
        for a in range(2):
            for b in range(2):
                for c in range(2):
                    if ORDERS[chain] in "xw":
                        at = (2 * unit + xx, a, b, c, rows)
                    elif ORDERS[chain] == "y":
                        at = (2 * unit + a, yy, b, c, rows)
                    else:
                        at = (2 * unit + a, b, parity, c, rows)
                    partial[at] = partial[at] + recv_one[unit, a, b, c, rows]

    def add_two(chain):
        two_copy(chain).wait_recv()
        unit, rows = half_of(chain)
        for a in range(2):
            for b in range(2):
                if ORDERS[chain] == "z":
                    at = (2 * unit + a, b, parity, high, rows)
                elif ORDERS[chain] == "w":
                    at = (2 * unit + xx, a, parity, b, rows)
                else:
                    at = (2 * unit + xx, yy, a, b, rows)
                partial[at] = partial[at] + recv_two[unit, a, b, rows]

    def add_three(chain):
        unit, rows = half_of(chain)
        value = partial[2 * unit + xx, yy, parity, high, rows].astype(F32)
        for step in (1, 2, 3):
            three_copy(chain, step).wait_recv()
        for step in (1, 2, 3):
            value = value + recv_three[unit, step - 1, rows].astype(F32)
        shares_out[unit, yy, rows] = value.astype(BF)

    def add_last_x(chain):
        three_copy(chain, 1).wait_recv()
        unit, rows = half_of(chain)
        for h in range(2):
            at = (2 * unit + xx, h, parity, high, rows)
            partial[at] = partial[at] + recv_three[unit, h, rows]

    def add_swap(chain):
        three_copy(chain, 2).wait_recv()
        unit, rows = half_of(chain)
        for h in range(2):
            value = partial[2 * unit + xx, h, parity, high, rows].astype(F32)
            value = value + recv_three[unit, 2 + h, rows].astype(F32)
            shares_out[unit, h, rows] = value.astype(BF)

    def start_three(chain):
        for step in (2, 1, 3):
            three_copy(chain, step).start()

    actions = {
        "core": (start_core, add_core),
        "one": (lambda unit: one_copy(unit).start(), add_one),
        "two": (lambda unit: two_copy(unit).start(), add_two),
        "three": (start_three, add_three),
        "last_x": (lambda unit: three_copy(unit, 1).start(), add_last_x),
        "swap": (lambda unit: three_copy(unit, 2).start(), add_swap),
        "gather": (
            lambda unit: gather_copy(unit).start(),
            lambda unit: gather_copy(unit).wait_recv(),
        ),
    }
    def row_copies(part, seq):
        source, target = (attended, mixed_out) if part == 0 else (inc, tokens_out)
        views = [source.at[pl.ds(seq * 128 + y * 64, 64)] for y in (yy, 1 - yy)]
        index, at = 4 * part + seq, yy * 4 + seq
        local = pltpu.make_async_copy(views[0], target.at[at], load_sem.at[13 + index])
        away = remote(views[1], target.at[at], back_ssem.at[index], back_rsem.at[index], y_peer)
        return local, away

    def start_rows(part):
        for seq in range(4) if part == 0 else (part - 1,):
            for copy in row_copies(min(part, 1), seq):
                copy.start()

    plan = schedule(ORDERS)
    cursor = [0]

    def pump(label):
        while True:
            kind, stage, unit = plan[cursor[0]]
            cursor[0] += 1
            if kind == "mark":
                assert stage == label
                return
            if stage == "rows":
                start_rows(unit)
            else:
                actions[stage][0 if kind == "start" else 1](unit)

    def wait_sent(units):
        for unit in units:
            core_copy(unit).wait_send()

    def place_block(low, high_rows, unit, x, p, q):
        own, away = 2 * unit + x, 2 * UNITS + 2 * (unit % 4) + x
        for value, at in (
            (low, own * (1 - core) + away * core),
            (high_rows, away * (1 - core) + own * core),
        ):
            value = value.astype(BF)
            for h in range(2):
                partial[at, h, p, q] = value[:, h * 512 : (h + 1) * 512]

    def send_tokens(batch):
        return remote(
            tokens_in.at[pl.ds((1 - turn) * 4 + 2 * batch, 2)],
            tokens.at[pl.ds(2 * batch, 2), own_half],
            token_ssem.at[batch],
            token_rsem.at[batch],
            y_peer,
        )

    def send_cot(seq):
        return remote(
            cotangent_in.at[(1 - turn) * 4 + seq],
            inc.at[pl.ds(seq * 128 + turn * 64, 64)],
            cot_ssem.at[seq],
            cot_rsem.at[seq],
            y_peer,
        )

    send_tokens(0).start()
    load_tokens.wait()

    def norm(value, gain, shift):
        center = value - jnp.mean(value, axis=1, keepdims=True)
        spread = jnp.mean(center * center, axis=1, keepdims=True)
        return (center * lax.rsqrt(spread + 1e-05) * gain + shift).astype(BF)

    def first_norm(seqs, side):
        starts = [pl.multiple_of(seq * 128 + side * 64, 64) for seq in seqs]
        for seq, start in zip(seqs, starts):

            def step(m, carry, seq=seq, start=start):
                rows = pl.ds(pl.multiple_of(start + m * 32, 32), 32)
                inner = pl.ds(pl.multiple_of(side * 64 + m * 32, 32), 32)
                value = tokens[seq, inner, :].astype(F32) + time_embed[seq : seq + 1, :]
                hidden[rows, :] = value
                grad_attn[rows, :] = norm(value, row_of(gain_one), row_of(shift_one))
                return carry

            lax.fori_loop(0, 2, step, 0)
        if len(seqs) == 4:
            send_tokens(1).start()
        rows = jnp.concatenate([grad_attn[pl.ds(start, 64), :] for start in starts], axis=0)
        for part in range(3):
            columns = slice(part * 1024, (part + 1) * 1024)
            if len(seqs) == 4:
                load_qkv(2 * part).wait()
                load_qkv(2 * part + 1).wait()
            value = mm(rows[:, :512], wide_a[:, columns], 1, 0)
            value = (value + mm(rows[:, 512:], wide_g[:, columns], 1, 0)).astype(BF)
            for index, start in enumerate(starts):
                piece = value[index * 64 : (index + 1) * 64]
                if part == 0:
                    wide_a[pl.ds(start, 64), 3072:4096] = piece
                else:
                    (normed, v_held)[part - 1][pl.ds(start, 64), :] = piece

    def forward_heads(seq, pair):
        rows = pl.ds(pl.multiple_of(seq * 128, 128), 128)
        lanes = pl.ds(pl.multiple_of(pair * 128, 128), 128)

        def turned(value):
            value = value.astype(F32)
            return value * cosine[...] + rotated_partner(value) * sine[...]

        first = lane_index(128) < 64
        q = (turned(wide_a[rows, pl.ds(pl.multiple_of(3072 + pair * 128, 128), 128)]) * 0.125).astype(BF)
        k = turned(normed[rows, lanes]).astype(BF)
        q_held[rows, lanes] = q
        k_held[rows, lanes] = k
        scores = mm(q, two_heads(k), 1, 1)
        highest, exponent = [], []
        for part in range(2):
            s = scores[:, part * 128 : (part + 1) * 128]
            highest.append(jnp.max(s, axis=1, keepdims=True))
            exponent.append(jnp.exp(s - highest[part]))
        sums = mm(
            jnp.concatenate(exponent, axis=1).astype(BF),
            jnp.concatenate(
                [two_heads(v_held[rows, lanes]), head_mask(64).astype(BF)], axis=1
            ),
            1,
            0,
        )
        attended[rows, lanes] = (sums[:, :128] / sums[:, 128:]).astype(BF)
        log_total = jnp.where(first, highest[0], highest[1]) + jnp.log(sums[:, 128:])
        log_held[rows, lanes] = in_terms(log_total)

    first_norm((0, 1, 2, 3), turn)
    for batch in range(2):
        send_tokens(batch).wait_recv()
        first_norm((2 * batch, 2 * batch + 1), 1 - turn)
        if batch == 0:
            for seq in range(4):
                send_cot(seq).start()

        def forward_step(index, carry, batch=batch):
            for pair in range(4):
                forward_heads(2 * batch + index // 2, (index % 2) * 4 + pair)
            return carry

        lax.fori_loop(0, 4, forward_step, 0)
        if batch == 0:
            load_weight(0).wait()
        rows = slice(batch * 256, (batch + 1) * 256)
        hidden[rows, :] = hidden[rows, :] + mm(attended[rows, :], weight[0], 1, 0)

        def second_step(m, carry, batch=batch):
            rows = pl.ds(pl.multiple_of(batch * 256 + m * 32, 32), 32)
            normed[rows, :] = norm(hidden[rows, :], row_of(gain_two), row_of(shift_two))
            return carry

        lax.fori_loop(0, 8, second_step, 0)
    spill_normed = load(7, grad_attn, normed_one_out)
    spill_hidden = load(12, hidden, hidden_one_out)
    spill_normed.start()
    spill_hidden.start()
    load_weight(2).start()
    pump("start")

    def up_tile(tile):
        columns = slice(tile * 1024, (tile + 1) * 1024)
        bias = row_of(b_up)

        def step(m, carry):
            for half in range(2):
                rows = pl.ds(pl.multiple_of(m * 256 + half * 128, 128), 128)
                u = mm(normed[rows, :], weight[(tile + 1) % 2], 1, 0) + bias[:, columns]
                square = u * u
                bend = jnp.tanh(u * (GELU_A + (GELU_A * GELU_B) * square))
                side = 0.5 * (1.0 + bend)
                wide_a[rows, columns] = (u * side).astype(BF)
                slope = side + (0.5 * u) * (1.0 - bend * bend) * (
                    GELU_A + (3.0 * GELU_A * GELU_B) * square
                )
                wide_g[rows, columns] = slope.astype(BF)
            return carry

        lax.fori_loop(0, 2, step, 0)

    def down_unit(unit):
        def step(m, carry):
            rows = pl.ds(pl.multiple_of(m * 512, 512), 512)
            value = mm(inc[:, rows], wide_a[:, unit * 1024 : (unit + 1) * 1024], 0, 0)
            for q in range(4):
                at = q * 128
                place_block(
                    value[at : at + 64], value[at + 64 : at + 128], unit, q % 2, q // 2, m
                )
            return carry

        lax.fori_loop(0, 2, step, 0)

    for part in range(4):
        load_weight(1 + part).wait()
        up_tile(part)
        load_weight(part + 3).start()
        pump("up%d" % part)
        if part == 0:
            for seq in range(4):
                load_cot(seq).wait()
                send_cot(seq).wait_recv()
        down_unit(UNIT_DOWN + part)
        pump("down%d" % part)

    for tile in range(4):
        load_weight(5 + tile).wait()
        columns = slice(tile * 1024, (tile + 1) * 1024)

        for part in range(2):
            at = tile * 1024 + part * 512
            grad = mm(inc[...], weight[(tile + 1) % 2, part * 512 : (part + 1) * 512, :], 1, 1)
            grad = (grad * wide_g[:, at : at + 512].astype(F32)).astype(BF)
            wide_g[:, at : at + 512] = grad
            sums = jnp.sum(grad.astype(F32), axis=0, keepdims=True)
            for row in range(4):
                message[2 * tile + part, 16 + row : 17 + row, :] = sums[
                    :, row * 128 : (row + 1) * 128
                ]
        load_weight(tile + 7).start()
        pump("gu%d" % tile)

    wait_sent(range(0, 4))

    def up_step(p, carry):
        columns = pl.ds(pl.multiple_of(p * 512, 512), 512)
        value = mm(wide_g[:, columns], normed[...], 0, 0)
        for j in range(4):
            low = value[j * 64 : (j + 1) * 64]
            high_rows = value[256 + j * 64 : 256 + (j + 1) * 64]
            place_block(low, high_rows, UNIT_UP + j, p % 2, (p // 2) % 2, p // 4)
        return carry

    for part in range(4):
        lax.fori_loop(2 * part, 2 * part + 2, up_step, 0)
        pump("gup%d" % part)

    for tile in range(9, 13):
        load_weight(tile).wait()
        columns = slice((tile - 9) * 1024, (tile - 8) * 1024)

        def norm_step(m, carry, tile=tile, columns=columns):
            rows = pl.ds(pl.multiple_of(m * 256, 256), 256)
            add = mm(wide_g[rows, columns], weight[tile % 2], 1, 1)
            total[rows, :] = add if tile == 9 else total[rows, :] + add
            return carry

        lax.fori_loop(0, 2, norm_step, 0)
        load_weight(tile + 2).start()
        pump("gn%d" % (tile - 9))

    spill_normed.wait()
    spill_hidden.wait()

    def norm_back(h, gain, rows):
        center = h - jnp.mean(h, axis=1, keepdims=True)
        scale = lax.rsqrt(jnp.mean(center * center, axis=1, keepdims=True) + 1e-05)
        xh = center * scale
        q = total[rows, :]
        e = q * gain
        grad = (
            e - jnp.mean(e, axis=1, keepdims=True) - xh * jnp.mean(e * xh, axis=1, keepdims=True)
        ) * scale
        return (
            grad,
            jnp.sum(q * xh, axis=0, keepdims=True),
            jnp.sum(q, axis=0, keepdims=True),
        )

    def norm_two_step(m, carry):
        rows = pl.ds(pl.multiple_of(m * 32, 32), 32)
        grad, gain_sum, shift_sum = norm_back(hidden[rows, :], row_of(gain_two), rows)
        cot = inc[rows, :].astype(F32)
        grad = cot + grad
        hidden[rows, :] = grad
        grad_attn[rows, :] = grad.astype(BF)
        return (
            carry[0] + gain_sum,
            carry[1] + shift_sum,
            carry[2] + jnp.sum(cot, axis=0, keepdims=True),
        )

    none = jnp.zeros((1, 1024), F32)
    gain_sum, shift_sum, down_sum = lax.fori_loop(0, 16, norm_two_step, (none, none, none))
    vec_rows[6:7, :] = gain_sum
    vec_rows[7:8, :] = shift_sum
    vec_rows[8:9, :] = down_sum
    pump("ln2")

    wait_sent(range(4, 5))

    def out_step(m, carry):
        rows = pl.ds(pl.multiple_of(m * 512, 512), 512)
        value = mm(grad_attn[:, rows], attended[...], 0, 0)
        for q in range(4):
            at = q * 128
            place_block(
                value[at : at + 64], value[at + 64 : at + 128], UNIT_OUT, q % 2, q // 2, m
            )
        return carry

    lax.fori_loop(0, 2, out_step, 0)
    pump("out")
    load_weight(13).wait()

    def mixed_back(m, carry):
        rows = pl.ds(pl.multiple_of(m * 256, 256), 256)
        normed[rows, :] = mm(grad_attn[rows, :], weight[1], 1, 1).astype(BF)
        return carry

    lax.fori_loop(0, 2, mixed_back, 0)
    load_weight(15).start()
    fill_normed = load(7, normed_one_out, grad_attn)
    fill_normed.start()
    pump("mb")


    def heads(seq, pair):
        rows = pl.ds(pl.multiple_of(seq * 128, 128), 128)

        def lanes(base):
            return pl.ds(pl.multiple_of(base + pair * 128, 128), 128)

        first = lane_index(128) < 64
        minus = (-head_mask(3)).astype(BF)
        both = jnp.where(
            (lax.broadcasted_iota(jnp.int32, (256, 128), 0) % 128) // 64 == lane_index(256) // 64,
            1.0,
            0.0,
        ).astype(BF)
        q = q_held[rows, lanes(0)]
        k_two = two_heads(k_held[rows, lanes(0)])
        v_two = two_heads(v_held[rows, lanes(0)])
        grad_out = normed[rows, lanes(0)]
        product_rows = grad_out.astype(F32) * attended[rows, lanes(0)].astype(F32)
        head_part = product_rows.astype(BF)
        tail_part = (product_rows - head_part.astype(F32)).astype(BF)
        inner = mm(jnp.concatenate([head_part, tail_part], axis=1), both, 1, 0)
        scores = mm(
            jnp.concatenate([q, log_held[rows, lanes(0)]], axis=1),
            jnp.concatenate([k_two, minus], axis=1),
            1,
            1,
        )
        grad_probs = mm(
            jnp.concatenate([grad_out, in_terms(inner)], axis=1),
            jnp.concatenate([v_two, minus], axis=1),
            1,
            1,
        )
        soft = jnp.exp(scores)
        grad_scores = (soft * grad_probs).astype(BF)
        grad_q = mm(grad_scores, k_two, 1, 0) * 0.125
        grad_k = mm(grad_scores, q, 0, 0)
        grad_v = mm(soft.astype(BF), grad_out, 0, 0)
        grad_k = jnp.where(first, grad_k[:128], grad_k[128:])
        grad_v = jnp.where(first, grad_v[:128], grad_v[128:])

        def unturn(value):
            return value * cosine[...] - rotated_partner(value) * sine[...]

        wide_g[rows, lanes(0)] = unturn(grad_q).astype(BF)
        wide_g[rows, lanes(1024)] = unturn(grad_k).astype(BF)
        wide_g[rows, lanes(2048)] = grad_v.astype(BF)

    def heads_step(index, carry):
        for pair in range(4):
            heads(index // 2, (index % 2) * 4 + pair)
        return carry

    for part in range(4):
        lax.fori_loop(2 * part, 2 * part + 2, heads_step, 0)
        pump("attn%d" % part)

    fill_normed.wait()
    wait_sent(range(5, 8))

    def qkv_step(p, carry):
        columns = pl.ds(pl.multiple_of(p * 384, 128), 384)
        value = mm(wide_g[:, columns], grad_attn[...], 0, 0)
        for j in range(3):
            low = value[j * 64 : (j + 1) * 64]
            high_rows = value[192 + j * 64 : 192 + (j + 1) * 64]
            place_block(low, high_rows, UNIT_QKV + j, p % 2, (p // 2) % 2, p // 4)
        return carry

    lax.fori_loop(0, 4, qkv_step, 0)
    pump("qkv0")
    lax.fori_loop(4, 8, qkv_step, 0)
    pump("qkv1")

    for tile in range(14, 17):
        load_weight(tile).wait()
        columns = slice((tile - 14) * 1024, (tile - 13) * 1024)

        def first_step(m, carry, tile=tile, columns=columns):
            rows = pl.ds(pl.multiple_of(m * 256, 256), 256)
            add = mm(wide_g[rows, columns], weight[tile % 2], 1, 1)
            total[rows, :] = add if tile == 14 else total[rows, :] + add
            return carry

        lax.fori_loop(0, 2, first_step, 0)
        load_weight(tile + 2).start()
        pump("gf%d" % (tile - 14))
    gain_sum, shift_sum = none, none
    for seq in range(4):

        def norm_one_step(m, carry, seq=seq):
            rows = pl.ds(pl.multiple_of(seq * 128 + m * 32, 32), 32)
            inner = pl.ds(pl.multiple_of(m * 32, 32), 32)
            value = tokens[seq, inner, :].astype(F32) + time_embed[seq : seq + 1, :]
            grad, gain_add, shift_add = norm_back(value, row_of(gain_one), rows)
            grad = grad + hidden[rows, :]
            inc[rows, :] = grad.astype(BF)
            return (
                carry[0] + gain_add,
                carry[1] + shift_add,
                carry[2] + jnp.sum(grad, axis=0, keepdims=True),
            )

        gain_sum, shift_sum, embed_sum = lax.fori_loop(
            0, 4, norm_one_step, (gain_sum, shift_sum, none)
        )
        vec_rows[seq : seq + 1, :] = embed_sum
    vec_rows[4:5, :] = gain_sum
    vec_rows[5:6, :] = shift_sum
    fill_hidden = load(12, hidden_one_out, hidden)
    fill_hidden.start()
    for pair in range(8):
        message[pair, 0:16, :] = vec_rows[:, pair * 128 : (pair + 1) * 128]

    def small_copy(other):
        return remote(
            message.at[other // 4],
            small_recv.at[me],
            small_ssem.at[other],
            small_rsem.at[me],
            (other // 2, other % 2),
        )

    def small_start(step, carry):
        small_copy(lax.rem(me + step, devices)).start()
        return carry

    lax.fori_loop(1, devices, small_start, 0)
    small_recv[me] = message[place // 2]
    pump("rows")
    fill_hidden.wait()
    for tile in range(4):
        load_weight(17 + tile).wait()
        columns = slice(tile * 1024, (tile + 1) * 1024)

        def mixed_step(m, carry, tile=tile, columns=columns):
            rows = pl.ds(pl.multiple_of(m * 256, 256), 256)
            add = mm(wide_a[rows, columns], weight[(tile + 1) % 2], 1, 0)
            if tile == 0:
                total[rows, :] = hidden[rows, :] + row_of(b_down) + add
            elif tile < 3:
                total[rows, :] = total[rows, :] + add
            else:
                attended[rows, :] = (total[rows, :] + add).astype(BF)
            return carry

        lax.fori_loop(0, 2, mixed_step, 0)
        if tile < 2:
            load_weight(19 + tile).start()
        pump("mx%d" % tile)
    pump("small")

    def small_wait(step, carry):
        source = lax.rem(me + step, devices)
        pltpu.make_async_remote_copy(
            src_ref=message.at[0],
            dst_ref=small_recv.at[source],
            send_sem=small_ssem.at[source],
            recv_sem=small_rsem.at[source],
            device_id=(source // 2, source % 2),
            device_id_type=MESH_ID,
        ).wait()
        return carry

    lax.fori_loop(1, devices, small_wait, 0)

    def spread(source, carry):
        for row in range(4):
            at = 4 * source + row
            embeds[pl.ds(at, 1), :] = small_recv[source, row : row + 1, :]
            tables[0, pl.ds(at, 1), :] = small_recv[source, 20 + row : 21 + row, :]
            tables[1, pl.ds(at, 1), :] = small_recv[source, 24 + row : 25 + row, :]
        return carry + small_recv[source, 0:24, :]

    sums = lax.fori_loop(0, devices, spread, jnp.zeros((24, 128), F32))
    rest, terms = embeds[...], []
    for _ in range(3):
        terms.append(rest.astype(BF))
        rest = rest - terms[-1].astype(F32)

    def own_lanes(value):
        return jnp.where(core == 0, value, pltpu.roll(value, 64, 1))

    for part in range(2):
        turned = tables[part].astype(BF)
        value = sum(mm(turned, term, 0, 0) for term in terms)
        small_out[part * 128 : (part + 1) * 128, :] = own_lanes(value)
    small_out[256:280, :] = own_lanes(sums)
    wide = jnp.where(core == 0, sums[16:18], sums[18:20])
    small_out[280:282, :] = wide
    pump("end")

    for part in range(2):
        for seq in range(4):
            for copy in row_copies(part, seq):
                copy.wait()
    wait_sent(range(8, 12))
    for batch in range(2):
        send_tokens(batch).wait_send()
    for seq in range(4):
        send_cot(seq).wait_send()
    for chain in range(2 * UNITS):
        one_copy(chain).wait_send()
        two_copy(chain).wait_send()
        for step in (1, 2, 3) if ORDERS[chain] in "xy" else (1, 2):
            three_copy(chain, step).wait_send()
        if ORDERS[chain] in "xy":
            gather_copy(chain).wait_send()


LAST_STEPS = 16
WINDOW = 0.14
BIAS = {"one": 0, "two": 0, "three": -12, "last_x": -12, "swap": 2, "gather": 8}
ROWS_RANK = (-10, 100)
LENGTHS = {
    "start": 25.0,
    "up": 2.5,
    "down": 1.9,
    "gu": 2.1,
    "mx": 1.8,
    "gup": 1.5,
    "gn": 1.9,
    "ln": 3.0,
    "out": 1.9,
    "mb": 2.0,
    "attn": 3.8,
    "qkv": 2.8,
    "gf": 1.9,
    "rows": 6.0,
}
PIECES = (
    ("start", ()),
    ("up0", ()),
    ("down0", (0,)),
    ("up1", ()),
    ("down1", (1,)),
    ("up2", ()),
    ("down2", (2,)),
    ("up3", ()),
    ("down3", (3,)),
    ("gu0", ()),
    ("gu1", ()),
    ("gu2", ()),
    ("gu3", ()),
    ("gup0", ()),
    ("gup1", ()),
    ("gup2", ()),
    ("gup3", (4, 5, 6, 7)),
    ("gn0", ()),
    ("gn1", ()),
    ("gn2", ()),
    ("gn3", ()),
    ("ln2", ()),
    ("out", (8,)),
    ("mb", ()),
    ("attn0", ()),
    ("attn1", ()),
    ("attn2", ()),
    ("attn3", ()),
    ("qkv0", ()),
    ("qkv1", (9, 10, 11)),
    ("gf0", ()),
    ("gf1", ()),
    ("gf2", ()),
    ("rows", ()),
    ("mx0", ()),
    ("mx1", ()),
    ("mx2", ()),
    ("mx3", ()),
)
CHAINS = {
    "x": ("one", "two", "three", "gather"),
    "y": ("one", "two", "three", "gather"),
    "z": ("one", "two", "last_x", "swap"),
    "w": ("one", "two", "last_x", "swap"),
}
COSTS = {"core": 0.5, "one": 0.2, "two": 0.15, "three": 0.25, "last_x": 0.15, "swap": 0.15, "gather": 0.05, "rows": 0.0}
FIRST = {"x": "x", "y": "y", "z": "a", "w": "x"}
SECOND = {"x": "y", "y": "x", "z": "b", "w": "a"}


def transfer(stage, kind):
    if stage == "one":
        return FIRST[kind], 0.262
    if stage == "two":
        return SECOND[kind], 0.262 if kind == "z" else 0.131
    if stage == "three":
        return "b", 0.131
    if stage == "last_x" and kind == "w":
        return "b", 0.131
    if stage in ("last_x", "swap"):
        return ("x" if stage == "last_x" else "y"), 0.0655
    return "y", 0.0328


def schedule(orders):
    rate, lag = 0.086 / 2, 1.4
    flying = {axis: [] for axis in "xyab"}
    queues = {axis: [] for axis in "xyab"}
    arrived, order = [], []
    now, clock = 0.0, 0.0
    core = []

    def advance(until):
        nonlocal now
        while now < until:
            step = until - now
            for fly in flying.values():
                if fly:
                    step = min(step, min(f[0] for f in fly) * len(fly) / rate)
            now += step
            for axis, fly in flying.items():
                if fly:
                    part = step * rate / len(fly)
                    for f in fly:
                        f[0] -= part
                    for f in [f for f in fly if f[0] < 1e-9]:
                        fly.remove(f)
                        if f[1] is None:
                            continue
                        arrived.append((now + lag, f[1]))
            if step <= 0:
                now = until

    def issue():
        for axis in "baxy":
            queue = queues[axis]
            while queue and sum(f[0] for f in flying[axis] if f[1] is not None) < WINDOW:
                queue.sort()
                _, key, size = queue.pop(0)
                flying[axis].append([size, key, clock])
                if axis == "b":
                    flying["a"].append([size * (0.75 if key[0] == "three" else 0.5), None, clock])
                order.append(("start",) + key)

    def ready(stage, chain):
        axis, size = transfer(stage, orders[chain])
        queues[axis].append((chain + BIAS[stage], (stage, chain), size))

    def take(when, key):
        nonlocal clock
        clock = max(clock, when)
        advance(clock)
        stage, chain = key
        if stage == "rows":
            issue()
            return
        order.append(("add",) + key)
        clock += COSTS[stage]
        advance(clock)
        if stage == "core":
            ready("one", 2 * chain)
            ready("one", 2 * chain + 1)
        else:
            names = CHAINS[orders[chain]]
            if stage != names[-1]:
                ready(names[names.index(stage) + 1], chain)
        issue()

    def due():
        while True:
            arrived.sort()
            if not arrived or arrived[0][0] > clock:
                return
            take(*arrived.pop(0))

    for label, units in PIECES:
        clock += LENGTHS[label.rstrip("0123456789")]
        advance(clock)
        for unit in units:
            order.append(("start", "core", unit))
            arrived.append((clock + 2.3 + 0.3 * units.index(unit), ("core", unit)))
        if label == "mx3":
            queues["y"].append((ROWS_RANK[0], ("rows", 0), 0.524))
        if label == "rows":
            for seq in range(4):
                queues["y"].append((ROWS_RANK[1], ("rows", 1 + seq), 0.131))
        issue()
        due()
        order.append(("mark", label, 0))
    while arrived or any(flying.values()):
        if arrived:
            arrived.sort()
            if arrived[0][0] <= now or not any(flying.values()):
                take(*arrived.pop(0))
                continue
        advance(now + 0.1)
    order.insert(len(order) - LAST_STEPS, ("mark", "small", 0))
    order.append(("mark", "end", 0))
    return order


def layer_call(operands, constants, times):
    vmem = pl.BlockSpec(memory_space=pltpu.VMEM)
    hbm = pl.BlockSpec(memory_space=pl.ANY)
    dma = pltpu.SemaphoreType.DMA
    chains = 2 * UNITS
    return pl.pallas_call(
        layer_kernel,
        name="layer",
        out_shape=(
            jax.ShapeDtypeStruct((8, 64, 1024), BF),
            jax.ShapeDtypeStruct((8, 64, 1024), BF),
            jax.ShapeDtypeStruct((UNITS, 2, 64, 512), BF),
            jax.ShapeDtypeStruct((288, 128), F32),
            jax.ShapeDtypeStruct((512, 1024), BF),
            jax.ShapeDtypeStruct((512, 1024), F32),
        ),
        in_specs=[hbm] * 6 + [vmem] * 10 + [pl.BlockSpec(memory_space=pltpu.SMEM)],
        out_specs=(hbm, hbm, vmem, vmem, hbm, hbm),
        scratch_shapes=[
            pltpu.VMEM((2 * UNITS + 8, 2, 2, 2, 64, 512), BF),
            pltpu.VMEM((4, 2, 2, 2, 2, 64, 512), BF),
            pltpu.VMEM((UNITS, 2, 2, 2, 64, 512), BF),
            pltpu.VMEM((UNITS, 2, 2, 64, 512), BF),
            pltpu.VMEM((UNITS, 4, 64, 512), BF),
            pltpu.VMEM((2, 1024, 1024), BF),
            pltpu.VMEM((512, 4096), BF),
            pltpu.VMEM((512, 4096), BF),
            pltpu.VMEM((512, 1024), BF),
            pltpu.VMEM((512, 1024), BF),
            pltpu.VMEM((512, 1024), BF),
            pltpu.VMEM((512, 1024), BF),
            pltpu.VMEM((4, 128, 1024), BF),
            pltpu.VMEM((512, 1024), BF),
            pltpu.VMEM((512, 1024), BF),
            pltpu.VMEM((512, 1024), F32),
            pltpu.VMEM((512, 1024), F32),
            pltpu.VMEM((512, 1024), BF),
            pltpu.VMEM((512, 1024), BF),
            pltpu.VMEM((8, 32, 128), F32),
            pltpu.VMEM((32, 32, 128), F32),
            pltpu.VMEM((16, 1024), F32),
            pltpu.VMEM((128, 128), F32),
            pltpu.VMEM((2, 128, 128), F32),
            pltpu.VMEM((8, 1024), F32),
            dma((21,)),
            dma((2,)),
            dma((2,)),
            dma((2,)),
            dma((4,)),
            dma((4,)),
            dma((4,)),
            dma((4,)),
            pltpu.SemaphoreType.REGULAR((4,)),
            dma((chains,)),
            dma((chains,)),
            dma((chains,)),
            dma((chains,)),
            dma((3 * chains,)),
            dma((3 * chains,)),
            dma((chains,)),
            dma((chains,)),
            dma((32,)),
            dma((32,)),
            dma((8,)),
            dma((8,)),
        ],
        compiler_params=pltpu.CompilerParams(
            collective_id=0, has_side_effects=True, vmem_limit_bytes=VMEM_LIMIT
        ),
    )(*operands, *constants, times)


def finish_kernel(
    mixed_in,
    tokens_in,
    shares_in,
    small_in,
    mixed_out,
    tokens_out,
    down_out,
    up_out,
    w_out_out,
    qkv_out,
    proj_out,
    time_bias,
    gain_one,
    shift_one,
    gain_two,
    shift_two,
    b_down,
    b_up,
    mixed,
    tokens,
    shares,
    small,
    down,
    up,
    w_out,
    qkv,
    proj,
    in_sem,
    out_sem,
):
    def inward(index):
        if index < UNITS:
            source, target = shares_in.at[index], shares.at[index]
        else:
            source, target = (
                (small_in, small),
                (mixed_in, mixed),
                (tokens_in, tokens),
            )[index - UNITS]
        return pltpu.make_async_copy(source, target, in_sem.at[index])

    def outward(index):
        if index < 4:
            columns = pl.ds(index * 1024, 1024)
            source, target = down.at[:, columns], down_out.at[:, columns]
        else:
            source, target = (
                (up, up_out),
                (w_out, w_out_out),
                (qkv, qkv_out),
                (proj, proj_out),
                (mixed, mixed_out),
                (tokens, tokens_out),
            )[index - 4]
        return pltpu.make_async_copy(source, target, out_sem.at[index])

    turn = list(range(UNIT_UP, UNIT_UP + 4)) + list(range(UNIT_DOWN, UNIT_DOWN + 4))
    turn += list(range(UNIT_OUT, UNITS)) + [UNITS, UNITS + 1, UNITS + 2]
    for index in turn:
        inward(index).start()

    def share(unit, h):
        return shares[unit, h].astype(F32)

    for j in range(4):
        inward(UNIT_UP + j).wait()
    for h in range(2):
        for j in range(0, 4, 2):
            both = jnp.concatenate([share(UNIT_UP + j, h), share(UNIT_UP + j + 1, h)], axis=0)
            up[h * 512 : (h + 1) * 512, j * 64 : (j + 2) * 64] = both.T
    outward(4).start()
    for j in range(4):
        inward(UNIT_DOWN + j).wait()
        for h in range(2):
            at = j * 1024 + h * 512
            down[:, at : at + 512] = share(UNIT_DOWN + j, h)
        outward(j).start()
    inward(UNIT_OUT).wait()
    for h in range(2):
        w_out[:, h * 512 : (h + 1) * 512] = share(UNIT_OUT, h)
    outward(5).start()
    for j in range(3):
        inward(UNIT_QKV + j).wait()
        for h in range(2):
            qkv[j * 64 : (j + 1) * 64, h * 512 : (h + 1) * 512] = share(UNIT_QKV + j, h)
    outward(6).start()
    inward(UNITS).wait()
    for part in range(2):
        proj[:, part * 128 : (part + 1) * 128] = small[part * 128 : (part + 1) * 128, :].T[:64]
    outward(7).start()
    inward(UNITS + 1).wait()
    outward(8).start()
    inward(UNITS + 2).wait()
    outward(9).start()
    rows = small[256:288, :]
    time_bias[...] = jnp.sum(rows[0:4], axis=0)[:64]
    for index, target in enumerate((gain_one, shift_one, gain_two, shift_two, b_down)):
        target[...] = rows[4 + index, :64]
    for index in range(2):
        b_up[index * 128 : (index + 1) * 128] = rows[24 + index, :]
    for index in range(10):
        outward(index).wait()


def finish_call(mixed, tokens, shares, small):
    vmem = pl.BlockSpec(memory_space=pltpu.VMEM)
    hbm = pl.BlockSpec(memory_space=pl.ANY)
    like = jax.ShapeDtypeStruct
    vector = like((64,), F32)
    wide = ((64, 4096), (1024, 256), (64, 1024), (192, 1024), (64, 256))
    return pl.pallas_call(
        finish_kernel,
        name="finish",
        out_shape=(like((8, 64, 1024), BF),) * 2
        + tuple(like(shape, F32) for shape in wide)
        + (vector,) * 6
        + (like((256,), F32),),
        in_specs=[hbm] * 4,
        out_specs=(hbm,) * 7 + (vmem,) * 7,
        scratch_shapes=[pltpu.VMEM((8, 64, 1024), BF)] * 2
        + [pltpu.VMEM((UNITS, 2, 64, 512), BF), pltpu.VMEM((288, 128), F32)]
        + [pltpu.VMEM(shape, F32) for shape in wide]
        + [pltpu.SemaphoreType.DMA((UNITS + 3,)), pltpu.SemaphoreType.DMA((10,))],
        compiler_params=pltpu.CompilerParams(vmem_limit_bytes=VMEM_LIMIT),
    )(mixed, tokens, shares, small)


def body(
    tokens,
    noise_times,
    time_proj,
    time_bias,
    gain_one,
    shift_one,
    w_qkv,
    w_out,
    gain_two,
    shift_two,
    w_up,
    b_up,
    w_down,
    b_down,
    cotangent,
):
    seq_ways, tok_ways = lax.axis_size("seq"), lax.axis_size("tok")
    model_width = tokens.shape[-1]
    seq_count, length = tokens.shape[0] // tok_ways, tokens.shape[1] * tok_ways
    row_count = seq_count * length
    all_times = lax.all_gather(noise_times, "seq", tiled=True)
    own_times = lax.dynamic_slice_in_dim(
        noise_times, lax.axis_index("tok") * seq_count, seq_count
    )
    embed_table = noise_table(own_times).astype(jnp.bfloat16)
    time_embed = product(embed_table, time_proj) + time_bias.astype(jnp.float32)
    tokens = gather_sequences(tokens)
    incoming = gather_sequences(cotangent).reshape(row_count, model_width)
    hidden_zero = (tokens.astype(jnp.float32) + time_embed[:, None, :]).reshape(
        row_count, model_width
    )
    normed_one, pull_one = jax.vjp(
        layer_norm, hidden_zero, gain_one.astype(jnp.float32), shift_one.astype(jnp.float32)
    )
    normed_one = normed_one.astype(jnp.bfloat16)
    projected = product(normed_one, w_qkv).astype(jnp.bfloat16)
    received, attended, log_total = attend_items(
        projected.reshape(seq_count, length, 3, 1, model_width)
    )
    attended = attended.reshape(row_count, model_width)
    hidden_one = hidden_zero + product(attended, w_out)
    normed_two, pull_two = jax.vjp(
        layer_norm, hidden_one, gain_two.astype(jnp.float32), shift_two.astype(jnp.float32)
    )
    normed_two = normed_two.astype(jnp.bfloat16)
    upward = product(normed_two, w_up) + b_up.astype(jnp.float32)
    active, pull_gelu = jax.vjp(jax.nn.gelu, upward)
    active = active.astype(jnp.bfloat16)
    out_wdown = scatter_sum(contract_rows(incoming, active))
    result = hidden_one + (product(active, w_down) + b_down.astype(jnp.float32))
    mixed_out = return_positions(
        result.astype(jnp.bfloat16).reshape(seq_count, length, model_width)
    )
    sum_down = jnp.sum(incoming, axis=0, dtype=jnp.float32)
    grad_active = times_transpose(incoming, w_down)
    (grad_upward,) = pull_gelu(grad_active)
    grad_upward = grad_upward.astype(jnp.bfloat16)
    sum_up = jnp.sum(grad_upward, axis=0, dtype=jnp.float32)
    out_wup = scatter_sum(contract_rows(grad_upward, normed_two))
    grad_norm_two = times_transpose(grad_upward, w_up)
    grad_hidden_two, grad_gain_two, grad_shift_two = pull_two(grad_norm_two)
    grad_hidden_one = incoming.astype(jnp.float32) + grad_hidden_two
    grad_attn = grad_hidden_one.astype(jnp.bfloat16)
    out_wout = scatter_sum(contract_rows(grad_attn, attended))
    grad_mixed = times_transpose(grad_attn, w_out).astype(jnp.bfloat16)
    grad_parts = attention_grad(
        received, log_total, grad_mixed.reshape(seq_count, length, 1, model_width)
    ).reshape(row_count, 3 * model_width)
    out_wqkv = scatter_sum(contract_rows(grad_parts, normed_one))
    grad_norm_one = times_transpose(grad_parts, w_qkv)
    grad_hidden_zero, grad_gain_one, grad_shift_one = pull_one(grad_norm_one)
    grad_total = grad_hidden_one + grad_hidden_zero
    grad_tokens = return_positions(
        grad_total.astype(jnp.bfloat16).reshape(seq_count, length, model_width)
    )
    grad_embed = jnp.sum(grad_total.reshape(seq_count, length, model_width), axis=1)
    wide = sum_up.shape[0] // model_width
    small = jnp.concatenate(
        [
            grad_embed.reshape(seq_count, seq_ways, -1).swapaxes(0, 1),
            grad_gain_one.reshape(seq_ways, 1, -1),
            grad_shift_one.reshape(seq_ways, 1, -1),
            grad_gain_two.reshape(seq_ways, 1, -1),
            grad_shift_two.reshape(seq_ways, 1, -1),
            sum_down.reshape(seq_ways, 1, -1),
            sum_up.reshape(seq_ways, wide, -1),
        ],
        axis=1,
    )
    small = lax.all_to_all(small, "seq", split_axis=0, concat_axis=0, tiled=True)
    small = lax.all_gather(small, "tok", axis=1)
    embeds = small[:, :, :seq_count].reshape(-1, small.shape[-1])
    out_proj = jnp.dot(
        noise_table(all_times).astype(jnp.bfloat16).astype(jnp.float32).T,
        embeds,
        precision=lax.Precision.HIGHEST,
    )
    out_bias = jnp.sum(embeds, axis=0)
    sums = jnp.sum(small[:, :, seq_count:], axis=(0, 1))
    return (
        mixed_out,
        grad_tokens,
        out_proj,
        out_bias,
        sums[0],
        sums[1],
        out_wqkv,
        out_wout,
        sums[2],
        sums[3],
        out_wup,
        sums[5:].reshape(-1),
        out_wdown,
        sums[4],
    )


def rotary_lanes():
    halves = HD // 2
    frequency = np.exp(-math.log(10000.0) * np.arange(halves, dtype=np.float32) / halves)
    angles = np.arange(128, dtype=np.float32)[:, None] * frequency.astype(np.float32)[None, :]
    cosine, sine = np.cos(angles), np.sin(angles)
    return (
        jnp.asarray(np.tile(cosine, (1, 4)), jnp.float32),
        jnp.asarray(np.concatenate([-sine, sine] * 2, axis=1), jnp.float32),
    )


def fast_body(
    tokens,
    noise_times,
    time_proj,
    time_bias,
    gain_one,
    shift_one,
    w_qkv,
    w_out,
    gain_two,
    shift_two,
    w_up,
    b_up,
    w_down,
    b_down,
    cotangent,
):
    cosine, sine = rotary_lanes()
    mixed_out, grad_tokens, shares, small, _, _ = layer_call(
        (tokens, cotangent, w_qkv, w_out, w_up, w_down),
        (
            time_proj,
            time_bias,
            gain_one,
            shift_one,
            gain_two,
            shift_two,
            b_up,
            b_down,
            cosine,
            sine,
        ),
        noise_times,
    )
    (
        mixed_out,
        grad_tokens,
        out_wdown,
        out_wup,
        out_wout,
        out_wqkv,
        out_proj,
        out_bias,
        out_gain_one,
        out_shift_one,
        out_gain_two,
        out_shift_two,
        out_bdown,
        out_bup,
    ) = finish_call(mixed_out, grad_tokens, shares, small)
    return (
        mixed_out,
        grad_tokens,
        out_proj.T,
        out_bias,
        out_gain_one,
        out_shift_one,
        out_wqkv.T,
        out_wout.T,
        out_gain_two,
        out_shift_two,
        out_wup,
        out_bup,
        out_wdown.T,
        out_bdown,
    )


def solution(mesh):
    chosen = fast_body if (mesh.shape["seq"], mesh.shape["tok"]) == (16, 2) else body
    in_specs = (
        P("seq", "tok", None),
        P("seq"),
        P(),
        P(),
        P(),
        P(),
        P(),
        P(),
        P(),
        P(),
        P(),
        P(),
        P(),
        P(),
        P("seq", "tok", None),
    )
    out_specs = (
        P("seq", "tok", None),
        P("seq", "tok", None),
        P(None, "seq"),
        P("seq"),
        P("seq"),
        P("seq"),
        P(None, "seq"),
        P(None, "seq"),
        P("seq"),
        P("seq"),
        P(None, "seq"),
        P("seq"),
        P(None, "seq"),
        P("seq"),
    )
    return jax.shard_map(chosen, mesh=mesh, in_specs=in_specs, out_specs=out_specs, check_vma=False)
```

```python
import math

import jax
import jax.numpy as jnp
import numpy as np
from jax import lax
from jax.experimental import pallas as pl
from jax.experimental.pallas import tpu as pltpu
from jax.sharding import PartitionSpec as P

HD = 64
TEMB = 256
VMEM_LIMIT = 64 * 1024 * 1024 - 65536


def layer_norm(hidden, gain_vec, shift_vec):
    center = hidden - jnp.mean(hidden, axis=-1, keepdims=True)
    spread = jnp.mean(center * center, axis=-1, keepdims=True)
    return center * lax.rsqrt(spread + 1e-05) * gain_vec + shift_vec


def noise_table(noise_steps):
    halves = TEMB // 2
    frequency = jnp.exp(-math.log(10000.0) * jnp.arange(halves, dtype=jnp.float32) / halves)
    angles = noise_steps.astype(jnp.float32)[:, None] * frequency[None, :]
    return jnp.concatenate([jnp.sin(angles), jnp.cos(angles)], axis=-1)


def rotary_tables(length):
    halves = HD // 2
    frequency = jnp.exp(-math.log(10000.0) * jnp.arange(halves, dtype=jnp.float32) / halves)
    angles = jnp.arange(length, dtype=jnp.float32)[:, None] * frequency[None, :]
    angles = jnp.concatenate([angles, angles], axis=-1)[:, None, :]
    return (jnp.cos(angles), jnp.sin(angles))


def rotate(values, cosine, sine_tab):
    halves = values.shape[-1] // 2
    turned = jnp.concatenate([-values[..., halves:], values[..., :halves]], axis=-1)
    return values * cosine + turned * sine_tab


def unrotate(gradient, cosine, sine_tab):
    halves = gradient.shape[-1] // 2
    scaled = gradient * sine_tab
    turned = jnp.concatenate([scaled[..., halves:], -scaled[..., :halves]], axis=-1)
    return gradient * cosine + turned


def product(left_side, right_side):
    return jnp.dot(left_side, right_side, preferred_element_type=jnp.float32)


def contract_rows(left_side, right_side):
    return jnp.einsum("ra,rb->ab", left_side, right_side, preferred_element_type=jnp.float32)


def times_transpose(left_side, right_side):
    return jnp.einsum("rb,ab->ra", left_side, right_side, preferred_element_type=jnp.float32)


def split_heads(received):
    batch_size, length = (received.shape[0], received.shape[1])
    local_heads = received.shape[-1] // HD
    split_view = received.reshape(batch_size, length, 3, local_heads, HD)
    cosine, sine_tab = rotary_tables(length)
    queries = rotate(split_view[:, :, 0].astype(jnp.float32), cosine, sine_tab).astype(jnp.bfloat16)
    keys_rot = rotate(split_view[:, :, 1].astype(jnp.float32), cosine, sine_tab).astype(
        jnp.bfloat16
    )
    return (queries, keys_rot, split_view[:, :, 2], cosine, sine_tab)


def attend_items(received):
    batch_size, length = (received.shape[0], received.shape[1])
    scaling = 1.0 / math.sqrt(HD)
    queries, keys_rot, values, cosine, sine_tab = split_heads(received)
    scores = (
        jnp.einsum("gqhd,gkhd->ghqk", queries, keys_rot, preferred_element_type=jnp.float32)
        * scaling
    )
    highest = jnp.max(scores, axis=-1, keepdims=True)
    exponent = jnp.exp(scores - highest)
    totals = jnp.sum(exponent, axis=-1, keepdims=True)
    prob_rows = (exponent / totals).astype(jnp.bfloat16)
    log_total = (highest + jnp.log(totals))[..., 0]
    attended = jnp.einsum("ghqk,gkhd->gqhd", prob_rows, values, preferred_element_type=jnp.float32)
    attended = attended.astype(jnp.bfloat16).reshape(batch_size, length, 1, -1)
    return (received, attended, log_total)


def attention_grad(received, log_total, grad_heads):
    batch_size, length = (received.shape[0], received.shape[1])
    scaling = 1.0 / math.sqrt(HD)
    queries, keys_rot, values, cosine, sine_tab = split_heads(received)
    scores = (
        jnp.einsum("gqhd,gkhd->ghqk", queries, keys_rot, preferred_element_type=jnp.float32)
        * scaling
    )
    prob_rows = jnp.exp(scores - log_total[..., None])
    grad_out = grad_heads.reshape(batch_size, length, values.shape[2], HD)
    grad_probs = jnp.einsum("gqhd,gkhd->ghqk", grad_out, values, preferred_element_type=jnp.float32)
    grad_values = jnp.einsum(
        "ghqk,gqhd->gkhd",
        prob_rows.astype(jnp.bfloat16),
        grad_out,
        preferred_element_type=jnp.float32,
    )
    inner_sum = jnp.sum(prob_rows * grad_probs, axis=-1, keepdims=True)
    grad_scores = (prob_rows * (grad_probs - inner_sum)).astype(jnp.bfloat16)
    grad_queries = (
        jnp.einsum("ghqk,gkhd->gqhd", grad_scores, keys_rot, preferred_element_type=jnp.float32)
        * scaling
    )
    grad_keys = (
        jnp.einsum("ghqk,gqhd->gkhd", grad_scores, queries, preferred_element_type=jnp.float32)
        * scaling
    )
    stacked = jnp.stack(
        [
            unrotate(grad_queries, cosine, sine_tab),
            unrotate(grad_keys, cosine, sine_tab),
            grad_values,
        ],
        axis=2,
    )
    return stacked.astype(jnp.bfloat16).reshape(batch_size, length, 3, 1, -1)


def gather_sequences(values):
    return lax.all_to_all(values, "tok", split_axis=0, concat_axis=1, tiled=True)


def return_positions(values):
    return lax.all_to_all(values, "tok", split_axis=1, concat_axis=0, tiled=True)


def group_scatter(parts, own, size, axis, perm_of):
    total = lax.dynamic_index_in_dim(parts, own, 0, keepdims=False).astype(jnp.float32)
    for shift in range(1, size):
        piece = lax.dynamic_index_in_dim(parts, (own + shift) % size, 0, keepdims=False)
        total = total + lax.ppermute(piece, axis, perm_of(shift)).astype(jnp.float32)
    return total.astype(jnp.bfloat16)


def group_gather(piece, own, size, axis, perm_of):
    held = jnp.zeros((size,) + piece.shape, piece.dtype)
    held = lax.dynamic_update_index_in_dim(held, piece, own, 0)
    for shift in range(1, size):
        other = lax.ppermute(piece, axis, perm_of(shift))
        held = lax.dynamic_update_index_in_dim(held, other, (own - shift) % size, 0)
    return held


def scatter_sum(gradient):
    seq_ways, tok_ways = lax.axis_size("seq"), lax.axis_size("tok")
    outer, middle = 4, seq_ways // 8
    place, turn = lax.axis_index("seq"), lax.axis_index("tok")
    core, mid, out = place % 2, (place // 2) % middle, place // (2 * middle)

    def core_perm(shift):
        return [(i, i ^ 1) for i in range(seq_ways)]

    def mid_perm(shift):
        return [
            (i, (i // (2 * middle)) * 2 * middle + ((i // 2 + shift) % middle) * 2 + i % 2)
            for i in range(seq_ways)
        ]

    def out_perm(shift):
        return [(i, (i + shift * 2 * middle) % seq_ways) for i in range(seq_ways)]

    def tok_perm(shift):
        return [(i, (i + shift) % tok_ways) for i in range(tok_ways)]

    rows, width = gradient.shape[0] // seq_ways, gradient.shape[1]
    parts = gradient.astype(jnp.bfloat16).reshape(outer * middle, 2, rows, width)
    parts = group_scatter(jnp.swapaxes(parts, 0, 1), core, 2, "seq", core_perm)
    parts = parts.reshape(outer, middle, rows, 2, tok_ways, width // (2 * tok_ways))
    first = jnp.transpose(parts[:, :, :, 0], (1, 3, 0, 2, 4))
    second = jnp.transpose(parts[:, :, :, 1], (3, 1, 0, 2, 4))
    first = group_scatter(first, mid, middle, "seq", mid_perm)
    second = group_scatter(second, turn, tok_ways, "tok", tok_perm)
    first = group_scatter(first, turn, tok_ways, "tok", tok_perm)
    second = group_scatter(second, mid, middle, "seq", mid_perm)
    both = jnp.stack([first, second], axis=1)
    both = group_scatter(both, out, outer, "seq", out_perm)
    both = group_gather(both, turn, tok_ways, "tok", tok_perm)
    return jnp.transpose(both, (2, 1, 0, 3)).reshape(rows, width).T.astype(jnp.float32)


MESH_ID = pl.DeviceIdType.MESH
BF = jnp.bfloat16
F32 = jnp.float32
UNITS = 12
UNIT_DOWN, UNIT_UP, UNIT_OUT, UNIT_QKV = 0, 4, 8, 9
ORDERS = "wzywywywwwyzwyyyywwwzwwy"
GELU_A = math.sqrt(2.0 / math.pi)
GELU_B = 0.044715


def mm(left, right, left_dim, right_dim):
    return lax.dot_general(
        left, right, (((left_dim,), (right_dim,)), ((), ())), preferred_element_type=F32
    )


def rotated_partner(values):
    lane = lax.broadcasted_iota(jnp.int32, values.shape, 1)
    return jnp.where(lane % 64 < 32, pltpu.roll(values, 96, 1), pltpu.roll(values, 32, 1))


def lane_index(rows):
    return lax.broadcasted_iota(jnp.int32, (rows, 128), 1)


def two_heads(value):
    first = lane_index(128) < 64
    zero = jnp.zeros_like(value)
    return jnp.concatenate([jnp.where(first, value, zero), jnp.where(first, zero, value)], axis=0)


def head_mask(count):
    lane = lane_index(256)
    row = lax.broadcasted_iota(jnp.int32, (256, 128), 0)
    return jnp.where((lane // 64 == row // 128) & (lane % 64 < count), 1.0, 0.0)


def in_terms(value):
    lane = lane_index(value.shape[0]) % 64
    out, rest = jnp.zeros(value.shape, BF), value
    for index in range(3):
        term = rest.astype(BF)
        rest = rest - term.astype(F32)
        out = jnp.where(lane == index, term, out)
    return out


def layer_kernel(
    tokens_in,
    cotangent_in,
    w_qkv,
    w_out,
    w_up,
    w_down,
    time_proj,
    time_bias,
    gain_one,
    shift_one,
    gain_two,
    shift_two,
    b_up,
    b_down,
    cosine,
    sine,
    noise_times,
    mixed_out,
    tokens_out,
    shares_out,
    small_out,
    normed_one_out,
    hidden_one_out,
    partial,
    core_recv,
    recv_one,
    recv_two,
    recv_three,
    weight,
    wide_a,
    wide_g,
    q_held,
    k_held,
    v_held,
    log_held,
    tokens,
    inc,
    normed,
    hidden,
    total,
    grad_attn,
    attended,
    message,
    small_recv,
    vec_rows,
    embeds,
    tables,
    time_embed,
    load_sem,
    weight_sem,
    token_ssem,
    token_rsem,
    cot_ssem,
    cot_rsem,
    core_ssem,
    core_rsem,
    credit,
    one_ssem,
    one_rsem,
    two_ssem,
    two_rsem,
    three_ssem,
    three_rsem,
    gather_ssem,
    gather_rsem,
    small_ssem,
    small_rsem,
    back_ssem,
    back_rsem,
):
    place, turn = lax.axis_index("seq"), lax.axis_index("tok")
    core, xx, zz = place % 2, (place // 2) % 2, place // 4
    yy = turn
    me = place * 2 + turn
    devices = 32

    def at_seq(z, x, c):
        return ((z * 2 + x) * 2 + c, turn)

    core_peer = at_seq(zz, xx, 1 - core)
    x_peer = at_seq(zz, 1 - xx, core)
    y_peer = (place, 1 - turn)

    def load(index, source, target):
        return pltpu.make_async_copy(source, target, load_sem.at[index])

    def load_weight(tile):
        if tile == 0 or tile == 13:
            source = w_out
        elif tile < 5:
            source = w_up.at[:, pl.ds((tile - 1) * 1024, 1024)]
        elif tile < 9:
            source = w_down.at[pl.ds((tile - 5) * 1024, 1024), :]
        elif tile < 13:
            source = w_up.at[:, pl.ds((tile - 9) * 1024, 1024)]
        elif tile < 17:
            source = w_qkv.at[:, pl.ds((tile - 14) * 1024, 1024)]
        else:
            source = w_down.at[pl.ds((tile - 17) * 1024, 1024), :]
        return pltpu.make_async_copy(source, weight.at[tile % 2], weight_sem.at[tile % 2])

    def row_of(vector):
        return vector[...].astype(F32).reshape(1, vector.shape[0])

    own_half = pl.ds(turn * 64, 64)

    def load_qkv(part):
        index, half = part // 2, part % 2
        columns = pl.ds(index * 1024, 1024)
        target = (wide_a, wide_g)[half]
        return load(
            1 + part, w_qkv.at[pl.ds(half * 512, 512), columns], target.at[:, columns]
        )

    def load_cot(seq):
        return load(
            8 + seq,
            cotangent_in.at[turn * 4 + seq],
            inc.at[pl.ds(seq * 128 + turn * 64, 64)],
        )

    load_tokens = load(0, tokens_in.at[pl.ds(turn * 4, 4)], tokens.at[:, own_half])
    load_tokens.start()
    for part in range(6):
        load_qkv(part).start()
    load_weight(0).start()
    load_weight(1).start()
    for seq in range(4):
        load_cot(seq).start()

    barrier = pltpu.get_barrier_semaphore()

    def greet(step, carry):
        other = lax.rem(me + step, devices)
        pl.semaphore_signal(
            barrier, inc=1, device_id=(other // 2, other % 2), device_id_type=MESH_ID
        )
        return carry

    lax.fori_loop(1, devices, greet, 0)
    message[...] = jnp.zeros_like(message)
    vec_rows[...] = jnp.zeros_like(vec_rows)
    lane = lax.broadcasted_iota(jnp.int32, (1, 128), 1).astype(F32)
    frequency = jnp.exp((-math.log(10000.0) * lane) / 128)
    steps = [jnp.where(turn == 0, noise_times[j], noise_times[4 + j]) for j in range(4)]
    angles = jnp.concatenate([frequency * step.astype(F32) for step in steps] * 2, axis=0)
    sine_rows = jnp.sin(angles).astype(BF)
    cosine_rows = jnp.cos(angles).astype(BF)
    time_embed[...] = (
        mm(jnp.concatenate([sine_rows, cosine_rows], axis=1), time_proj[...], 1, 0)
        + row_of(time_bias)
    )
    for pair in range(8):
        message[pair, 20:24, :] = sine_rows.astype(F32)[0:4]
        message[pair, 24:28, :] = cosine_rows.astype(F32)[0:4]
    pl.semaphore_wait(barrier, devices - 1)

    def remote(source, target, send, recv, device):
        return pltpu.make_async_remote_copy(
            src_ref=source,
            dst_ref=target,
            send_sem=send,
            recv_sem=recv,
            device_id=device,
            device_id_type=MESH_ID,
        )

    parity, high = zz % 2, zz // 2

    def core_copy(unit):
        slot = unit % 4
        return remote(
            partial.at[pl.ds(2 * UNITS + 2 * slot, 2)],
            core_recv.at[slot],
            core_ssem.at[slot],
            core_rsem.at[slot],
            core_peer,
        )

    def half_of(chain):
        return chain // 2, pl.ds(32 * (chain % 2), 32)

    def one_copy(chain):
        unit, rows = half_of(chain)
        if ORDERS[chain] in "xw":
            source, device = partial.at[2 * unit + 1 - xx, :, :, :, rows], x_peer
        elif ORDERS[chain] == "y":
            source, device = partial.at[pl.ds(2 * unit, 2), 1 - yy, :, :, rows], y_peer
        else:
            source = partial.at[pl.ds(2 * unit, 2), :, 1 - parity, :, rows]
            device = at_seq(2 * high + 1 - parity, xx, core)
        target = recv_one.at[unit, :, :, :, rows]
        return remote(source, target, one_ssem.at[chain], one_rsem.at[chain], device)

    def two_copy(chain):
        unit, rows = half_of(chain)
        if ORDERS[chain] == "x":
            source, device = partial.at[2 * unit + xx, 1 - yy, :, :, rows], y_peer
        elif ORDERS[chain] == "y":
            source, device = partial.at[2 * unit + 1 - xx, yy, :, :, rows], x_peer
        elif ORDERS[chain] == "w":
            source = partial.at[2 * unit + xx, :, 1 - parity, :, rows]
            device = at_seq(2 * high + 1 - parity, xx, core)
        else:
            source = partial.at[pl.ds(2 * unit, 2), :, parity, 1 - high, rows]
            device = at_seq(2 * (1 - high) + parity, xx, core)
        target = recv_two.at[unit, :, :, rows]
        return remote(source, target, two_ssem.at[chain], two_rsem.at[chain], device)

    def three_copy(chain, step):
        unit, rows = half_of(chain)
        index = 3 * chain + step - 1
        if ORDERS[chain] in "xy":
            other = (zz + step) % 4
            source = partial.at[2 * unit + xx, yy, other % 2, other // 2, rows]
            target, device = recv_three.at[unit, step - 1, rows], at_seq(other, xx, core)
        elif step == 1 and ORDERS[chain] == "w":
            source = partial.at[2 * unit + xx, :, parity, 1 - high, rows]
            target = recv_three.at[unit, pl.ds(0, 2), rows]
            device = at_seq(2 * (1 - high) + parity, xx, core)
        elif step == 1:
            source = partial.at[2 * unit + 1 - xx, :, parity, high, rows]
            target, device = recv_three.at[unit, pl.ds(0, 2), rows], x_peer
        else:
            source = partial.at[2 * unit + xx, :, parity, high, rows]
            target, device = recv_three.at[unit, pl.ds(2, 2), rows], y_peer
        return remote(source, target, three_ssem.at[index], three_rsem.at[index], device)

    def gather_copy(chain):
        unit, rows = half_of(chain)
        view = shares_out.at[unit, yy, rows]
        return remote(view, view, gather_ssem.at[chain], gather_rsem.at[chain], y_peer)

    def start_core(unit):
        if unit >= 4:
            pl.semaphore_wait(credit.at[unit % 4], 1)
        core_copy(unit).start()

    def add_core(unit):
        core_copy(unit).wait_recv()

        def add(index, carry):
            x, h, p = index // 4, (index // 2) % 2, index % 2
            partial[2 * unit + x, h, p] = (
                partial[2 * unit + x, h, p] + core_recv[unit % 4, x, h, p]
            )
            return carry

        lax.fori_loop(0, 8, add, 0)
        if unit < UNITS - 4:
            pl.semaphore_signal(
                credit.at[unit % 4], inc=1, device_id=core_peer, device_id_type=MESH_ID
            )

    def add_one(chain):
        one_copy(chain).wait_recv()
        unit, rows = half_of(chain)
        for a in range(2):
            for b in range(2):
                for c in range(2):
                    if ORDERS[chain] in "xw":
                        at = (2 * unit + xx, a, b, c, rows)
                    elif ORDERS[chain] == "y":
                        at = (2 * unit + a, yy, b, c, rows)
                    else:
                        at = (2 * unit + a, b, parity, c, rows)
                    partial[at] = partial[at] + recv_one[unit, a, b, c, rows]

    def add_two(chain):
        two_copy(chain).wait_recv()
        unit, rows = half_of(chain)
        for a in range(2):
            for b in range(2):
                if ORDERS[chain] == "z":
                    at = (2 * unit + a, b, parity, high, rows)
                elif ORDERS[chain] == "w":
                    at = (2 * unit + xx, a, parity, b, rows)
                else:
                    at = (2 * unit + xx, yy, a, b, rows)
                partial[at] = partial[at] + recv_two[unit, a, b, rows]

    def add_three(chain):
        unit, rows = half_of(chain)
        value = partial[2 * unit + xx, yy, parity, high, rows].astype(F32)
        for step in (1, 2, 3):
            three_copy(chain, step).wait_recv()
        for step in (1, 2, 3):
            value = value + recv_three[unit, step - 1, rows].astype(F32)
        shares_out[unit, yy, rows] = value.astype(BF)

    def add_last_x(chain):
        three_copy(chain, 1).wait_recv()
        unit, rows = half_of(chain)
        for h in range(2):
            at = (2 * unit + xx, h, parity, high, rows)
            partial[at] = partial[at] + recv_three[unit, h, rows]

    def add_swap(chain):
        three_copy(chain, 2).wait_recv()
        unit, rows = half_of(chain)
        for h in range(2):
            value = partial[2 * unit + xx, h, parity, high, rows].astype(F32)
            value = value + recv_three[unit, 2 + h, rows].astype(F32)
            shares_out[unit, h, rows] = value.astype(BF)

    def start_three(chain):
        for step in (2, 1, 3):
            three_copy(chain, step).start()

    actions = {
        "core": (start_core, add_core),
        "one": (lambda unit: one_copy(unit).start(), add_one),
        "two": (lambda unit: two_copy(unit).start(), add_two),
        "three": (start_three, add_three),
        "last_x": (lambda unit: three_copy(unit, 1).start(), add_last_x),
        "swap": (lambda unit: three_copy(unit, 2).start(), add_swap),
        "gather": (
            lambda unit: gather_copy(unit).start(),
            lambda unit: gather_copy(unit).wait_recv(),
        ),
    }
    def row_copies(part, seq):
        source, target = (attended, mixed_out) if part == 0 else (inc, tokens_out)
        views = [source.at[pl.ds(seq * 128 + y * 64, 64)] for y in (yy, 1 - yy)]
        index, at = 4 * part + seq, yy * 4 + seq
        local = pltpu.make_async_copy(views[0], target.at[at], load_sem.at[13 + index])
        away = remote(views[1], target.at[at], back_ssem.at[index], back_rsem.at[index], y_peer)
        return local, away

    def start_rows(part):
        for seq in range(4) if part == 0 else (part - 1,):
            for copy in row_copies(min(part, 1), seq):
                copy.start()

    plan = schedule(ORDERS)
    cursor = [0]

    def pump(label):
        while True:
            kind, stage, unit = plan[cursor[0]]
            cursor[0] += 1
            if kind == "mark":
                assert stage == label
                return
            if stage == "rows":
                start_rows(unit)
            else:
                actions[stage][0 if kind == "start" else 1](unit)

    def wait_sent(units):
        for unit in units:
            core_copy(unit).wait_send()

    def place_block(low, high_rows, unit, x, p, q):
        own, away = 2 * unit + x, 2 * UNITS + 2 * (unit % 4) + x
        for value, at in (
            (low, own * (1 - core) + away * core),
            (high_rows, away * (1 - core) + own * core),
        ):
            value = value.astype(BF)
            for h in range(2):
                partial[at, h, p, q] = value[:, h * 512 : (h + 1) * 512]

    def send_tokens(batch):
        return remote(
            tokens_in.at[pl.ds((1 - turn) * 4 + 2 * batch, 2)],
            tokens.at[pl.ds(2 * batch, 2), own_half],
            token_ssem.at[batch],
            token_rsem.at[batch],
            y_peer,
        )

    def send_cot(seq):
        return remote(
            cotangent_in.at[(1 - turn) * 4 + seq],
            inc.at[pl.ds(seq * 128 + turn * 64, 64)],
            cot_ssem.at[seq],
            cot_rsem.at[seq],
            y_peer,
        )

    send_tokens(0).start()
    load_tokens.wait()

    def norm(value, gain, shift):
        center = value - jnp.mean(value, axis=1, keepdims=True)
        spread = jnp.mean(center * center, axis=1, keepdims=True)
        return (center * lax.rsqrt(spread + 1e-05) * gain + shift).astype(BF)

    def first_norm(seqs, side):
        starts = [pl.multiple_of(seq * 128 + side * 64, 64) for seq in seqs]
        for seq, start in zip(seqs, starts):

            def step(m, carry, seq=seq, start=start):
                rows = pl.ds(pl.multiple_of(start + m * 32, 32), 32)
                inner = pl.ds(pl.multiple_of(side * 64 + m * 32, 32), 32)
                value = tokens[seq, inner, :].astype(F32) + time_embed[seq : seq + 1, :]
                hidden[rows, :] = value
                grad_attn[rows, :] = norm(value, row_of(gain_one), row_of(shift_one))
                return carry

            lax.fori_loop(0, 2, step, 0)
        if len(seqs) == 4:
            send_tokens(1).start()
        rows = jnp.concatenate([grad_attn[pl.ds(start, 64), :] for start in starts], axis=0)
        for part in range(3):
            columns = slice(part * 1024, (part + 1) * 1024)
            if len(seqs) == 4:
                load_qkv(2 * part).wait()
                load_qkv(2 * part + 1).wait()
            value = mm(rows[:, :512], wide_a[:, columns], 1, 0)
            value = (value + mm(rows[:, 512:], wide_g[:, columns], 1, 0)).astype(BF)
            for index, start in enumerate(starts):
                piece = value[index * 64 : (index + 1) * 64]
                if part == 0:
                    wide_a[pl.ds(start, 64), 3072:4096] = piece
                else:
                    (normed, v_held)[part - 1][pl.ds(start, 64), :] = piece

    def forward_heads(seq, pair):
        rows = pl.ds(pl.multiple_of(seq * 128, 128), 128)
        lanes = pl.ds(pl.multiple_of(pair * 128, 128), 128)

        def turned(value):
            value = value.astype(F32)
            return value * cosine[...] + rotated_partner(value) * sine[...]

        first = lane_index(128) < 64
        q = (turned(wide_a[rows, pl.ds(pl.multiple_of(3072 + pair * 128, 128), 128)]) * 0.125).astype(BF)
        k = turned(normed[rows, lanes]).astype(BF)
        q_held[rows, lanes] = q
        k_held[rows, lanes] = k
        scores = mm(q, two_heads(k), 1, 1)
        highest, exponent = [], []
        for part in range(2):
            s = scores[:, part * 128 : (part + 1) * 128]
            highest.append(jnp.max(s, axis=1, keepdims=True))
            exponent.append(jnp.exp(s - highest[part]))
        sums = mm(
            jnp.concatenate(exponent, axis=1).astype(BF),
            jnp.concatenate(
                [two_heads(v_held[rows, lanes]), head_mask(64).astype(BF)], axis=1
            ),
            1,
            0,
        )
        attended[rows, lanes] = (sums[:, :128] / sums[:, 128:]).astype(BF)
        log_total = jnp.where(first, highest[0], highest[1]) + jnp.log(sums[:, 128:])
        log_held[rows, lanes] = in_terms(log_total)

    first_norm((0, 1, 2, 3), turn)
    for batch in range(2):
        send_tokens(batch).wait_recv()
        if batch == 0:
            for seq in range(4):
                send_cot(seq).start()
        first_norm((2 * batch, 2 * batch + 1), 1 - turn)

        def forward_step(index, carry, batch=batch):
            for pair in range(4):
                forward_heads(2 * batch + index // 2, (index % 2) * 4 + pair)
            return carry

        lax.fori_loop(0, 4, forward_step, 0)
        if batch == 0:
            load_weight(0).wait()
        rows = slice(batch * 256, (batch + 1) * 256)
        hidden[rows, :] = hidden[rows, :] + mm(attended[rows, :], weight[0], 1, 0)

        def second_step(m, carry, batch=batch):
            rows = pl.ds(pl.multiple_of(batch * 256 + m * 32, 32), 32)
            normed[rows, :] = norm(hidden[rows, :], row_of(gain_two), row_of(shift_two))
            return carry

        lax.fori_loop(0, 8, second_step, 0)
    spill_normed = load(7, grad_attn, normed_one_out)
    spill_hidden = load(12, hidden, hidden_one_out)
    spill_normed.start()
    spill_hidden.start()
    load_weight(2).start()
    pump("start")

    def up_tile(tile):
        columns = slice(tile * 1024, (tile + 1) * 1024)
        bias = row_of(b_up)

        def step(m, carry):
            for half in range(2):
                rows = pl.ds(pl.multiple_of(m * 256 + half * 128, 128), 128)
                u = mm(normed[rows, :], weight[(tile + 1) % 2], 1, 0) + bias[:, columns]
                square = u * u
                bend = jnp.tanh(u * (GELU_A + (GELU_A * GELU_B) * square))
                side = 0.5 * (1.0 + bend)
                wide_a[rows, columns] = (u * side).astype(BF)
                slope = side + (0.5 * u) * (1.0 - bend * bend) * (
                    GELU_A + (3.0 * GELU_A * GELU_B) * square
                )
                wide_g[rows, columns] = slope.astype(BF)
            return carry

        lax.fori_loop(0, 2, step, 0)

    def down_unit(unit):
        def step(m, carry):
            rows = pl.ds(pl.multiple_of(m * 512, 512), 512)
            value = mm(inc[:, rows], wide_a[:, unit * 1024 : (unit + 1) * 1024], 0, 0)
            for q in range(4):
                at = q * 128
                place_block(
                    value[at : at + 64], value[at + 64 : at + 128], unit, q % 2, q // 2, m
                )
            return carry

        lax.fori_loop(0, 2, step, 0)

    for part in range(4):
        load_weight(1 + part).wait()
        up_tile(part)
        load_weight(part + 3).start()
        pump("up%d" % part)
        if part == 0:
            for seq in range(4):
                load_cot(seq).wait()
                send_cot(seq).wait_recv()
        down_unit(UNIT_DOWN + part)
        pump("down%d" % part)

    for tile in range(4):
        load_weight(5 + tile).wait()
        columns = slice(tile * 1024, (tile + 1) * 1024)

        for part in range(2):
            at = tile * 1024 + part * 512
            grad = mm(inc[...], weight[(tile + 1) % 2, part * 512 : (part + 1) * 512, :], 1, 1)
            grad = (grad * wide_g[:, at : at + 512].astype(F32)).astype(BF)
            wide_g[:, at : at + 512] = grad
            sums = jnp.sum(grad.astype(F32), axis=0, keepdims=True)
            for row in range(4):
                message[2 * tile + part, 16 + row : 17 + row, :] = sums[
                    :, row * 128 : (row + 1) * 128
                ]
        load_weight(tile + 7).start()
        pump("gu%d" % tile)

    wait_sent(range(0, 4))

    def up_step(p, carry):
        columns = pl.ds(pl.multiple_of(p * 512, 512), 512)
        value = mm(wide_g[:, columns], normed[...], 0, 0)
        for j in range(4):
            low = value[j * 64 : (j + 1) * 64]
            high_rows = value[256 + j * 64 : 256 + (j + 1) * 64]
            place_block(low, high_rows, UNIT_UP + j, p % 2, (p // 2) % 2, p // 4)
        return carry

    for part in range(4):
        lax.fori_loop(2 * part, 2 * part + 2, up_step, 0)
        pump("gup%d" % part)

    for tile in range(9, 13):
        load_weight(tile).wait()
        columns = slice((tile - 9) * 1024, (tile - 8) * 1024)

        def norm_step(m, carry, tile=tile, columns=columns):
            rows = pl.ds(pl.multiple_of(m * 256, 256), 256)
            add = mm(wide_g[rows, columns], weight[tile % 2], 1, 1)
            total[rows, :] = add if tile == 9 else total[rows, :] + add
            return carry

        lax.fori_loop(0, 2, norm_step, 0)
        load_weight(tile + 2).start()
        pump("gn%d" % (tile - 9))

    spill_normed.wait()
    spill_hidden.wait()

    def norm_back(h, gain, rows):
        center = h - jnp.mean(h, axis=1, keepdims=True)
        scale = lax.rsqrt(jnp.mean(center * center, axis=1, keepdims=True) + 1e-05)
        xh = center * scale
        q = total[rows, :]
        e = q * gain
        grad = (
            e - jnp.mean(e, axis=1, keepdims=True) - xh * jnp.mean(e * xh, axis=1, keepdims=True)
        ) * scale
        return (
            grad,
            jnp.sum(q * xh, axis=0, keepdims=True),
            jnp.sum(q, axis=0, keepdims=True),
        )

    def norm_two_step(m, carry):
        rows = pl.ds(pl.multiple_of(m * 32, 32), 32)
        grad, gain_sum, shift_sum = norm_back(hidden[rows, :], row_of(gain_two), rows)
        cot = inc[rows, :].astype(F32)
        grad = cot + grad
        hidden[rows, :] = grad
        grad_attn[rows, :] = grad.astype(BF)
        return (
            carry[0] + gain_sum,
            carry[1] + shift_sum,
            carry[2] + jnp.sum(cot, axis=0, keepdims=True),
        )

    none = jnp.zeros((1, 1024), F32)
    gain_sum, shift_sum, down_sum = lax.fori_loop(0, 16, norm_two_step, (none, none, none))
    vec_rows[6:7, :] = gain_sum
    vec_rows[7:8, :] = shift_sum
    vec_rows[8:9, :] = down_sum
    pump("ln2")

    wait_sent(range(4, 5))

    def out_step(m, carry):
        rows = pl.ds(pl.multiple_of(m * 512, 512), 512)
        value = mm(grad_attn[:, rows], attended[...], 0, 0)
        for q in range(4):
            at = q * 128
            place_block(
                value[at : at + 64], value[at + 64 : at + 128], UNIT_OUT, q % 2, q // 2, m
            )
        return carry

    lax.fori_loop(0, 2, out_step, 0)
    pump("out")
    load_weight(13).wait()

    def mixed_back(m, carry):
        rows = pl.ds(pl.multiple_of(m * 256, 256), 256)
        normed[rows, :] = mm(grad_attn[rows, :], weight[1], 1, 1).astype(BF)
        return carry

    lax.fori_loop(0, 2, mixed_back, 0)
    load_weight(15).start()
    fill_normed = load(7, normed_one_out, grad_attn)
    fill_normed.start()
    pump("mb")


    def heads(seq, pair):
        rows = pl.ds(pl.multiple_of(seq * 128, 128), 128)

        def lanes(base):
            return pl.ds(pl.multiple_of(base + pair * 128, 128), 128)

        first = lane_index(128) < 64
        minus = (-head_mask(3)).astype(BF)
        both = jnp.where(
            (lax.broadcasted_iota(jnp.int32, (256, 128), 0) % 128) // 64 == lane_index(256) // 64,
            1.0,
            0.0,
        ).astype(BF)
        q = q_held[rows, lanes(0)]
        k_two = two_heads(k_held[rows, lanes(0)])
        v_two = two_heads(v_held[rows, lanes(0)])
        grad_out = normed[rows, lanes(0)]
        product_rows = grad_out.astype(F32) * attended[rows, lanes(0)].astype(F32)
        head_part = product_rows.astype(BF)
        tail_part = (product_rows - head_part.astype(F32)).astype(BF)
        inner = mm(jnp.concatenate([head_part, tail_part], axis=1), both, 1, 0)
        scores = mm(
            jnp.concatenate([q, log_held[rows, lanes(0)]], axis=1),
            jnp.concatenate([k_two, minus], axis=1),
            1,
            1,
        )
        grad_probs = mm(
            jnp.concatenate([grad_out, in_terms(inner)], axis=1),
            jnp.concatenate([v_two, minus], axis=1),
            1,
            1,
        )
        soft = jnp.exp(scores)
        grad_scores = (soft * grad_probs).astype(BF)
        grad_q = mm(grad_scores, k_two, 1, 0) * 0.125
        grad_k = mm(grad_scores, q, 0, 0)
        grad_v = mm(soft.astype(BF), grad_out, 0, 0)
        grad_k = jnp.where(first, grad_k[:128], grad_k[128:])
        grad_v = jnp.where(first, grad_v[:128], grad_v[128:])

        def unturn(value):
            return value * cosine[...] - rotated_partner(value) * sine[...]

        wide_g[rows, lanes(0)] = unturn(grad_q).astype(BF)
        wide_g[rows, lanes(1024)] = unturn(grad_k).astype(BF)
        wide_g[rows, lanes(2048)] = grad_v.astype(BF)

    def heads_step(index, carry):
        for pair in range(4):
            heads(index // 2, (index % 2) * 4 + pair)
        return carry

    for part in range(4):
        lax.fori_loop(2 * part, 2 * part + 2, heads_step, 0)
        pump("attn%d" % part)

    fill_normed.wait()
    wait_sent(range(5, 8))

    def qkv_step(p, carry):
        columns = pl.ds(pl.multiple_of(p * 384, 128), 384)
        value = mm(wide_g[:, columns], grad_attn[...], 0, 0)
        for j in range(3):
            low = value[j * 64 : (j + 1) * 64]
            high_rows = value[192 + j * 64 : 192 + (j + 1) * 64]
            place_block(low, high_rows, UNIT_QKV + j, p % 2, (p // 2) % 2, p // 4)
        return carry

    lax.fori_loop(0, 4, qkv_step, 0)
    pump("qkv0")
    lax.fori_loop(4, 8, qkv_step, 0)
    pump("qkv1")

    for tile in range(14, 17):
        load_weight(tile).wait()
        columns = slice((tile - 14) * 1024, (tile - 13) * 1024)

        def first_step(m, carry, tile=tile, columns=columns):
            rows = pl.ds(pl.multiple_of(m * 256, 256), 256)
            add = mm(wide_g[rows, columns], weight[tile % 2], 1, 1)
            total[rows, :] = add if tile == 14 else total[rows, :] + add
            return carry

        lax.fori_loop(0, 2, first_step, 0)
        load_weight(tile + 2).start()
        pump("gf%d" % (tile - 14))
    gain_sum, shift_sum = none, none
    for seq in range(4):

        def norm_one_step(m, carry, seq=seq):
            rows = pl.ds(pl.multiple_of(seq * 128 + m * 32, 32), 32)
            inner = pl.ds(pl.multiple_of(m * 32, 32), 32)
            value = tokens[seq, inner, :].astype(F32) + time_embed[seq : seq + 1, :]
            grad, gain_add, shift_add = norm_back(value, row_of(gain_one), rows)
            grad = grad + hidden[rows, :]
            inc[rows, :] = grad.astype(BF)
            return (
                carry[0] + gain_add,
                carry[1] + shift_add,
                carry[2] + jnp.sum(grad, axis=0, keepdims=True),
            )

        gain_sum, shift_sum, embed_sum = lax.fori_loop(
            0, 4, norm_one_step, (gain_sum, shift_sum, none)
        )
        vec_rows[seq : seq + 1, :] = embed_sum
    vec_rows[4:5, :] = gain_sum
    vec_rows[5:6, :] = shift_sum
    fill_hidden = load(12, hidden_one_out, hidden)
    fill_hidden.start()
    for pair in range(8):
        message[pair, 0:16, :] = vec_rows[:, pair * 128 : (pair + 1) * 128]

    def small_copy(other):
        return remote(
            message.at[other // 4],
            small_recv.at[me],
            small_ssem.at[other],
            small_rsem.at[me],
            (other // 2, other % 2),
        )

    def small_start(step, carry):
        small_copy(lax.rem(me + step, devices)).start()
        return carry

    lax.fori_loop(1, devices, small_start, 0)
    small_recv[me] = message[place // 2]
    pump("rows")
    fill_hidden.wait()
    for tile in range(4):
        load_weight(17 + tile).wait()
        columns = slice(tile * 1024, (tile + 1) * 1024)

        def mixed_step(m, carry, tile=tile, columns=columns):
            rows = pl.ds(pl.multiple_of(m * 256, 256), 256)
            add = mm(wide_a[rows, columns], weight[(tile + 1) % 2], 1, 0)
            if tile == 0:
                total[rows, :] = hidden[rows, :] + row_of(b_down) + add
            elif tile < 3:
                total[rows, :] = total[rows, :] + add
            else:
                attended[rows, :] = (total[rows, :] + add).astype(BF)
            return carry

        lax.fori_loop(0, 2, mixed_step, 0)
        if tile < 2:
            load_weight(19 + tile).start()
        pump("mx%d" % tile)
    pump("small")

    def small_wait(step, carry):
        source = lax.rem(me + step, devices)
        pltpu.make_async_remote_copy(
            src_ref=message.at[0],
            dst_ref=small_recv.at[source],
            send_sem=small_ssem.at[source],
            recv_sem=small_rsem.at[source],
            device_id=(source // 2, source % 2),
            device_id_type=MESH_ID,
        ).wait()
        return carry

    lax.fori_loop(1, devices, small_wait, 0)

    def spread(source, carry):
        for row in range(4):
            at = 4 * source + row
            embeds[pl.ds(at, 1), :] = small_recv[source, row : row + 1, :]
            tables[0, pl.ds(at, 1), :] = small_recv[source, 20 + row : 21 + row, :]
            tables[1, pl.ds(at, 1), :] = small_recv[source, 24 + row : 25 + row, :]
        return carry + small_recv[source, 0:24, :]

    sums = lax.fori_loop(0, devices, spread, jnp.zeros((24, 128), F32))
    rest, terms = embeds[...], []
    for _ in range(3):
        terms.append(rest.astype(BF))
        rest = rest - terms[-1].astype(F32)

    def own_lanes(value):
        return jnp.where(core == 0, value, pltpu.roll(value, 64, 1))

    for part in range(2):
        turned = tables[part].astype(BF)
        value = sum(mm(turned, term, 0, 0) for term in terms)
        small_out[part * 128 : (part + 1) * 128, :] = own_lanes(value)
    small_out[256:280, :] = own_lanes(sums)
    wide = jnp.where(core == 0, sums[16:18], sums[18:20])
    small_out[280:282, :] = wide
    pump("end")

    for part in range(2):
        for seq in range(4):
            for copy in row_copies(part, seq):
                copy.wait()
    wait_sent(range(8, 12))
    for batch in range(2):
        send_tokens(batch).wait_send()
    for seq in range(4):
        send_cot(seq).wait_send()
    for chain in range(2 * UNITS):
        one_copy(chain).wait_send()
        two_copy(chain).wait_send()
        for step in (1, 2, 3) if ORDERS[chain] in "xy" else (1, 2):
            three_copy(chain, step).wait_send()
        if ORDERS[chain] in "xy":
            gather_copy(chain).wait_send()


LAST_STEPS = 16
WINDOW = 0.14
BIAS = {"one": 0, "two": 0, "three": -12, "last_x": -12, "swap": 2, "gather": 8}
ROWS_RANK = (-10, 100)
LENGTHS = {
    "start": 25.0,
    "up": 2.5,
    "down": 1.9,
    "gu": 2.1,
    "mx": 1.8,
    "gup": 1.5,
    "gn": 1.9,
    "ln": 3.0,
    "out": 1.9,
    "mb": 2.0,
    "attn": 3.8,
    "qkv": 2.8,
    "gf": 1.9,
    "rows": 6.0,
}
PIECES = (
    ("start", ()),
    ("up0", ()),
    ("down0", (0,)),
    ("up1", ()),
    ("down1", (1,)),
    ("up2", ()),
    ("down2", (2,)),
    ("up3", ()),
    ("down3", (3,)),
    ("gu0", ()),
    ("gu1", ()),
    ("gu2", ()),
    ("gu3", ()),
    ("gup0", ()),
    ("gup1", ()),
    ("gup2", ()),
    ("gup3", (4, 5, 6, 7)),
    ("gn0", ()),
    ("gn1", ()),
    ("gn2", ()),
    ("gn3", ()),
    ("ln2", ()),
    ("out", (8,)),
    ("mb", ()),
    ("attn0", ()),
    ("attn1", ()),
    ("attn2", ()),
    ("attn3", ()),
    ("qkv0", ()),
    ("qkv1", (9, 10, 11)),
    ("gf0", ()),
    ("gf1", ()),
    ("gf2", ()),
    ("rows", ()),
    ("mx0", ()),
    ("mx1", ()),
    ("mx2", ()),
    ("mx3", ()),
)
CHAINS = {
    "x": ("one", "two", "three", "gather"),
    "y": ("one", "two", "three", "gather"),
    "z": ("one", "two", "last_x", "swap"),
    "w": ("one", "two", "last_x", "swap"),
}
COSTS = {"core": 0.5, "one": 0.2, "two": 0.15, "three": 0.25, "last_x": 0.15, "swap": 0.15, "gather": 0.05, "rows": 0.0}
FIRST = {"x": "x", "y": "y", "z": "a", "w": "x"}
SECOND = {"x": "y", "y": "x", "z": "b", "w": "a"}


def transfer(stage, kind):
    if stage == "one":
        return FIRST[kind], 0.262
    if stage == "two":
        return SECOND[kind], 0.262 if kind == "z" else 0.131
    if stage == "three":
        return "b", 0.131
    if stage == "last_x" and kind == "w":
        return "b", 0.131
    if stage in ("last_x", "swap"):
        return ("x" if stage == "last_x" else "y"), 0.0655
    return "y", 0.0328


def schedule(orders):
    rate, lag = 0.086 / 2, 1.4
    flying = {axis: [] for axis in "xyab"}
    queues = {axis: [] for axis in "xyab"}
    arrived, order = [], []
    now, clock = 0.0, 0.0
    core = []

    def advance(until):
        nonlocal now
        while now < until:
            step = until - now
            for fly in flying.values():
                if fly:
                    step = min(step, min(f[0] for f in fly) * len(fly) / rate)
            now += step
            for axis, fly in flying.items():
                if fly:
                    part = step * rate / len(fly)
                    for f in fly:
                        f[0] -= part
                    for f in [f for f in fly if f[0] < 1e-9]:
                        fly.remove(f)
                        if f[1] is None:
                            continue
                        arrived.append((now + lag, f[1]))
            if step <= 0:
                now = until

    def issue():
        for axis in "baxy":
            queue = queues[axis]
            while queue and sum(f[0] for f in flying[axis] if f[1] is not None) < WINDOW:
                queue.sort()
                _, key, size = queue.pop(0)
                flying[axis].append([size, key, clock])
                if axis == "b":
                    flying["a"].append([size * (0.75 if key[0] == "three" else 0.5), None, clock])
                order.append(("start",) + key)

    def ready(stage, chain):
        axis, size = transfer(stage, orders[chain])
        queues[axis].append((chain + BIAS[stage], (stage, chain), size))

    def take(when, key):
        nonlocal clock
        clock = max(clock, when)
        advance(clock)
        stage, chain = key
        if stage == "rows":
            issue()
            return
        order.append(("add",) + key)
        clock += COSTS[stage]
        advance(clock)
        if stage == "core":
            ready("one", 2 * chain)
            ready("one", 2 * chain + 1)
        else:
            names = CHAINS[orders[chain]]
            if stage != names[-1]:
                ready(names[names.index(stage) + 1], chain)
        issue()

    def due():
        while True:
            arrived.sort()
            if not arrived or arrived[0][0] > clock:
                return
            take(*arrived.pop(0))

    for label, units in PIECES:
        clock += LENGTHS[label.rstrip("0123456789")]
        advance(clock)
        for unit in units:
            order.append(("start", "core", unit))
            arrived.append((clock + 2.3 + 0.3 * units.index(unit), ("core", unit)))
        if label == "mx3":
            queues["y"].append((ROWS_RANK[0], ("rows", 0), 0.524))
        if label == "rows":
            for seq in range(4):
                queues["y"].append((ROWS_RANK[1], ("rows", 1 + seq), 0.131))
        issue()
        due()
        order.append(("mark", label, 0))
    while arrived or any(flying.values()):
        if arrived:
            arrived.sort()
            if arrived[0][0] <= now or not any(flying.values()):
                take(*arrived.pop(0))
                continue
        advance(now + 0.1)
    order.insert(len(order) - LAST_STEPS, ("mark", "small", 0))
    order.append(("mark", "end", 0))
    return order


def layer_call(operands, constants, times):
    vmem = pl.BlockSpec(memory_space=pltpu.VMEM)
    hbm = pl.BlockSpec(memory_space=pl.ANY)
    dma = pltpu.SemaphoreType.DMA
    chains = 2 * UNITS
    return pl.pallas_call(
        layer_kernel,
        name="layer",
        out_shape=(
            jax.ShapeDtypeStruct((8, 64, 1024), BF),
            jax.ShapeDtypeStruct((8, 64, 1024), BF),
            jax.ShapeDtypeStruct((UNITS, 2, 64, 512), BF),
            jax.ShapeDtypeStruct((288, 128), F32),
            jax.ShapeDtypeStruct((512, 1024), BF),
            jax.ShapeDtypeStruct((512, 1024), F32),
        ),
        in_specs=[hbm] * 6 + [vmem] * 10 + [pl.BlockSpec(memory_space=pltpu.SMEM)],
        out_specs=(hbm, hbm, vmem, vmem, hbm, hbm),
        scratch_shapes=[
            pltpu.VMEM((2 * UNITS + 8, 2, 2, 2, 64, 512), BF),
            pltpu.VMEM((4, 2, 2, 2, 2, 64, 512), BF),
            pltpu.VMEM((UNITS, 2, 2, 2, 64, 512), BF),
            pltpu.VMEM((UNITS, 2, 2, 64, 512), BF),
            pltpu.VMEM((UNITS, 4, 64, 512), BF),
            pltpu.VMEM((2, 1024, 1024), BF),
            pltpu.VMEM((512, 4096), BF),
            pltpu.VMEM((512, 4096), BF),
            pltpu.VMEM((512, 1024), BF),
            pltpu.VMEM((512, 1024), BF),
            pltpu.VMEM((512, 1024), BF),
            pltpu.VMEM((512, 1024), BF),
            pltpu.VMEM((4, 128, 1024), BF),
            pltpu.VMEM((512, 1024), BF),
            pltpu.VMEM((512, 1024), BF),
            pltpu.VMEM((512, 1024), F32),
            pltpu.VMEM((512, 1024), F32),
            pltpu.VMEM((512, 1024), BF),
            pltpu.VMEM((512, 1024), BF),
            pltpu.VMEM((8, 32, 128), F32),
            pltpu.VMEM((32, 32, 128), F32),
            pltpu.VMEM((16, 1024), F32),
            pltpu.VMEM((128, 128), F32),
            pltpu.VMEM((2, 128, 128), F32),
            pltpu.VMEM((8, 1024), F32),
            dma((21,)),
            dma((2,)),
            dma((2,)),
            dma((2,)),
            dma((4,)),
            dma((4,)),
            dma((4,)),
            dma((4,)),
            pltpu.SemaphoreType.REGULAR((4,)),
            dma((chains,)),
            dma((chains,)),
            dma((chains,)),
            dma((chains,)),
            dma((3 * chains,)),
            dma((3 * chains,)),
            dma((chains,)),
            dma((chains,)),
            dma((32,)),
            dma((32,)),
            dma((8,)),
            dma((8,)),
        ],
        compiler_params=pltpu.CompilerParams(
            collective_id=0, has_side_effects=True, vmem_limit_bytes=VMEM_LIMIT
        ),
    )(*operands, *constants, times)


def finish_kernel(
    mixed_in,
    tokens_in,
    shares_in,
    small_in,
    mixed_out,
    tokens_out,
    down_out,
    up_out,
    w_out_out,
    qkv_out,
    proj_out,
    time_bias,
    gain_one,
    shift_one,
    gain_two,
    shift_two,
    b_down,
    b_up,
    mixed,
    tokens,
    shares,
    small,
    down,
    up,
    w_out,
    qkv,
    proj,
    in_sem,
    out_sem,
):
    def inward(index):
        if index < UNITS:
            source, target = shares_in.at[index], shares.at[index]
        else:
            source, target = (
                (small_in, small),
                (mixed_in, mixed),
                (tokens_in, tokens),
            )[index - UNITS]
        return pltpu.make_async_copy(source, target, in_sem.at[index])

    def outward(index):
        if index < 4:
            columns = pl.ds(index * 1024, 1024)
            source, target = down.at[:, columns], down_out.at[:, columns]
        else:
            source, target = (
                (up, up_out),
                (w_out, w_out_out),
                (qkv, qkv_out),
                (proj, proj_out),
                (mixed, mixed_out),
                (tokens, tokens_out),
            )[index - 4]
        return pltpu.make_async_copy(source, target, out_sem.at[index])

    turn = list(range(UNIT_UP, UNIT_UP + 4)) + list(range(UNIT_DOWN, UNIT_DOWN + 4))
    turn += list(range(UNIT_OUT, UNITS)) + [UNITS, UNITS + 1, UNITS + 2]
    for index in turn:
        inward(index).start()

    def share(unit, h):
        return shares[unit, h].astype(F32)

    for j in range(4):
        inward(UNIT_UP + j).wait()
    for h in range(2):
        for j in range(0, 4, 2):
            both = jnp.concatenate([share(UNIT_UP + j, h), share(UNIT_UP + j + 1, h)], axis=0)
            up[h * 512 : (h + 1) * 512, j * 64 : (j + 2) * 64] = both.T
    outward(4).start()
    for j in range(4):
        inward(UNIT_DOWN + j).wait()
        for h in range(2):
            at = j * 1024 + h * 512
            down[:, at : at + 512] = share(UNIT_DOWN + j, h)
        outward(j).start()
    inward(UNIT_OUT).wait()
    for h in range(2):
        w_out[:, h * 512 : (h + 1) * 512] = share(UNIT_OUT, h)
    outward(5).start()
    for j in range(3):
        inward(UNIT_QKV + j).wait()
        for h in range(2):
            qkv[j * 64 : (j + 1) * 64, h * 512 : (h + 1) * 512] = share(UNIT_QKV + j, h)
    outward(6).start()
    inward(UNITS).wait()
    for part in range(2):
        proj[:, part * 128 : (part + 1) * 128] = small[part * 128 : (part + 1) * 128, :].T[:64]
    outward(7).start()
    inward(UNITS + 1).wait()
    outward(8).start()
    inward(UNITS + 2).wait()
    outward(9).start()
    rows = small[256:288, :]
    time_bias[...] = jnp.sum(rows[0:4], axis=0)[:64]
    for index, target in enumerate((gain_one, shift_one, gain_two, shift_two, b_down)):
        target[...] = rows[4 + index, :64]
    for index in range(2):
        b_up[index * 128 : (index + 1) * 128] = rows[24 + index, :]
    for index in range(10):
        outward(index).wait()


def finish_call(mixed, tokens, shares, small):
    vmem = pl.BlockSpec(memory_space=pltpu.VMEM)
    hbm = pl.BlockSpec(memory_space=pl.ANY)
    like = jax.ShapeDtypeStruct
    vector = like((64,), F32)
    wide = ((64, 4096), (1024, 256), (64, 1024), (192, 1024), (64, 256))
    return pl.pallas_call(
        finish_kernel,
        name="finish",
        out_shape=(like((8, 64, 1024), BF),) * 2
        + tuple(like(shape, F32) for shape in wide)
        + (vector,) * 6
        + (like((256,), F32),),
        in_specs=[hbm] * 4,
        out_specs=(hbm,) * 7 + (vmem,) * 7,
        scratch_shapes=[pltpu.VMEM((8, 64, 1024), BF)] * 2
        + [pltpu.VMEM((UNITS, 2, 64, 512), BF), pltpu.VMEM((288, 128), F32)]
        + [pltpu.VMEM(shape, F32) for shape in wide]
        + [pltpu.SemaphoreType.DMA((UNITS + 3,)), pltpu.SemaphoreType.DMA((10,))],
        compiler_params=pltpu.CompilerParams(vmem_limit_bytes=VMEM_LIMIT),
    )(mixed, tokens, shares, small)


def body(
    tokens,
    noise_times,
    time_proj,
    time_bias,
    gain_one,
    shift_one,
    w_qkv,
    w_out,
    gain_two,
    shift_two,
    w_up,
    b_up,
    w_down,
    b_down,
    cotangent,
):
    seq_ways, tok_ways = lax.axis_size("seq"), lax.axis_size("tok")
    model_width = tokens.shape[-1]
    seq_count, length = tokens.shape[0] // tok_ways, tokens.shape[1] * tok_ways
    row_count = seq_count * length
    all_times = lax.all_gather(noise_times, "seq", tiled=True)
    own_times = lax.dynamic_slice_in_dim(
        noise_times, lax.axis_index("tok") * seq_count, seq_count
    )
    embed_table = noise_table(own_times).astype(jnp.bfloat16)
    time_embed = product(embed_table, time_proj) + time_bias.astype(jnp.float32)
    tokens = gather_sequences(tokens)
    incoming = gather_sequences(cotangent).reshape(row_count, model_width)
    hidden_zero = (tokens.astype(jnp.float32) + time_embed[:, None, :]).reshape(
        row_count, model_width
    )
    normed_one, pull_one = jax.vjp(
        layer_norm, hidden_zero, gain_one.astype(jnp.float32), shift_one.astype(jnp.float32)
    )
    normed_one = normed_one.astype(jnp.bfloat16)
    projected = product(normed_one, w_qkv).astype(jnp.bfloat16)
    received, attended, log_total = attend_items(
        projected.reshape(seq_count, length, 3, 1, model_width)
    )
    attended = attended.reshape(row_count, model_width)
    hidden_one = hidden_zero + product(attended, w_out)
    normed_two, pull_two = jax.vjp(
        layer_norm, hidden_one, gain_two.astype(jnp.float32), shift_two.astype(jnp.float32)
    )
    normed_two = normed_two.astype(jnp.bfloat16)
    upward = product(normed_two, w_up) + b_up.astype(jnp.float32)
    active, pull_gelu = jax.vjp(jax.nn.gelu, upward)
    active = active.astype(jnp.bfloat16)
    out_wdown = scatter_sum(contract_rows(incoming, active))
    result = hidden_one + (product(active, w_down) + b_down.astype(jnp.float32))
    mixed_out = return_positions(
        result.astype(jnp.bfloat16).reshape(seq_count, length, model_width)
    )
    sum_down = jnp.sum(incoming, axis=0, dtype=jnp.float32)
    grad_active = times_transpose(incoming, w_down)
    (grad_upward,) = pull_gelu(grad_active)
    grad_upward = grad_upward.astype(jnp.bfloat16)
    sum_up = jnp.sum(grad_upward, axis=0, dtype=jnp.float32)
    out_wup = scatter_sum(contract_rows(grad_upward, normed_two))
    grad_norm_two = times_transpose(grad_upward, w_up)
    grad_hidden_two, grad_gain_two, grad_shift_two = pull_two(grad_norm_two)
    grad_hidden_one = incoming.astype(jnp.float32) + grad_hidden_two
    grad_attn = grad_hidden_one.astype(jnp.bfloat16)
    out_wout = scatter_sum(contract_rows(grad_attn, attended))
    grad_mixed = times_transpose(grad_attn, w_out).astype(jnp.bfloat16)
    grad_parts = attention_grad(
        received, log_total, grad_mixed.reshape(seq_count, length, 1, model_width)
    ).reshape(row_count, 3 * model_width)
    out_wqkv = scatter_sum(contract_rows(grad_parts, normed_one))
    grad_norm_one = times_transpose(grad_parts, w_qkv)
    grad_hidden_zero, grad_gain_one, grad_shift_one = pull_one(grad_norm_one)
    grad_total = grad_hidden_one + grad_hidden_zero
    grad_tokens = return_positions(
        grad_total.astype(jnp.bfloat16).reshape(seq_count, length, model_width)
    )
    grad_embed = jnp.sum(grad_total.reshape(seq_count, length, model_width), axis=1)
    wide = sum_up.shape[0] // model_width
    small = jnp.concatenate(
        [
            grad_embed.reshape(seq_count, seq_ways, -1).swapaxes(0, 1),
            grad_gain_one.reshape(seq_ways, 1, -1),
            grad_shift_one.reshape(seq_ways, 1, -1),
            grad_gain_two.reshape(seq_ways, 1, -1),
            grad_shift_two.reshape(seq_ways, 1, -1),
            sum_down.reshape(seq_ways, 1, -1),
            sum_up.reshape(seq_ways, wide, -1),
        ],
        axis=1,
    )
    small = lax.all_to_all(small, "seq", split_axis=0, concat_axis=0, tiled=True)
    small = lax.all_gather(small, "tok", axis=1)
    embeds = small[:, :, :seq_count].reshape(-1, small.shape[-1])
    out_proj = jnp.dot(
        noise_table(all_times).astype(jnp.bfloat16).astype(jnp.float32).T,
        embeds,
        precision=lax.Precision.HIGHEST,
    )
    out_bias = jnp.sum(embeds, axis=0)
    sums = jnp.sum(small[:, :, seq_count:], axis=(0, 1))
    return (
        mixed_out,
        grad_tokens,
        out_proj,
        out_bias,
        sums[0],
        sums[1],
        out_wqkv,
        out_wout,
        sums[2],
        sums[3],
        out_wup,
        sums[5:].reshape(-1),
        out_wdown,
        sums[4],
    )


def rotary_lanes():
    halves = HD // 2
    frequency = np.exp(-math.log(10000.0) * np.arange(halves, dtype=np.float32) / halves)
    angles = np.arange(128, dtype=np.float32)[:, None] * frequency.astype(np.float32)[None, :]
    cosine, sine = np.cos(angles), np.sin(angles)
    return (
        jnp.asarray(np.tile(cosine, (1, 4)), jnp.float32),
        jnp.asarray(np.concatenate([-sine, sine] * 2, axis=1), jnp.float32),
    )


def fast_body(
    tokens,
    noise_times,
    time_proj,
    time_bias,
    gain_one,
    shift_one,
    w_qkv,
    w_out,
    gain_two,
    shift_two,
    w_up,
    b_up,
    w_down,
    b_down,
    cotangent,
):
    cosine, sine = rotary_lanes()
    mixed_out, grad_tokens, shares, small, _, _ = layer_call(
        (tokens, cotangent, w_qkv, w_out, w_up, w_down),
        (
            time_proj,
            time_bias,
            gain_one,
            shift_one,
            gain_two,
            shift_two,
            b_up,
            b_down,
            cosine,
            sine,
        ),
        noise_times,
    )
    (
        mixed_out,
        grad_tokens,
        out_wdown,
        out_wup,
        out_wout,
        out_wqkv,
        out_proj,
        out_bias,
        out_gain_one,
        out_shift_one,
        out_gain_two,
        out_shift_two,
        out_bdown,
        out_bup,
    ) = finish_call(mixed_out, grad_tokens, shares, small)
    return (
        mixed_out,
        grad_tokens,
        out_proj.T,
        out_bias,
        out_gain_one,
        out_shift_one,
        out_wqkv.T,
        out_wout.T,
        out_gain_two,
        out_shift_two,
        out_wup,
        out_bup,
        out_wdown.T,
        out_bdown,
    )


def solution(mesh):
    chosen = fast_body if (mesh.shape["seq"], mesh.shape["tok"]) == (16, 2) else body
    in_specs = (
        P("seq", "tok", None),
        P("seq"),
        P(),
        P(),
        P(),
        P(),
        P(),
        P(),
        P(),
        P(),
        P(),
        P(),
        P(),
        P(),
        P("seq", "tok", None),
    )
    out_specs = (
        P("seq", "tok", None),
        P("seq", "tok", None),
        P(None, "seq"),
        P("seq"),
        P("seq"),
        P("seq"),
        P(None, "seq"),
        P(None, "seq"),
        P("seq"),
        P("seq"),
        P(None, "seq"),
        P("seq"),
        P(None, "seq"),
        P("seq"),
    )
    return jax.shard_map(chosen, mesh=mesh, in_specs=in_specs, out_specs=out_specs, check_vma=False)
```
